32 devices in a mesh: dp: 16 (over z, x, core), fsdp: 2 (over y).
Axes of the slice: x: 2, y: 2, z: 4, core: 2. Of those that a mesh axis runs over, the one named last changes fastest.
Arguments:
- alignment_input: bfloat16 [32, 32, 32, 768], P(('dp', 'fsdp')), may hold values from -6 to 6
- sequence_mask: int32 [32, 32], P(('dp', 'fsdp')), may hold values from 0 to 1, as said below
- column_length: int32 [32], P(('dp', 'fsdp')), may hold values from 8 to 32, as said below
- output_cotangent: bfloat16 [32, 32, 32, 768], P(('dp', 'fsdp')), may hold values from -6 to 6
- row_projection_weight: bfloat16 [768, 2304], P('fsdp', 'dp'), may hold values from -0.21875 to 0.21875
- row_out_weight: bfloat16 [768, 768], P('dp', 'fsdp'), may hold values from -1.25 to 1.25
- column_projection_weight: bfloat16 [768, 2304], P('fsdp', 'dp'), may hold values from -0.21875 to 0.21875
- column_out_weight: bfloat16 [768, 768], P('dp', 'fsdp'), may hold values from -1.25 to 1.25
- feedforward_in_weight: bfloat16 [768, 3072], P('fsdp', 'dp'), may hold values from -0.21875 to 0.21875
- feedforward_out_weight: bfloat16 [3072, 768], P('dp', 'fsdp'), may hold values from -0.109375 to 0.109375
- layer_norm_gain: bfloat16 [3, 768], P(None, ('dp', 'fsdp')), may hold values from 0.5 to 1.5
- layer_norm_bias: bfloat16 [3, 768], P(None, ('dp', 'fsdp')), may hold values from -2.5 to 2.5
Outputs:
- layer_out: bfloat16 [32, 32, 32, 768], P(('dp', 'fsdp'))
- grad_input: float32 [32, 32, 32, 768], P(('dp', 'fsdp'))
- grad_row_qkv: float32 [768, 2304], P('fsdp', 'dp')
- grad_row_out: float32 [768, 768], P('dp', 'fsdp')
- grad_col_qkv: float32 [768, 2304], P('fsdp', 'dp')
- grad_col_out: float32 [768, 768], P('dp', 'fsdp')
- grad_ffn_in: float32 [768, 3072], P('fsdp', 'dp')
- grad_ffn_out: float32 [3072, 768], P('dp', 'fsdp')
- grad_norm_gain: float32 [3, 768], P(None, ('dp', 'fsdp'))
- grad_norm_bias: float32 [2, 768], P(None, ('dp', 'fsdp'))
- grad_ffn_norm_bias: float32 [768], P(('dp', 'fsdp'))
- penalty: float32 [], replicated
The draws below stay inside these ranges and needn't reach their ends.
Inputs may be any that keep to these rules, and one draw needn't show every extreme that they name: `sequence_mask`: an alignment's true sequences are its first rows; each alignment has 8 or more, and alignment 0 has all 32. `column_length`: the true columns of alignment a rise with a, from 8 at alignment 0 to 32 at the last alignment, within one of the straight line between them.
All inputs are finite; a program needn't handle non-finite values.
Results may differ from the reference program's by a relative error of at most 0.024.
Values may be sent and summed in bfloat16 or wider, within the bound.
No kernel may reach another device: no remote copies, remote signals or barrier semaphores. Data moves between devices by JAX's collectives and lax.ppermute only.
A program may use at most 192 MiB of HBM per device.

```python
import jax
import jax.numpy as jnp
from jax import lax

MODEL_WIDTH = 768
HEADS = 12
HD = 64
FF = 3072
COLUMN_SLOTS = 32
SEQUENCE_SLOTS = 32
ALIGNMENT_TOTAL = 32


def draw_sequence_mask(key, part):
    first, second = jax.random.split(jax.random.fold_in(key, 11))
    partial_count = jax.random.randint(first, (ALIGNMENT_TOTAL,), max(SEQUENCE_SLOTS // 4, 1), SEQUENCE_SLOTS + 1)
    selector = jax.random.randint(second, (ALIGNMENT_TOTAL,), 0, 3)
    counts = jnp.where(selector == 0, SEQUENCE_SLOTS, partial_count)
    counts = counts.at[0].set(SEQUENCE_SLOTS)
    return (jnp.arange(SEQUENCE_SLOTS)[None, :] < counts[:, None]).astype(jnp.int32)


def draw_column_length(key, part):
    least = COLUMN_SLOTS // 4
    places = jnp.arange(ALIGNMENT_TOTAL, dtype=jnp.int32)
    line = least + places * (COLUMN_SLOTS - least) // max(ALIGNMENT_TOTAL - 1, 1)
    jitter = jax.random.randint(jax.random.fold_in(key, 23), (ALIGNMENT_TOTAL,), -1, 2)
    lengths = jnp.clip(line + jitter, least, COLUMN_SLOTS)
    lengths = lengths.at[0].set(least)
    lengths = lengths.at[ALIGNMENT_TOTAL - 1].set(COLUMN_SLOTS)
    return lengths.astype(jnp.int32)


def raised(array, rng, source, target, shards_of, factor):
    owner, partner = [(jnp.arange(array.shape[dim]) // (array.shape[dim] // shards_of)).reshape([-1 if axis == dim else 1 for axis in range(array.ndim)]) for dim in (source, target)]
    chosen = jax.random.permutation(rng, shards_of)[partner]
    strong = (owner == chosen) | (owner == (partner + shards_of // 2) % shards_of)
    return jnp.where(strong, factor * array, array)


def block_levels(own_key, extent, cuts, low, high):
    loudness = 1.0
    for axis_at, parts in cuts:
        steps = jax.random.uniform(jax.random.fold_in(jax.random.fold_in(own_key, 6), axis_at), (parts,), jnp.float32, low / len(cuts), high / len(cuts))
        loudness = loudness * jnp.repeat(jnp.exp(steps), extent[axis_at] // parts).reshape((-1,) + (1,) * (len(extent) - 1 - axis_at))
    return loudness


def gaussian(own_key, extent, deviation, reach, cuts=(), kind=jnp.bfloat16):
    values = jax.random.normal(own_key, extent, jnp.float32) * deviation
    if len(cuts) > 0:
        values = block_levels(own_key, extent, cuts, -0.22, 0.18) * values
    return jnp.clip(values, min=-reach, max=reach).astype(kind)


def heavy_noise(key, shape, width, reach, pieces, heavy, held_as=jnp.bfloat16):
    values = width * jax.random.normal(key, shape, jnp.float32)
    if pieces:
        values = values * block_levels(key, shape, pieces, -0.22, 0.18)
    return jnp.clip(raised(values, jax.random.fold_in(key, 3), *heavy), -reach, reach).astype(held_as)


def setup_inputs(seed: int = 0) -> dict:
    key_list = jax.random.split(jax.random.key(seed), 13)
    alignment_input = gaussian(key_list[0], (ALIGNMENT_TOTAL, SEQUENCE_SLOTS, COLUMN_SLOTS, MODEL_WIDTH), 1.0, 6.0, ((0, 32),))
    sequence_mask = draw_sequence_mask(jax.random.fold_in(key_list[12], 71), 0)
    column_length = draw_column_length(jax.random.fold_in(key_list[12], 71), 0)
    output_cotangent = heavy_noise(key_list[3], (ALIGNMENT_TOTAL, SEQUENCE_SLOTS, COLUMN_SLOTS, MODEL_WIDTH), 1.0, 6.0, ((0, 32),), (0, 3, 32, 2.75))
    row_projection_weight = gaussian(key_list[4], (MODEL_WIDTH, 3 * MODEL_WIDTH), MODEL_WIDTH ** -0.5, 0.21875, ((0, 2), (1, 16)))
    row_out_weight = gaussian(key_list[5], (MODEL_WIDTH, MODEL_WIDTH), (MODEL_WIDTH // COLUMN_SLOTS) ** -0.5, 1.25, ((0, 16), (1, 2)))
    column_projection_weight = gaussian(key_list[6], (MODEL_WIDTH, 3 * MODEL_WIDTH), MODEL_WIDTH ** -0.5, 0.21875, ((0, 2), (1, 16)))
    column_out_weight = gaussian(key_list[7], (MODEL_WIDTH, MODEL_WIDTH), (MODEL_WIDTH // SEQUENCE_SLOTS) ** -0.5, 1.25, ((0, 16), (1, 2)))
    feedforward_in_weight = gaussian(key_list[8], (MODEL_WIDTH, FF), MODEL_WIDTH ** -0.5, 0.21875, ((0, 2), (1, 16)))
    feedforward_out_weight = gaussian(key_list[9], (FF, MODEL_WIDTH), FF ** -0.5, 0.109375, ((0, 16), (1, 2)))
    layer_norm_gain = jnp.clip(1.0 + 0.1 * jax.random.normal(key_list[10], (3, MODEL_WIDTH), jnp.float32), 0.5, 1.5).astype(jnp.bfloat16)
    layer_norm_bias = gaussian(key_list[11], (3, MODEL_WIDTH), 0.3, 2.5, ((1, 32),))
    return dict(alignment_input=alignment_input, sequence_mask=sequence_mask, column_length=column_length, output_cotangent=output_cotangent, row_projection_weight=row_projection_weight, row_out_weight=row_out_weight, column_projection_weight=column_projection_weight, column_out_weight=column_out_weight, feedforward_in_weight=feedforward_in_weight, feedforward_out_weight=feedforward_out_weight, layer_norm_gain=layer_norm_gain, layer_norm_bias=layer_norm_bias)


@jax.custom_vjp
def low(v):
    return lax.optimization_barrier(v.astype(jnp.bfloat16)).astype(jnp.float32)

@jax.custom_vjp
def low_back(v):
    return v

def low_keep(v):
    return (low(v), None)

def low_pass(kept, grad):
    return (grad,)

def back_keep(v):
    return (v, None)

def back_low(kept, grad):
    return (low(grad),)
low.defvjp(low_keep, low_pass)
low_back.defvjp(back_keep, back_low)
PRECISE = lax.Precision.HIGHEST
norm_eps = 1e-05
penalty_weight = 1.0
masked_score = -1000000000.0

def layer_norm(values, gain_vec, bias_vec):
    centred = values - lax.optimization_barrier(jnp.mean(values, -1, keepdims=True))
    spread = lax.optimization_barrier(jnp.mean(centred * centred, -1, keepdims=True))
    return centred * lax.rsqrt(spread + norm_eps) * gain_vec + bias_vec

def gelu_exact(values):
    return jax.nn.gelu(values, approximate=False)

def project(inputs, matrix):
    return jnp.einsum('rcd,de->rce', inputs, matrix, precision=PRECISE)

def one_alignment(token_grid, seq_keep, col_keep, weight_set):
    row_projection_weight, row_out_weight, column_projection_weight, column_out_weight, feedforward_in_weight, feedforward_out_weight, layer_norm_gain, layer_norm_bias = weight_set
    split_shape = (SEQUENCE_SLOTS, COLUMN_SLOTS, 3, HEADS, HD)
    normed_row = low(layer_norm(token_grid, layer_norm_gain[0], layer_norm_bias[0]))
    packed_row = low_back(low(project(normed_row, row_projection_weight))).reshape(split_shape)
    queries = packed_row[:, :, 0] * seq_keep[:, None, None, None]
    row_scale = 0.125 * lax.rsqrt(jnp.sum(seq_keep))
    row_scores = jnp.einsum('rihd,rjhd->hij', queries, packed_row[:, :, 1], precision=PRECISE) * row_scale
    row_scores = jnp.where(col_keep[None, None, :] > 0, low_back(row_scores), masked_score)
    log_prob = row_scores - jax.nn.logsumexp(row_scores, -1, keepdims=True)
    prob_row = jnp.exp(log_prob)
    entropy = -lax.optimization_barrier(jnp.sum(prob_row * log_prob, -1))
    ent_sum = jnp.sum(entropy * col_keep[None, :])
    mixed_row = jnp.einsum('hij,rjhd->rihd', low(prob_row), packed_row[:, :, 2], precision=PRECISE)
    mixed_row = low_back(low(mixed_row)).reshape(SEQUENCE_SLOTS, COLUMN_SLOTS, MODEL_WIDTH)
    after_row = token_grid + low_back(project(mixed_row, row_out_weight))
    normed_col = low(layer_norm(after_row, layer_norm_gain[1], layer_norm_bias[1]))
    packed_col = low_back(low(project(normed_col, column_projection_weight))).reshape(split_shape)
    col_scores = jnp.einsum('rihd,sihd->hirs', packed_col[:, :, 0], packed_col[:, :, 1], precision=PRECISE) * 0.125
    col_scores = jnp.where(seq_keep[None, None, None, :] > 0, low_back(col_scores), masked_score)
    prob_col = jax.nn.softmax(col_scores, -1)
    mixed_col = jnp.einsum('hirs,sihd->rihd', low(prob_col), packed_col[:, :, 2], precision=PRECISE)
    mixed_col = low_back(low(mixed_col)).reshape(SEQUENCE_SLOTS, COLUMN_SLOTS, MODEL_WIDTH)
    after_col = after_row + low_back(project(mixed_col, column_out_weight))
    normed_ffn = low(layer_norm(after_col, layer_norm_gain[2], layer_norm_bias[2]))
    hidden = low_back(project(normed_ffn, feedforward_in_weight))
    active = low(gelu_exact(hidden))
    result = after_col + low_back(project(active, feedforward_out_weight))
    return (result, ent_sum)

def reference(alignment_input, sequence_mask, column_length, output_cotangent, row_projection_weight, row_out_weight, column_projection_weight, column_out_weight, feedforward_in_weight, feedforward_out_weight, layer_norm_gain, layer_norm_bias):
    seq_keep = (sequence_mask > 0).astype(jnp.float32)
    col_keep = (jnp.arange(COLUMN_SLOTS).astype(jnp.int32)[None, :] < column_length[:, None]).astype(jnp.float32)
    total_cols = jnp.sum(col_keep)
    weight_set = (row_projection_weight.astype(jnp.float32), row_out_weight.astype(jnp.float32), column_projection_weight.astype(jnp.float32), column_out_weight.astype(jnp.float32), feedforward_in_weight.astype(jnp.float32), feedforward_out_weight.astype(jnp.float32), layer_norm_gain.astype(jnp.float32), layer_norm_bias.astype(jnp.float32))
    token_grid = alignment_input.astype(jnp.float32)

    def forward(tokens_all, weights_all):

        def per_item(items):
            return one_alignment(items[0], items[1], items[2], weights_all)
        outputs, entropies = lax.map(jax.checkpoint(per_item), (tokens_all, seq_keep, col_keep))
        return (outputs, jnp.sum(entropies) / total_cols)
    (outputs, penalty), pullback = jax.vjp(forward, token_grid, weight_set)
    cotangent = output_cotangent.astype(jnp.float32) * seq_keep[:, :, None, None] * col_keep[:, None, :, None]
    grad_tokens, grad_weights = pullback((cotangent, jnp.ones_like(penalty) * penalty_weight))
    bias_rows = grad_weights[7]
    return (outputs.astype(jnp.bfloat16), grad_tokens, grad_weights[0], grad_weights[1], grad_weights[2], grad_weights[3], grad_weights[4], grad_weights[5], grad_weights[6], bias_rows[:2], bias_rows[2], penalty)
```

```python
import jax
import jax.numpy as jnp
import numpy as np
from jax import lax
from jax.experimental import pallas as pl
from jax.experimental.pallas import tpu as pltpu
from jax.sharding import PartitionSpec as P

HD = 64
AXES = ("dp", "fsdp")
norm_eps = 1e-05
penalty_weight = 1.0
masked_score = -1000000000.0
never = -1e30

F32 = jnp.float32
BF16 = jnp.bfloat16
MIB = 1 << 20


def dot(a, b, ca, cb):
    return lax.dot_general(a, b, (((ca,), (cb,)), ((), ())), preferred_element_type=F32)


class Weights:
    def __init__(self, bufs, row0, rows, whole_rows, width, blocked, table=0):
        self.bufs, self.row0, self.rows, self.table = bufs, row0, rows, table
        self.whole_rows, self.width, self.blocked = whole_rows, width, blocked


class Loaded:
    def __init__(self, ref, copies):
        self.ref, self.copies = ref, copies

    def start(self, rows=None):
        for c in self.copies:
            c.start()

    def wait(self):
        for c in self.copies:
            c.wait()
        return self.ref


class Out:
    def __init__(self, shape, dtype, vmem=True, hbm=False):
        self.shape, self.dtype, self.vmem, self.hbm = shape, dtype, vmem, hbm


def fused(name, body, smem, ins, weights, outs, grads, plan, resident, micros, scratch=(), deps=()):
    arrays, index, spaces = [], {}, []

    def slot(a):
        if id(a) not in index:
            index[id(a)] = len(arrays)
            stays = id(a) in resident
            spaces.append(pltpu.VMEM if stays else pltpu.HBM)
            arrays.append(pltpu.with_memory_space_constraint(a, spaces[-1]))
        return index[id(a)]

    in_slots = [slot(a) for a in ins]
    w_slots = [[slot(b) for b in w.bufs] for w in weights]
    for a in deps:
        arrays.append(a)
        spaces.append(pl.ANY)
    n_smem = len(smem)
    vm, n_sem = [], 0
    for a in ins:
        if id(a) not in resident:
            vm.append(pltpu.VMEM(a.shape, a.dtype))
            n_sem += 1
    for w in weights:
        vm.append(pltpu.VMEM((w.whole_rows, w.width), BF16))
        n_sem += sum(b.shape[0] for b in w.bufs) if w.blocked else 1
    out_shapes, out_spaces = [], []
    for o in outs:
        if o.vmem:
            out_shapes.append(pltpu.VMEM(o.shape, o.dtype))
            out_spaces.append(pltpu.VMEM)
        else:
            vm.append(pltpu.VMEM(o.shape, o.dtype))
        if o.hbm:
            out_shapes.append(pltpu.HBM(o.shape, o.dtype))
            out_spaces.append(pltpu.HBM)
            n_sem += 1
    g_at = len(out_shapes)
    width = plan.width
    for rows in grads:
        vm.append(pltpu.VMEM((rows, width), BF16))
        n_sem += plan.dp * plan.fsdp if plan.fast else 1
    if grads and plan.fast:
        per = sum(rows // plan.dp for rows in grads)
        shape = pltpu.HBM((plan.slots, per, width // plan.fsdp), BF16)
        out_shapes += [shape, shape]
    elif grads:
        out_shapes += [pltpu.HBM((rows, width), BF16) for rows in grads]
    out_spaces += [pltpu.HBM] * (len(out_shapes) - g_at)
    n_in, n_out, n_vm = len(arrays), len(out_shapes), len(vm)
    used_vmem = sum(int(np.prod(m.shape)) * np.dtype(m.dtype).itemsize for m in (*vm, *scratch))

    def kernel(*refs):
        sm = refs[:n_smem]
        hb = refs[n_smem : n_smem + n_in]
        ob = refs[n_smem + n_in : n_smem + n_in + n_out]
        rest = refs[n_smem + n_in + n_out :]
        vrefs, extra, sems = list(rest[:n_vm]), rest[n_vm:-1], rest[-1]
        used = [0]

        def sem():
            used[0] += 1
            return sems.at[used[0] - 1]

        loads = []
        for a, s in zip(ins, in_slots):
            if id(a) in resident:
                loads.append(Loaded(hb[s], []))
            else:
                ref = vrefs.pop(0)
                loads.append(Loaded(ref, [pltpu.make_async_copy(hb[s], ref, sem())]))
        wl = []
        for w, slots in zip(weights, w_slots):
            dst = vrefs.pop(0)
            copies = []
            if w.blocked:
                cols = w.width // plan.fsdp
                count = 0
                for s in slots:
                    for j in range(arrays[s].shape[0]):
                        block = sm[w.table][count] if w.table is not None else count
                        count += 1
                        row = (block // plan.fsdp) * w.rows
                        col = (block % plan.fsdp) * cols
                        if w.table is not None:
                            row, col = pl.multiple_of(row, 16), pl.multiple_of(col, 128)
                        copies.append(
                            pltpu.make_async_copy(
                                hb[s].at[j, pl.ds(w.row0, w.rows), :],
                                dst.at[pl.ds(row, w.rows), pl.ds(col, cols)],
                                sem(),
                            )
                        )
            else:
                copies.append(pltpu.make_async_copy(hb[slots[0]], dst, sem()))
            wl.append(Loaded(dst, copies))
        ol = []
        at = 0
        for o in outs:
            if o.vmem:
                ref = ob[at]
                at += 1
            else:
                ref = vrefs.pop(0)
            copies = []
            if o.hbm:
                copies.append(pltpu.make_async_copy(ref, ob[at], sem()))
                at += 1
            ol.append(Loaded(ref, copies))
        gl = []
        row0 = 0
        for k, rows in enumerate(grads):
            src = vrefs.pop(0)
            if plan.fast:
                gl.append(Blocks(src, ob[at], ob[at + 1], sm[1], plan, rows, row0, sem))
                row0 += rows // plan.dp
            else:
                gl.append(Loaded(src, [pltpu.make_async_copy(src, ob[at + k], sem())]))
        for l in loads + wl:
            l.start()
        body(sm[2:], loads, wl, ol, gl, extra)
        for l in ol + gl:
            l.wait()

    res = pl.pallas_call(
        kernel,
        name=name,
        out_shape=out_shapes,
        in_specs=[pl.BlockSpec(memory_space=pltpu.SMEM)] * n_smem
        + [pl.BlockSpec(memory_space=m) for m in spaces],
        out_specs=[pl.BlockSpec(memory_space=m) for m in out_spaces],
        scratch_shapes=vm + list(scratch) + [pltpu.SemaphoreType.DMA((n_sem,))],
        compiler_params=pltpu.CompilerParams(vmem_limit_bytes=used_vmem + 7 * MIB),
        cost_estimate=pl.CostEstimate(
            flops=int(micros * 1.1e9), bytes_accessed=int(micros * 3e6), transcendentals=0
        ),
    )(*smem, *arrays)
    got, at = [], 0
    for o in outs:
        both = res[at : at + o.vmem + o.hbm]
        at += o.vmem + o.hbm
        if o.vmem:
            resident[id(both[0])] = both[0]
        got.append(both[0] if len(both) == 1 else both)
    return got, res[at:]


class Blocks:
    def __init__(self, ref, kept, sent, table, plan, rows, row0, sem):
        self.ref, self.plan = ref, plan
        self.per, self.cols = rows // plan.dp, plan.width // plan.fsdp
        self.kept, self.sent, self.table, self.row0 = kept, sent, table, row0
        self.sems = [sem() for _ in range(plan.dp * plan.fsdp)]
        self.begun = 0

    def copy(self, n, out, slot):
        row, col = (n // self.plan.fsdp) * self.per, (n % self.plan.fsdp) * self.cols
        return pltpu.make_async_copy(
            self.ref.at[row : row + self.per, col : col + self.cols],
            out.at[slot, pl.ds(self.row0, self.per), :],
            self.sems[n],
        )

    def start(self, rows=None):
        rows = self.ref.shape[0] if rows is None else rows
        end = rows // self.per * self.plan.fsdp
        slots = self.plan.slots
        for n in range(self.begun, end):
            place = self.table[n]

            @pl.when(place < slots)
            def _():
                self.copy(n, self.kept, place).start()

            @pl.when(place >= slots)
            def _():
                self.copy(n, self.sent, place - slots).start()

        self.begun = end

    def wait(self):
        for n in range(self.begun):
            self.copy(n, self.kept, 0).wait()


def normal_form(v):
    centred = v - jnp.mean(v, -1, keepdims=True)
    rstd = lax.rsqrt(jnp.mean(centred * centred, -1, keepdims=True) + norm_eps)
    return centred * rstd, rstd


def norm_rows(src, dst, gb, k, total):
    for t in range(0, total, 256):
        xhat, _ = normal_form(src[t : t + 256, :].astype(F32))
        dst[t : t + 256, :] = (xhat * gb[k : k + 1, :] + gb[k + 3 : k + 4, :]).astype(BF16)


def norm_back(dn_ref, src, base, gb, k, total, emit, sums):
    gain = gb[k : k + 1, :]
    gain_sum = jnp.zeros_like(gain)
    bias_sum = jnp.zeros_like(gain)
    for t in range(0, total, 256):
        xhat, rstd = normal_form(src[t : t + 256, :].astype(F32))
        dn = dn_ref[t : t + 256, :]
        gain_sum = gain_sum + jnp.sum(dn * xhat, 0, keepdims=True)
        bias_sum = bias_sum + jnp.sum(dn, 0, keepdims=True)
        dx = dn * gain
        low = jnp.mean(dx, -1, keepdims=True)
        mix = jnp.mean(dx * xhat, -1, keepdims=True)
        emit(t, base[t : t + 256, :].astype(F32) + rstd * (dx - low - xhat * mix))
    sums[...] = jnp.concatenate([gain_sum, bias_sum, jnp.zeros((6, gain.shape[1]), F32)], 0)


def head_masks(lanes):
    lane = lax.broadcasted_iota(jnp.int32, (1, lanes), 1)
    low = ((lane // HD) % 2 == 0).astype(F32)
    return low.astype(BF16), (1.0 - low).astype(BF16)


def four(ref, col):
    return jnp.concatenate([ref[g * 256 : (g + 1) * 256, col : col + 128] for g in range(4)], 1)


def pick(big):
    seg = lax.broadcasted_iota(jnp.int32, (32, 256), 1) // 32
    out = big[:32, :]
    for k in range(1, 8):
        out = jnp.where(seg == k, big[k * 32 : (k + 1) * 32, :], out)
    out = out[:, :128] + out[:, 128:]
    out = out + pltpu.roll(out, 64, 1)
    return out + pltpu.roll(out, 32, 1)


def spread(small):
    seg = lax.broadcasted_iota(jnp.int32, (32, 256), 1) // 32
    wide = jnp.concatenate([small, small], 1)
    return jnp.concatenate([jnp.where(seg == k, wide, 0.0).astype(BF16) for k in range(8)], 0)


def row_forward(sm, I, W, O, G, X):
    ints, flts = sm
    x, gb = I
    normed, packed, mixed, prob, logp, ent = O
    xr, g = x.wait(), gb.wait()
    norm_rows(xr, normed.ref, g, 0, 1024)
    normed.start()
    wt = W[0].wait()
    nr = normed.ref[...]
    n_seq, n_col = ints[0], ints[1]
    keep = (lax.broadcasted_iota(jnp.int32, (1024, 1), 0) // 32 < n_seq).astype(F32)
    width = nr.shape[1]
    heads = width // HD
    pr = packed.ref
    for n in range(0, 3 * width, 256):
        out = dot(nr, wt[n : n + 256, :], 1, 1)
        if n < width:
            out = out * keep
        pr[:, n : n + 256] = out.astype(BF16)
    packed.start()
    sc = X[0]
    halves = head_masks(512)
    for m in range(heads // 2):
        q, k = four(pr, m * 128), four(pr, width + m * 128)
        for e in range(2):
            h = 2 * m + e
            sc[h * 32 : (h + 1) * 32, :] = pick(dot(q * halves[e], k, 1, 1))
    lane = lax.broadcasted_iota(jnp.int32, (1, 128), 1) % 32
    s = jnp.where(lane < n_col, sc[...] * flts[0], masked_score)
    top = jnp.max(s, -1, keepdims=True)
    total = jnp.sum(jnp.exp(s - top), -1, keepdims=True) * 0.25
    lp = s - (top + jnp.log(total))
    p = jnp.exp(lp)
    prob.ref[...] = p
    logp.ref[...] = lp
    prob.start()
    logp.start()
    entropy = jnp.sum(p * lp, -1, keepdims=True) * -0.25
    row = lax.broadcasted_iota(jnp.int32, entropy.shape, 0) % 32
    ent.ref[...] = jnp.full(ent.ref.shape, jnp.sum(jnp.where(row < n_col, entropy, 0.0)), F32)
    ent.start()
    second = (lax.broadcasted_iota(jnp.int32, (1, 512), 1) // HD) % 2 == 1
    for m in range(heads // 2):
        v = four(pr, 2 * width + m * 128)
        both = [
            dot(spread(prob.ref[h * 32 : (h + 1) * 32, :]), v, 1, 0) for h in (2 * m, 2 * m + 1)
        ]
        out = jnp.where(second, both[1], both[0]).astype(BF16)
        for t in range(4):
            mixed.ref[t * 256 : (t + 1) * 256, m * 128 : (m + 1) * 128] = out[
                :, t * 128 : (t + 1) * 128
            ]
    mixed.start()


def stacked(x, halves):
    return jnp.concatenate([x * halves[0], x * halves[1]], 0)


def segment(rows):
    return (lax.broadcasted_iota(jnp.int32, (rows, 256), 1) // 32) % 4


def pick_four(big):
    seg = segment(32)
    out = big[:32, :]
    for k in range(1, 4):
        out = jnp.where(seg == k, big[k * 32 : (k + 1) * 32, :], out)
    return out


def spread_four(small):
    seg = segment(32)
    return jnp.concatenate([jnp.where(seg == k, small, 0.0).astype(BF16) for k in range(4)], 0)


def unstack(both):
    lane = lax.broadcasted_iota(jnp.int32, (128, 128), 1)
    return jnp.where(lane < HD, both[:128], both[128:])


def to_columns(src, take):
    for t in range(0, 1024, 256):
        lanes = [
            jnp.concatenate([src[j, pl.ds(t // 32 + k, 32, stride=32), :] for k in range(8)], 0)
            for j in range(src.shape[0])
        ]
        take(t, jnp.concatenate(lanes, 1))


def put(dst, rows, n, value):
    for j in range(value.shape[1] // 128):
        dst[n // 128 + j, rows, :] = value[:, j * 128 : (j + 1) * 128]


def column_forward(sm, I, W, O, G, X):
    x, mixed_row, gb = I
    after, normed, packed = O
    (ar,) = X
    width = normed.ref.shape[1]
    mr, xr = mixed_row.wait(), x.wait()
    wo = W[0].wait()
    for n in range(0, width, 256):
        out = xr[:, n : n + 256].astype(F32) + dot(mr[...], wo[:, n : n + 256], 1, 0)
        put(ar, slice(None), n, out)
    g = gb.wait()

    def take(t, rows):
        after.ref[t : t + 256, :] = rows

    to_columns(ar, take)
    after.start()
    norm_rows(after.ref, normed.ref, g, 1, 1024)
    normed.start()
    wt = W[1].wait()
    nr = normed.ref[...]
    pr = packed.ref
    for n in range(0, 3 * width, 256):
        pr[:, n : n + 256] = dot(nr, wt[n : n + 256, :], 1, 1).astype(BF16)
    packed.start()


def column_softmax(sc, n_seq):
    def block(b, carry):
        at = pl.ds(pl.multiple_of(b * 32, 32), 32)
        s = sc[at, :]
        s = jnp.where(lax.broadcasted_iota(jnp.int32, s.shape, 0) < n_seq, s, never)
        p = jnp.exp(s - jnp.max(s, 0, keepdims=True))
        sc[at, :] = p * (1.0 / jnp.sum(p, 0, keepdims=True))
        return carry

    lax.fori_loop(0, sc.shape[0] // 32, block, 0)


def column_attend(sm, I, W, O, G, X):
    (ints,) = sm
    (mixed,) = O
    (sc,) = X
    width = mixed.ref.shape[1]
    pr = I[0].wait()
    halves = head_masks(128)

    def scores(b, carry):
        rows = pl.ds(pl.multiple_of(b * 128, 128), 128)
        at = pl.ds(pl.multiple_of(b * 32, 32), 32)
        for lo in range(0, width, 128):
            qs = stacked(pr[rows, lo : lo + 128] * 0.125, halves)
            k = pr[rows, width + lo : width + lo + 128]
            sc[at, 2 * lo : 2 * lo + 256] = pick_four(dot(k, qs, 1, 1))
        return carry

    lax.fori_loop(0, 8, scores, 0)
    column_softmax(sc, ints[0])

    def mix(b, carry):
        rows = pl.ds(pl.multiple_of(b * 128, 128), 128)
        at = pl.ds(pl.multiple_of(b * 32, 32), 32)
        for lo in range(0, width, 128):
            v = pr[rows, 2 * width + lo : 2 * width + lo + 128]
            p = spread_four(sc[at, 2 * lo : 2 * lo + 256])
            mixed.ref[rows, lo : lo + 128] = unstack(dot(p, v, 0, 0)).astype(BF16)
        return carry

    lax.fori_loop(0, 8, mix, 0)
    mixed.start()


def feed_forward(sm, I, W, O, G, X):
    after_row, mixed, gb = I
    after, normed, active, slope = O
    width = normed.ref.shape[1]
    hidden = active.ref.shape[1]
    ar, mr = after_row.wait(), mixed.wait()
    wo = W[0].wait()
    for n in range(0, width, 256):
        after.ref[:, n : n + 256] = ar[:, n : n + 256] + dot(mr[...], wo[:, n : n + 256], 1, 0)
    after.start()
    norm_rows(after.ref, normed.ref, gb.wait(), 2, 1024)
    normed.start()
    wt = W[1].wait()
    nr = normed.ref[...]
    for n in range(0, hidden, 256):
        h = dot(nr, wt[n : n + 256, :], 1, 1)
        cdf = 0.5 + 0.5 * lax.erf(h * (0.5**0.5))
        active.ref[:, n : n + 256] = (h * cdf).astype(BF16)
        bell = jnp.exp(h * h * -0.5) * (0.5 / np.pi) ** 0.5
        slope.ref[:, n : n + 256] = (cdf + h * bell).astype(BF16)
    active.start()
    slope.start()


def cotangent(sm, I, W, O, G, X):
    (ints,) = sm
    (cot,) = I
    (g3,) = O
    (wide,) = X
    put(wide, slice(None), 0, cot.wait()[...].astype(F32))
    n_seq, n_col = ints[0], ints[1]

    def take(t, rows):
        at = lax.broadcasted_iota(jnp.int32, (256, 1), 0) + t
        keep = ((at % 32 < n_seq) & (at // 32 < n_col)).astype(F32)
        g3.ref[t : t + 256, :] = (rows * keep).astype(BF16)

    to_columns(wide, take)
    g3.start()


def weight_grad(dst, left, right, step=768):
    rows = dst.ref.shape[0]
    blocks = isinstance(dst, Blocks)
    for n in range(0, rows, step):
        dst.ref[n : n + step, :] = dot(left[:, n : n + step], right[...], 0, 0).astype(BF16)
        if blocks:
            dst.start(n + step)
    if not blocks:
        dst.start()


def ffn_out_grad(sm, I, W, O, G, X):
    active, g3 = I
    ar, gr = active.wait(), g3.wait()
    weight_grad(G[0], ar, gr)


def ffn_back(sm, I, W, O, G, X):
    g3, slope, normed = I
    (grad_hidden,) = O
    wf = W[0].wait()
    gr, sl = g3.wait(), slope.wait()
    gh = grad_hidden.ref
    hidden = gh.shape[1]
    gv = gr[...]
    for n in range(0, hidden, 256):
        d = dot(gv, wf[n : n + 256, :], 1, 1)
        gh[:, n : n + 256] = (d * sl[:, n : n + 256].astype(F32)).astype(BF16)
    grad_hidden.start()
    weight_grad(G[0], gh, normed.wait())


def ffn_result(sm, I, W, O, G, X):
    active, after = I
    (layer_out,) = O
    (res,) = X
    width = layer_out.ref.shape[1]
    wf = W[0].wait()
    ac, ar = active.wait(), after.wait()
    for n in range(0, width, 256):
        put(res, slice(None), n, ar[:, n : n + 256] + dot(ac[...], wf[:, n : n + 256], 1, 0))

    def take(t, rows):
        layer_out.ref[t : t + 256, :] = rows.astype(BF16)

    to_columns(res, take)
    layer_out.start()


def column_back(sm, I, W, O, G, X):
    grad_hidden, after_col, g3, gb = I
    grad_after, branch, grad_mixed, sums = O
    (dn,) = X
    g2, gm = branch.ref, grad_mixed.ref
    width = g2.shape[1]
    gh = grad_hidden.wait()
    wf = W[0].wait()
    for n in range(0, width, 256):
        dn[:, n : n + 256] = dot(gh[...], wf[:, n : n + 256], 1, 0)
    ac, base, g = after_col.wait(), g3.wait(), gb.wait()

    def emit(t, rows):
        grad_after.ref[t : t + 256, :] = rows
        g2[t : t + 256, :] = rows.astype(BF16)

    norm_back(dn, ac, base, g, 2, 1024, emit, sums.ref)
    grad_after.start()
    sums.start()
    wo = W[1].wait()
    for n in range(0, width, 256):
        gm[:, n : n + 256] = dot(g2[...], wo[n : n + 256, :], 1, 1).astype(BF16)
    grad_mixed.start()


def column_attend_back(sm, I, W, O, G, X):
    (ints,) = sm
    packed, grad_mixed = I
    (gq,) = O
    sc, dsc = X
    pr, gm = packed.wait(), grad_mixed.wait()
    width = gm.shape[1]
    halves = head_masks(128)
    out = gq.ref

    def scores(b, carry):
        rows = pl.ds(pl.multiple_of(b * 128, 128), 128)
        at = pl.ds(pl.multiple_of(b * 32, 32), 32)
        for lo in range(0, width, 128):
            qs = stacked(pr[rows, lo : lo + 128] * 0.125, halves)
            k = pr[rows, width + lo : width + lo + 128]
            v = pr[rows, 2 * width + lo : 2 * width + lo + 128]
            des = stacked(gm[rows, lo : lo + 128], halves)
            sc[at, 2 * lo : 2 * lo + 256] = pick_four(dot(k, qs, 1, 1))
            dsc[at, 2 * lo : 2 * lo + 256] = pick_four(dot(v, des, 1, 1))
        return carry

    lax.fori_loop(0, 8, scores, 0)
    column_softmax(sc, ints[0])

    def pull(b, carry):
        at = pl.ds(pl.multiple_of(b * 32, 32), 32)
        p, dp = sc[at, :], dsc[at, :]
        dsc[at, :] = p * (dp - jnp.sum(p * dp, 0, keepdims=True))
        return carry

    lax.fori_loop(0, 8, pull, 0)

    def spreads(b, carry):
        rows = pl.ds(pl.multiple_of(b * 128, 128), 128)
        at = pl.ds(pl.multiple_of(b * 32, 32), 32)
        for lo in range(0, width, 128):
            qs = stacked(pr[rows, lo : lo + 128] * 0.125, halves)
            k = pr[rows, width + lo : width + lo + 128]
            des = stacked(gm[rows, lo : lo + 128], halves)
            ds = spread_four(dsc[at, 2 * lo : 2 * lo + 256])
            dq = unstack(dot(ds, k, 0, 0)) * 0.125
            out[rows, lo : lo + 128] = dq.astype(BF16)
            out[rows, width + lo : width + lo + 128] = dot(ds, qs, 1, 0).astype(BF16)
            dv = dot(spread_four(sc[at, 2 * lo : 2 * lo + 256]), des, 1, 0)
            out[rows, 2 * width + lo : 2 * width + lo + 128] = dv.astype(BF16)
        return carry

    lax.fori_loop(0, 8, spreads, 0)
    gq.start()


def product_grads(sm, I, W, O, G, X):
    for k, g in enumerate(G):
        weight_grad(g, I[2 * k].wait(), I[2 * k + 1].wait())


def row_back(sm, I, W, O, G, X):
    gq_col, after_row, grad_after, gb = I
    grad_row, branch, grad_mixed, sums = O
    dn, wide = X
    g1, gm = branch.ref, grad_mixed.ref
    width = g1.shape[1]
    wc = W[0].wait()
    gc = gq_col.wait()
    for n in range(0, width, 256):
        dn[:, n : n + 256] = dot(gc[...], wc[:, n : n + 256], 1, 0)
    ar, base, g = after_row.wait(), grad_after.wait(), gb.wait()

    def emit(t, rows):
        put(wide, slice(t, t + 256), 0, rows)

    norm_back(dn, ar, base, g, 1, 1024, emit, sums.ref)
    sums.start()

    def take(t, rows):
        grad_row.ref[t : t + 256, :] = rows
        g1[t : t + 256, :] = rows.astype(BF16)

    to_columns(wide, take)
    grad_row.start()
    wo = W[1].wait()
    for n in range(0, width, 256):
        gm[:, n : n + 256] = dot(g1[...], wo[n : n + 256, :], 1, 1).astype(BF16)
    grad_mixed.start()


def row_attend_back(sm, I, W, O, G, X):
    ints, flts = sm
    packed, grad_mixed, prob, logp, mixed, g1, normed = I
    (gq,) = O
    (sc,) = X
    n_seq, n_col = ints[0], ints[1]
    pr, gm = packed.wait(), grad_mixed.wait()
    width = gm.shape[1]
    heads = width // HD
    halves = head_masks(512)
    for m in range(heads // 2):
        d, v = four(gm, m * 128), four(pr, 2 * width + m * 128)
        for e in range(2):
            h = 2 * m + e
            sc[h * 32 : (h + 1) * 32, :] = pick(dot(d * halves[e], v, 1, 1))
    p, lp = prob.wait()[...], logp.wait()[...]
    dp = sc[...]
    ent = jnp.sum(p * lp, -1, keepdims=True) * -0.25
    row = lax.broadcasted_iota(jnp.int32, ent.shape, 0) % 32
    w = jnp.where(row < n_col, flts[1], 0.0)
    ds = p * (dp - jnp.sum(p * dp, -1, keepdims=True) * 0.25) - w * p * (lp + ent)
    sc[...] = ds
    keep = (lax.broadcasted_iota(jnp.int32, (1024, 1), 0) // 32 < n_seq).astype(F32)
    scale = flts[0]
    out = gq.ref
    for m in range(heads // 2):
        lo = m * 128
        q, k, d = four(pr, lo), four(pr, width + lo), four(gm, lo)
        dq = dk = dv = 0.0
        for e in range(2):
            h = 2 * m + e
            pb = spread(prob.ref[h * 32 : (h + 1) * 32, :])
            sb = spread(sc[h * 32 : (h + 1) * 32, :])
            dq = dq + dot(sb, k * halves[e], 1, 0)
            dk = dk + dot(sb, q * halves[e], 0, 0)
            dv = dv + dot(pb, d * halves[e], 0, 0)
        for t in range(4):
            rows, lanes = slice(t * 256, (t + 1) * 256), slice(t * 128, (t + 1) * 128)
            out[rows, lo : lo + 128] = (
                dq[:, lanes] * (scale * keep[t * 256 : (t + 1) * 256])
            ).astype(BF16)
            out[rows, width + lo : width + lo + 128] = (dk[:, lanes] * scale).astype(BF16)
            out[rows, 2 * width + lo : 2 * width + lo + 128] = dv[:, lanes].astype(BF16)
    gq.start()
    weight_grad(G[0], mixed.wait(), g1.wait())
    weight_grad(G[1], out, normed.wait())


def input_back(sm, I, W, O, G, X):
    gq, x, grad_row, gb = I
    grad_in, sums = O
    (dn,) = X
    width = dn.shape[1]
    gr = gq.wait()
    wt = W[0].wait()
    for n in range(0, width, 256):
        dn[:, n : n + 256] = dot(gr[...], wt[:, n : n + 256], 1, 0)

    def emit(t, rows):
        grad_in.ref[t : t + 256, :] = rows

    norm_back(dn, x.wait(), grad_row.wait(), gb.wait(), 0, 1024, emit, sums.ref)
    grad_in.start()
    sums.start()


class Plan:
    def __init__(self, dp, fsdp, width):
        self.dp, self.fsdp, self.width = dp, fsdp, width
        self.fast = fsdp == 2 and dp % 4 == 0 and dp >= 4
        self.slots = 2 * dp // 2
        if not self.fast:
            return
        zs = dp // 4
        self.zs = zs
        place = [(z, x, c, y) for z in range(zs) for x in range(2) for c in range(2) for y in range(2)]
        index = {p: n for n, p in enumerate(place)}

        def flip(p, first):
            z, x, c, y = p
            return (z, 1 - x, c, y) if (c == 0) == first else (z, x, c, 1 - y)

        def up(p, k):
            return ((p[0] + k) % zs, *p[1:])

        def mate(p):
            return (p[0], p[1], 1 - p[2], p[3])

        def pairs(f):
            return [(n, index[f(p)]) for n, p in enumerate(place)]

        self.one = pairs(lambda p: flip(p, True))
        self.two = pairs(lambda p: flip(p, False))
        self.core = pairs(mate)
        self.ups = [pairs(lambda p, k=k: up(p, k)) for k in range(1, zs)]
        gathered, owners = [], []
        for p in place:
            mine = [[up(r, -k) for k in range(zs)] for r in (p, flip(p, True))]
            far = flip(p, False)
            other = [[up(r, -k) for k in range(zs)] for r in (far, flip(far, True))]
            gathered.append([index[r] for part in (mine, other) for line in part for r in line])
            owners.append(
                [
                    index[up(s, k)]
                    for r in (p, flip(p, True))
                    for s in (r, flip(r, False))
                    for k in range(zs)
                ]
            )
        self.gather_table = np.array(
            [gathered[n] + gathered[index[mate(p)]] for n, p in enumerate(place)], np.int32
        )
        owned = [owners[n] + owners[index[mate(p)]] for n, p in enumerate(place)]
        self.owner_table = np.argsort(np.array(owned, np.int32), 1).astype(np.int32)

    def gather(self, shard):
        def go(v, perm):
            return lax.ppermute(v, AXES, perm)

        line = jnp.stack([shard] + [go(shard, p) for p in self.ups])
        mine = jnp.concatenate([line, go(line, self.one)], 0)
        other = go(mine, self.two)
        return [mine, other, go(mine, self.core), go(other, self.core)]


    def everywhere(self, v):
        if not self.fast:
            return lax.psum(v, AXES)
        for perm in (self.core, self.one, self.two):
            v = v + lax.ppermute(v, AXES, perm)
        return sum((lax.ppermute(v, AXES, perm) for perm in self.ups), v)


class Reduction:
    def __init__(self, plan, grads, names, shards):
        self.plan, self.waiting = plan, []
        self.names = [(n, shards[n].shape[0]) for n in names]
        if plan.fast:
            self.kept, self.sent = grads
        else:
            self.whole = grads

    def go(self, v, perm):
        got = lax.ppermute(v.astype(BF16), AXES, perm)
        self.waiting.append(got)
        return got.astype(F32)

    def landed(self):
        out, self.waiting = self.waiting, []
        return out

    def core(self):
        if not self.plan.fast:
            return
        shape = (2, 2, self.plan.zs) + self.kept.shape[1:]
        got = self.go(self.sent, self.plan.core).reshape(shape)
        self.part = self.kept.astype(F32).reshape(shape) + got

    def first(self):
        if self.plan.fast:
            self.part = self.part[0] + self.go(self.part[1], self.plan.one)

    def second(self):
        if self.plan.fast:
            self.part = self.part[0] + self.go(self.part[1], self.plan.two)

    def last(self):
        if not self.plan.fast:
            return
        total = self.part[0]
        for k, p in enumerate(self.plan.ups):
            total = total + self.go(self.part[k + 1], p)
        self.part = total

    def result(self):
        if self.plan.fast:
            cuts = np.cumsum([rows for _, rows in self.names])[:-1]
            return {n: v for (n, _), v in zip(self.names, jnp.split(self.part, cuts, 0))}
        got = {}
        for (n, _), g in zip(self.names, self.whole):
            half = lax.psum_scatter(g, "dp", scatter_dimension=0, tiled=True)
            got[n] = lax.psum_scatter(half, "fsdp", scatter_dimension=1, tiled=True).astype(F32)
        return got


def local(
    plan,
    alignment_input,
    sequence_mask,
    column_length,
    output_cotangent,
    row_projection_weight,
    row_out_weight,
    column_projection_weight,
    column_out_weight,
    feedforward_in_weight,
    feedforward_out_weight,
    layer_norm_gain,
    layer_norm_bias,
):
    width = alignment_input.shape[3]
    tokens = alignment_input.shape[1] * alignment_input.shape[2]
    heads = width // HD
    hidden = feedforward_out_weight.shape[0] * plan.dp
    x = alignment_input.reshape(tokens, width)
    cot = output_cotangent.reshape(tokens, width)
    shards = dict(
        row_qkv=row_projection_weight.T,
        row_out=row_out_weight,
        col_qkv=column_projection_weight.T,
        col_out=column_out_weight,
        ffn_in=feedforward_in_weight.T,
        ffn_out=feedforward_out_weight,
    )
    whole_rows = {k: v.shape[0] * plan.dp for k, v in shards.items()}
    norms = jnp.concatenate([layer_norm_gain, layer_norm_bias], 0)
    share = norms.shape[1]
    devices = plan.dp * plan.fsdp
    me = lax.axis_index(AXES)
    n_seq = jnp.sum((sequence_mask > 0).astype(jnp.int32))
    n_col = column_length[0].astype(jnp.int32)
    ints = jnp.stack([n_seq, n_col])
    row_scale = 0.125 * lax.rsqrt(n_seq.astype(F32))

    w = {}
    if plan.fast:
        gather_row = lax.dynamic_index_in_dim(jnp.asarray(plan.gather_table), me, 0, False)
        owner_row = lax.dynamic_index_in_dim(jnp.asarray(plan.owner_table), me, 0, False)
        tables = [gather_row, owner_row]
        extra = jnp.concatenate([norms.reshape(-1), n_col.astype(BF16)[None]])
        cols = shards["row_out"].shape[1]
        extra = jnp.pad(extra[None], ((0, 15), (0, cols - extra.shape[0])))
        groups = (("row_qkv",), ("row_out", "col_qkv"), ("col_out", "ffn_in"), ("ffn_out",))
        for gi, names in enumerate(groups):
            parts = [shards[n] for n in names] + ([extra] if gi == 0 else [])
            packed = jnp.concatenate(parts, 0) if len(parts) > 1 else parts[0]
            bufs = plan.gather(packed) if gi < 2 else [lax.all_gather(packed, AXES)]
            row0 = 0
            for n in names:
                rows = shards[n].shape[0]
                w[n] = Weights(bufs, row0, rows, whole_rows[n], width, True, 0 if gi < 2 else None)
                row0 += rows
            if gi == 0:
                tail = jnp.concatenate([b[:, row0, :] for b in bufs], 0)[:, : 6 * share + 1]
        order = (gather_row[None, :] == jnp.arange(devices, dtype=jnp.int32)[:, None]).astype(BF16)
        tail = jnp.dot(order, tail, preferred_element_type=F32)
        gb = tail[:, : 6 * share].reshape(devices, 6, share).transpose(1, 0, 2).reshape(6, width)
        col_total = jnp.sum(tail[:, 6 * share])
    else:
        tables = [jnp.zeros((1,), jnp.int32)] * 2
        for n, s in shards.items():
            half = lax.all_gather(s, "fsdp", axis=1, tiled=True)
            full = lax.all_gather(half, "dp", axis=0, tiled=True)
            w[n] = Weights([full], 0, s.shape[0], whole_rows[n], width, False)
        gb = lax.all_gather(norms, "fsdp", axis=1, tiled=True)
        gb = lax.all_gather(gb, "dp", axis=1, tiled=True).astype(F32)
        col_total = lax.psum(n_col.astype(F32), AXES)
    gb = jnp.pad(gb, ((0, 2), (0, 0)))
    flts = jnp.stack([row_scale, penalty_weight / col_total])

    micros = dict(
        cot=4,
        rowf=9,
        colf=8,
        cola=4,
        ffnf=12,
        fout=7,
        ffnb=12,
        colb=10,
        colt=7,
        colg=7,
        rowb=10,
        rowt=13,
        inpb=9,
        lout=9,
    )

    def arr(n, dtype, rows=tokens, vmem=True, hbm=False):
        return Out((rows, n), dtype, vmem, hbm)

    resident = {}

    def run(name, body, smem, ins, weights, outs, grads=(), scratch=(), deps=()):
        lists = tables + list(smem), ins, [w[n] for n in weights], outs, grads
        return fused(name, body, *lists, plan, resident, micros[name], scratch, deps)

    wide = pltpu.VMEM((tokens, width), F32)
    turn = pltpu.VMEM((width // 128, tokens, 128), F32)
    score = pltpu.VMEM((heads * 32, 128), F32)
    flat = pltpu.VMEM((tokens // 4, 2 * width), F32)
    sums = arr(width, F32, 8, False, True)
    keep = dict(vmem=False, hbm=True)

    (g3,), _ = run("cot", cotangent, [ints], [cot], [], [arr(width, BF16, **keep)], (), [turn])
    (normed_row, packed_row, mixed_row, prob, logp, ent), _ = run(
        "rowf",
        row_forward,
        [ints, flts],
        [x, gb],
        ["row_qkv"],
        [
            arr(width, BF16, **keep),
            arr(3 * width, BF16, **keep),
            arr(width, BF16, hbm=True),
            arr(128, F32, heads * 32, **keep),
            arr(128, F32, heads * 32, **keep),
            arr(128, F32, 8, **keep),
        ],
        (),
        [score],
    )
    (after_row, normed_col, packed_col), _ = run(
        "colf",
        column_forward,
        [],
        [x, mixed_row[0], gb],
        ["row_out", "col_qkv"],
        [arr(width, F32, hbm=True), arr(width, BF16, **keep), arr(3 * width, BF16, hbm=True)],
        (),
        [turn],
    )
    (mixed_col,), _ = run(
        "cola",
        column_attend,
        [ints],
        [packed_col[0]],
        [],
        [arr(width, BF16, hbm=True)],
        (),
        [flat],
    )
    (after_col, normed_ffn, active, slope), _ = run(
        "ffnf",
        feed_forward,
        [],
        [after_row[0], mixed_col[0], gb],
        ["col_out", "ffn_in"],
        [
            arr(width, F32, **keep),
            arr(width, BF16, **keep),
            arr(hidden, BF16, hbm=True),
            arr(hidden, BF16),
        ],
    )
    _, grads = run("fout", ffn_out_grad, [], [active[0], g3], [], [], [hidden])
    r1 = Reduction(plan, grads, ["ffn_out"], shards)
    r1.core()
    (grad_hidden,), grads = run(
        "ffnb",
        ffn_back,
        [],
        [g3, slope, normed_ffn],
        ["ffn_out"],
        [arr(hidden, BF16)],
        [hidden],
    )
    r2 = Reduction(plan, grads, ["ffn_in"], shards)
    r1.first()
    r2.core()
    (grad_after, g2, gm_col, sums_two), _ = run(
        "colb",
        column_back,
        [],
        [grad_hidden, after_col, g3, gb],
        ["ffn_in", "col_out"],
        [arr(width, F32, **keep), arr(width, BF16), arr(width, BF16), sums],
        (),
        [wide],
        r1.landed() + r2.landed(),
    )
    r1.second()
    r2.first()
    (gq_col,), _ = run(
        "colt",
        column_attend_back,
        [ints],
        [packed_col[1], gm_col],
        [],
        [arr(3 * width, BF16)],
        (),
        [flat, flat],
    )
    _, grads = run(
        "colg",
        product_grads,
        [],
        [gq_col, normed_col, mixed_col[1], g2],
        [],
        [],
        [3 * width, width],
        (),
        r1.landed() + r2.landed(),
    )
    r3 = Reduction(plan, grads, ["col_qkv", "col_out"], shards)
    r1.last()
    r2.second()
    r3.core()
    (grad_row, g1, gm_row, sums_one), _ = run(
        "rowb",
        row_back,
        [],
        [gq_col, after_row[1], grad_after, gb],
        ["col_qkv", "row_out"],
        [arr(width, F32, **keep), arr(width, BF16), arr(width, BF16), sums],
        (),
        [wide, turn],
        r2.landed() + r3.landed(),
    )
    r2.last()
    r3.first()
    (gq_row,), grads = run(
        "rowt",
        row_attend_back,
        [ints, flts],
        [packed_row, gm_row, prob, logp, mixed_row[1], g1, normed_row],
        [],
        [arr(3 * width, BF16)],
        [width, 3 * width],
        [score],
        r1.landed() + r3.landed(),
    )
    r4 = Reduction(plan, grads, ["row_out", "row_qkv"], shards)
    r3.second()
    r4.core()
    (grad_in, sums_zero), _ = run(
        "inpb",
        input_back,
        [],
        [gq_row, x, grad_row, gb],
        ["row_qkv"],
        [arr(width, F32, **keep), sums],
        (),
        [wide],
        r2.landed() + r3.landed() + r4.landed(),
    )
    r3.last()
    r4.first()
    (layer_out,), _ = run(
        "lout",
        ffn_result,
        [],
        [active[1], after_col],
        ["ffn_out"],
        [arr(width, BF16, **keep)],
        (),
        [turn],
        r3.landed() + r4.landed(),
    )
    r4.second()
    r4.last()
    got = {}
    for r in (r1, r2, r3, r4):
        got.update(r.result())
    sums_all = jnp.concatenate([sums_zero[:2], sums_one[:2], sums_two[:2]], 0)
    ent_row = jnp.broadcast_to(ent[:1, :1], (1, width))
    sums_all = plan.everywhere(jnp.concatenate([sums_all, ent_row], 0))
    owned = lax.dynamic_slice_in_dim(sums_all[:6], me * share, share, 1)
    gains, biases = owned[0::2], owned[1::2]
    shape = alignment_input.shape
    return (
        layer_out.reshape(shape),
        grad_in.reshape(shape),
        got["row_qkv"].T,
        got["row_out"],
        got["col_qkv"].T,
        got["col_out"],
        got["ffn_in"].T,
        got["ffn_out"],
        gains,
        biases[:2],
        biases[2],
        sums_all[6, 0] / col_total,
    )


def solution(mesh):
    def whole(*args):
        plan = Plan(mesh.shape["dp"], mesh.shape["fsdp"], args[0].shape[3])
        return jax.shard_map(
            lambda *blocks: local(plan, *blocks),
            mesh=mesh,
            in_specs=(
                P(AXES, None, None, None),
                P(AXES, None),
                P(AXES),
                P(AXES, None, None, None),
                P("fsdp", "dp"),
                P("dp", "fsdp"),
                P("fsdp", "dp"),
                P("dp", "fsdp"),
                P("fsdp", "dp"),
                P("dp", "fsdp"),
                P(None, AXES),
                P(None, AXES),
            ),
            out_specs=(
                P(AXES, None, None, None),
                P(AXES, None, None, None),
                P("fsdp", "dp"),
                P("dp", "fsdp"),
                P("fsdp", "dp"),
                P("dp", "fsdp"),
                P("fsdp", "dp"),
                P("dp", "fsdp"),
                P(None, AXES),
                P(None, AXES),
                P(AXES),
                P(),
            ),
            check_vma=False,
        )(*args)

    return whole
```

```python
import jax
import jax.numpy as jnp
import numpy as np
from jax import lax
from jax.experimental import pallas as pl
from jax.experimental.pallas import tpu as pltpu
from jax.sharding import PartitionSpec as P

HD = 64
AXES = ("dp", "fsdp")
norm_eps = 1e-05
penalty_weight = 1.0
masked_score = -1000000000.0
never = -1e30

F32 = jnp.float32
BF16 = jnp.bfloat16
MIB = 1 << 20


def dot(a, b, ca, cb):
    return lax.dot_general(a, b, (((ca,), (cb,)), ((), ())), preferred_element_type=F32)


class Weights:
    def __init__(self, bufs, row0, rows, whole_rows, width, blocked, table=0):
        self.raw = self.here = False
        self.dtype = BF16
        self.bufs, self.row0, self.rows, self.table = bufs, row0, rows, table
        self.whole_rows, self.width, self.blocked = whole_rows, width, blocked


    @staticmethod
    def of(a):
        w = Weights([a], 0, a.shape[0], a.shape[0], a.shape[1], False)
        w.dtype = a.dtype
        return w

    @staticmethod
    def held(a):
        w = Weights.of(a)
        w.here = True
        return w

    def copies(self, plan):
        if self.here:
            return 0
        return sum(b.shape[0] for b in self.bufs) if self.blocked else 1


class Loaded:
    def __init__(self, ref, copies):
        self.ref, self.copies = ref, copies

    def start(self, part=None):
        for c in self.copies if part is None else self.copies[part : part + 1]:
            c.start()

    def wait(self):
        for c in self.copies:
            c.wait()
        return self.ref


class Out:
    def __init__(self, shape, dtype, vmem=True, hbm=False):
        self.shape, self.dtype, self.vmem, self.hbm = shape, dtype, vmem, hbm
        self.parts = max(1, shape[1] // 768) if hbm else 0


def fused(
    name, body, smem, ins, weights, outs, grads, plan, resident, micros, scratch=(), deps=(), fetch=()
):
    arrays, index, spaces = [], {}, []

    def slot(a):
        if id(a) not in index:
            index[id(a)] = len(arrays)
            stays = id(a) in resident
            spaces.append(pltpu.VMEM if stays else pltpu.HBM)
            arrays.append(pltpu.with_memory_space_constraint(a, spaces[-1]))
        return index[id(a)]

    in_slots = [slot(a) for a in ins]
    w_slots = [[slot(b) for b in w.bufs] for w in (*weights, *fetch)]
    weights = list(weights)
    n_weights = len(weights)
    for a in deps:
        arrays.append(a)
        spaces.append(pl.ANY)
    n_smem = len(smem)
    vm, n_sem = [], 0
    for a in ins:
        if id(a) not in resident:
            vm.append(pltpu.VMEM(a.shape, a.dtype))
            n_sem += 1
    for w in (*weights, *fetch):
        n_sem += w.copies(plan)
    for w in weights:
        if w.here:
            continue
        raw = (w.whole_rows // w.rows * plan.fsdp, w.rows, w.width // plan.fsdp)
        vm.append(pltpu.VMEM(raw if w.raw else (w.whole_rows, w.width), BF16))
    out_shapes, out_spaces = [], []
    for o in outs:
        if o.vmem:
            out_shapes.append(pltpu.VMEM(o.shape, o.dtype))
            out_spaces.append(pltpu.VMEM)
        else:
            vm.append(pltpu.VMEM(o.shape, o.dtype))
        if o.hbm:
            out_shapes.append(pltpu.HBM(o.shape, o.dtype))
            out_spaces.append(pltpu.HBM)
            n_sem += o.parts
    f_at = len(out_shapes)
    for w in fetch:
        out_shapes.append(pltpu.VMEM((w.whole_rows, w.width), w.dtype))
        out_spaces.append(pltpu.VMEM)
    g_at = len(out_shapes)
    width = plan.width
    for rows in grads:
        vm.append(pltpu.VMEM((rows, width), BF16))
        n_sem += plan.dp * plan.fsdp if plan.fast else 1
    if grads and plan.fast:
        per = sum(rows // plan.dp for rows in grads)
        shape = pltpu.HBM((plan.slots, per, width // plan.fsdp), BF16)
        out_shapes += [shape, shape]
    elif grads:
        out_shapes += [pltpu.HBM((rows, width), BF16) for rows in grads]
    out_spaces += [pltpu.HBM] * (len(out_shapes) - g_at)
    n_in, n_out, n_vm = len(arrays), len(out_shapes), len(vm)
    used_vmem = sum(int(np.prod(m.shape)) * np.dtype(m.dtype).itemsize for m in (*vm, *scratch))

    def kernel(*refs):
        sm = refs[:n_smem]
        hb = refs[n_smem : n_smem + n_in]
        ob = refs[n_smem + n_in : n_smem + n_in + n_out]
        rest = refs[n_smem + n_in + n_out :]
        vrefs, extra, sems = list(rest[:n_vm]), rest[n_vm:-1], rest[-1]
        used = [0]

        def sem():
            used[0] += 1
            return sems.at[used[0] - 1]

        loads = Loads()
        for a, s in zip(ins, in_slots):
            if id(a) in resident:
                loads.append(Loaded(hb[s], []))
            else:
                ref = vrefs.pop(0)
                loads.append(Loaded(ref, [pltpu.make_async_copy(hb[s], ref, sem())]))
        wl = []
        for n, (w, slots) in enumerate(zip((*weights, *fetch), w_slots)):
            copies = []
            if w.here:
                dst = hb[slots[0]]
            elif n < n_weights:
                dst = vrefs.pop(0)
            else:
                dst = ob[f_at + n - n_weights]
            if w.here:
                pass
            elif w.blocked:
                cols = w.width // plan.fsdp
                count = 0
                for s in slots:
                    for j in range(arrays[s].shape[0]):
                        block = sm[w.table][count] if w.table is not None else count
                        count += 1
                        row = (block // plan.fsdp) * w.rows
                        col = (block % plan.fsdp) * cols
                        if w.table is not None:
                            row, col = pl.multiple_of(row, 16), pl.multiple_of(col, 128)
                        spot = dst.at[pl.ds(row, w.rows), pl.ds(col, cols)]
                        if w.raw:
                            spot = dst.at[count - 1]
                        src = hb[s].at[j, pl.ds(w.row0, w.rows), :]
                        copies.append(pltpu.make_async_copy(src, spot, sem()))
            else:
                copies.append(pltpu.make_async_copy(hb[slots[0]], dst, sem()))
            (wl if n < n_weights else loads.fetched).append(Loaded(dst, copies))
        ol = []
        at = 0
        for o in outs:
            if o.vmem:
                ref = ob[at]
                at += 1
            else:
                ref = vrefs.pop(0)
            copies = []
            if o.hbm:
                for k in range(o.parts):
                    lanes = slice(None)
                    if o.parts > 1:
                        lanes = pl.ds(k * 768, 768)
                    copies.append(
                        pltpu.make_async_copy(ref.at[:, lanes], ob[at].at[:, lanes], sem())
                    )
                at += 1
            ol.append(Loaded(ref, copies))
        gl = []
        row0 = 0
        for k, rows in enumerate(grads):
            src = vrefs.pop(0)
            if plan.fast:
                gl.append(Blocks(src, ob[g_at], ob[g_at + 1], sm[1], plan, rows, row0, sem))
                row0 += rows // plan.dp
            else:
                gl.append(Loaded(src, [pltpu.make_async_copy(src, ob[g_at + k], sem())]))
        for l in (*wl, *loads):
            l.start()
        body(sm[:1] + sm[2:] if name == "rowf" else sm[2:], loads, wl, ol, gl, extra)
        for l in (*ol, *gl, *loads.fetched):
            l.wait()

    res = pl.pallas_call(
        kernel,
        name=name,
        out_shape=out_shapes,
        in_specs=[pl.BlockSpec(memory_space=pltpu.SMEM)] * n_smem
        + [pl.BlockSpec(memory_space=m) for m in spaces],
        out_specs=[pl.BlockSpec(memory_space=m) for m in out_spaces],
        scratch_shapes=vm + list(scratch) + [pltpu.SemaphoreType.DMA((n_sem,))],
        compiler_params=pltpu.CompilerParams(vmem_limit_bytes=used_vmem + 7 * MIB),
        cost_estimate=pl.CostEstimate(
            flops=int(micros * 1e6), bytes_accessed=int(micros * 3e3), transcendentals=0
        ),
    )(*smem, *arrays)
    got, at = [], 0
    for o in outs:
        both = res[at : at + o.vmem + o.hbm]
        at += o.vmem + o.hbm
        if o.vmem:
            resident[id(both[0])] = both[0]
        got.append(both[0] if len(both) == 1 else both)
    for a in res[f_at:g_at]:
        resident[id(a)] = a
        got.append(Weights.held(a))
    return got, res[g_at:]


class Loads(list):
    def __init__(self):
        self.fetched = []

    def later(self):
        for l in self.fetched:
            l.start()


class Blocks:
    def __init__(self, ref, kept, sent, table, plan, rows, row0, sem):
        self.ref, self.plan = ref, plan
        self.per, self.cols = rows // plan.dp, plan.width // plan.fsdp
        self.kept, self.sent, self.table, self.row0 = kept, sent, table, row0
        self.sems = [sem() for _ in range(plan.dp * plan.fsdp)]
        self.begun = 0

    def copy(self, n, out, slot):
        row, col = (n // self.plan.fsdp) * self.per, (n % self.plan.fsdp) * self.cols
        return pltpu.make_async_copy(
            self.ref.at[row : row + self.per, col : col + self.cols],
            out.at[slot, pl.ds(self.row0, self.per), :],
            self.sems[n],
        )

    def start(self, rows=None):
        rows = self.ref.shape[0] if rows is None else rows
        end = rows // self.per * self.plan.fsdp
        slots = self.plan.slots
        for n in range(self.begun, end):
            place = self.table[n]

            @pl.when(place < slots)
            def _():
                self.copy(n, self.kept, place).start()

            @pl.when(place >= slots)
            def _():
                self.copy(n, self.sent, place - slots).start()

        self.begun = end

    def wait(self):
        for n in range(self.begun):
            self.copy(n, self.kept, 0).wait()


def stamp(out):
    out.ref[...] = jnp.zeros(out.ref.shape, out.ref.dtype)
    out.start()


def normal_form(v):
    centred = v - jnp.mean(v, -1, keepdims=True)
    rstd = lax.rsqrt(jnp.mean(centred * centred, -1, keepdims=True) + norm_eps)
    return centred * rstd, rstd


def norm_rows(src, dst, gb, k, total):
    for t in range(0, total, 256):
        xhat, _ = normal_form(src[t : t + 256, :].astype(F32))
        dst[t : t + 256, :] = (xhat * gb[k : k + 1, :] + gb[k + 3 : k + 4, :]).astype(BF16)


def norm_back(dn_ref, src, base, gb, k, total, emit, sums):
    gain = gb[k : k + 1, :]
    gain_sum = jnp.zeros_like(gain)
    bias_sum = jnp.zeros_like(gain)
    for t in range(0, total, 256):
        xhat, rstd = normal_form(src[t : t + 256, :].astype(F32))
        dn = dn_ref[t : t + 256, :]
        gain_sum = gain_sum + jnp.sum(dn * xhat, 0, keepdims=True)
        bias_sum = bias_sum + jnp.sum(dn, 0, keepdims=True)
        dx = dn * gain
        low = jnp.mean(dx, -1, keepdims=True)
        mix = jnp.mean(dx * xhat, -1, keepdims=True)
        emit(t, base[t : t + 256, :].astype(F32) + rstd * (dx - low - xhat * mix))
    none = jnp.zeros((1, gain.shape[1]), F32)
    rows = [none] * (2 * k) + [gain_sum, bias_sum] + [none] * (6 - 2 * k)
    sums[...] = jnp.concatenate(rows, 0)


def head_masks(lanes):
    lane = lax.broadcasted_iota(jnp.int32, (1, lanes), 1)
    low = ((lane // HD) % 2 == 0).astype(F32)
    return low.astype(BF16), (1.0 - low).astype(BF16)


def four(ref, col):
    return jnp.concatenate([ref[g * 256 : (g + 1) * 256, col : col + 128] for g in range(4)], 1)


def pick(big):
    seg = lax.broadcasted_iota(jnp.int32, (32, 256), 1) // 32
    out = big[:32, :]
    for k in range(1, 8):
        out = jnp.where(seg == k, big[k * 32 : (k + 1) * 32, :], out)
    out = out[:, :128] + out[:, 128:]
    out = out + pltpu.roll(out, 64, 1)
    return out + pltpu.roll(out, 32, 1)


def spread(small):
    seg = lax.broadcasted_iota(jnp.int32, (32, 256), 1) // 32
    wide = jnp.concatenate([small, small], 1)
    return jnp.concatenate([jnp.where(seg == k, wide, 0.0).astype(BF16) for k in range(8)], 0)


def gathered_norms(blocks, table):
    slots = blocks.shape[0]
    values = jnp.sum(blocks[...].astype(F32), 1).astype(BF16)
    place = lax.broadcasted_iota(jnp.int32, (slots, 1), 0)
    owner = jnp.zeros((slots, 1), jnp.int32)
    for j in range(slots):
        owner = jnp.where(place == j, table[j], owner)
    share = 768 // slots
    lane = lax.broadcasted_iota(jnp.int32, (1, 768), 1)
    row = lax.broadcasted_iota(jnp.int32, (values.shape[1], 1), 0)
    mine = lane // share == owner
    rows = []
    for k in range(6):
        spot = (row == k * share + lane % share).astype(F32).astype(BF16)
        rows.append(jnp.sum(jnp.where(mine, dot(values, spot, 1, 0), 0.0), 0, keepdims=True))
    count = jnp.where(lax.broadcasted_iota(jnp.int32, (1, values.shape[1]), 1) == 6 * share, 1.0, 0.0)
    total = jnp.sum(values.astype(F32) * count)
    rows.append(jnp.full((1, 768), total, F32))
    rows.append(jnp.zeros((1, 768), F32))
    return jnp.concatenate(rows, 0)


def row_forward(sm, I, W, O, G, X):
    ints, flts = sm[-2:]
    x = I[0]
    normed, packed, mixed, prob, logp, ent, norms = O
    sc = X[0]
    if len(W) > 1:
        norms.ref[...] = gathered_norms(W[1].wait(), sm[0])
    else:
        norms.ref[...] = I[1].wait()[...]
    norms.start()
    xr, g = x.wait(), norms.ref
    norm_rows(xr, normed.ref, g, 0, 1024)
    normed.start()
    wt = W[0].wait()
    nr = normed.ref[...]
    n_seq, n_col = ints[0], ints[1]
    keep = (lax.broadcasted_iota(jnp.int32, (1024, 1), 0) // 32 < n_seq).astype(F32)
    width = nr.shape[1]
    heads = width // HD
    pr = packed.ref
    for n in range(0, 3 * width, 256):
        out = dot(nr, wt[n : n + 256, :], 1, 1)
        if n < width:
            out = out * keep
        pr[:, n : n + 256] = out.astype(BF16)
        if (n + 256) % 768 == 0:
            packed.start(n // 768)
    halves = head_masks(512)
    for m in range(heads // 2):
        q, k = four(pr, m * 128), four(pr, width + m * 128)
        for e in range(2):
            h = 2 * m + e
            sc[h * 32 : (h + 1) * 32, :] = pick(dot(q * halves[e], k, 1, 1))
    lane = lax.broadcasted_iota(jnp.int32, (1, 128), 1) % 32
    s = jnp.where(lane < n_col, sc[...] * flts[0], masked_score)
    top = jnp.max(s, -1, keepdims=True)
    total = jnp.sum(jnp.exp(s - top), -1, keepdims=True) * 0.25
    lp = s - (top + jnp.log(total))
    p = jnp.exp(lp)
    prob.ref[...] = p
    logp.ref[...] = lp
    prob.start()
    logp.start()
    entropy = jnp.sum(p * lp, -1, keepdims=True) * -0.25
    row = lax.broadcasted_iota(jnp.int32, entropy.shape, 0) % 32
    total = jnp.sum(jnp.where(row < n_col, entropy, 0.0))
    ent.ref[...] = jnp.where(lax.broadcasted_iota(jnp.int32, ent.ref.shape, 0) == 6, total, 0.0)
    ent.start()
    second = (lax.broadcasted_iota(jnp.int32, (1, 512), 1) // HD) % 2 == 1
    for m in range(heads // 2):
        v = four(pr, 2 * width + m * 128)
        both = [
            dot(spread(prob.ref[h * 32 : (h + 1) * 32, :]), v, 1, 0) for h in (2 * m, 2 * m + 1)
        ]
        out = jnp.where(second, both[1], both[0]).astype(BF16)
        for t in range(4):
            mixed.ref[t * 256 : (t + 1) * 256, m * 128 : (m + 1) * 128] = out[
                :, t * 128 : (t + 1) * 128
            ]
    mixed.start()


def stacked(x, halves):
    return jnp.concatenate([x * halves[0], x * halves[1]], 0)


def segment(rows):
    return (lax.broadcasted_iota(jnp.int32, (rows, 256), 1) // 32) % 4


def pick_four(big):
    seg = segment(32)
    out = big[:32, :]
    for k in range(1, 4):
        out = jnp.where(seg == k, big[k * 32 : (k + 1) * 32, :], out)
    return out


def spread_four(small):
    seg = segment(32)
    return jnp.concatenate([jnp.where(seg == k, small, 0.0).astype(BF16) for k in range(4)], 0)


def unstack(both):
    lane = lax.broadcasted_iota(jnp.int32, (128, 128), 1)
    return jnp.where(lane < HD, both[:128], both[128:])


def to_columns(src, take):
    for t in range(0, 1024, 256):
        lanes = [
            jnp.concatenate([src[j, pl.ds(t // 32 + k, 32, stride=32), :] for k in range(8)], 0)
            for j in range(src.shape[0])
        ]
        take(t, jnp.concatenate(lanes, 1))


def put(dst, rows, n, value):
    for j in range(value.shape[1] // 128):
        dst[n // 128 + j, rows, :] = value[:, j * 128 : (j + 1) * 128]


def column_forward(sm, I, W, O, G, X):
    x, mixed_row, gb = I
    after, normed, packed = O
    (ar,) = X
    width = normed.ref.shape[1]
    mr, xr = mixed_row.wait(), x.wait()
    wo = W[0].wait()
    for n in range(0, width, 256):
        out = xr[:, n : n + 256].astype(F32) + dot(mr[...], wo[:, n : n + 256], 1, 0)
        put(ar, slice(None), n, out)
    g = gb.wait()

    def take(t, rows):
        after.ref[t : t + 256, :] = rows

    to_columns(ar, take)
    after.start()
    norm_rows(after.ref, normed.ref, g, 1, 1024)
    normed.start()
    wt = W[1].wait()
    nr = normed.ref[...]
    pr = packed.ref
    for n in range(0, 3 * width, 256):
        pr[:, n : n + 256] = dot(nr, wt[n : n + 256, :], 1, 1).astype(BF16)
        if (n + 256) % 768 == 0:
            packed.start(n // 768)


def column_softmax(sc, n_seq):
    def block(b, carry):
        at = pl.ds(pl.multiple_of(b * 32, 32), 32)
        s = sc[at, :]
        s = jnp.where(lax.broadcasted_iota(jnp.int32, s.shape, 0) < n_seq, s, never)
        p = jnp.exp(s - jnp.max(s, 0, keepdims=True))
        sc[at, :] = p * (1.0 / jnp.sum(p, 0, keepdims=True))
        return carry

    lax.fori_loop(0, sc.shape[0] // 32, block, 0)


def column_attend(sm, I, W, O, G, X):
    (ints,) = sm
    (mixed,) = O
    (sc,) = X
    width = mixed.ref.shape[1]
    pr = I[0].wait()
    halves = head_masks(128)

    def scores(b, carry):
        rows = pl.ds(pl.multiple_of(b * 128, 128), 128)
        at = pl.ds(pl.multiple_of(b * 32, 32), 32)
        for lo in range(0, width, 128):
            qs = stacked(pr[rows, lo : lo + 128] * 0.125, halves)
            k = pr[rows, width + lo : width + lo + 128]
            sc[at, 2 * lo : 2 * lo + 256] = pick_four(dot(k, qs, 1, 1))
        return carry

    lax.fori_loop(0, 8, scores, 0)
    column_softmax(sc, ints[0])

    def mix(b, carry):
        rows = pl.ds(pl.multiple_of(b * 128, 128), 128)
        at = pl.ds(pl.multiple_of(b * 32, 32), 32)
        for lo in range(0, width, 128):
            v = pr[rows, 2 * width + lo : 2 * width + lo + 128]
            p = spread_four(sc[at, 2 * lo : 2 * lo + 256])
            mixed.ref[rows, lo : lo + 128] = unstack(dot(p, v, 0, 0)).astype(BF16)
        return carry

    lax.fori_loop(0, 8, mix, 0)
    mixed.start()


def feed_forward(sm, I, W, O, G, X):
    after_row, mixed, gb = I
    after, normed, active, slope = O
    width = normed.ref.shape[1]
    hidden = active.ref.shape[1]
    ar, mr = after_row.wait(), mixed.wait()
    wo = W[0].wait()
    for n in range(0, width, 256):
        after.ref[:, n : n + 256] = ar[:, n : n + 256] + dot(mr[...], wo[:, n : n + 256], 1, 0)
    after.start()
    norm_rows(after.ref, normed.ref, gb.wait(), 2, 1024)
    normed.start()
    wt = W[1].wait()
    I.later()
    nr = normed.ref[...]
    for n in range(0, hidden, 256):
        h = dot(nr, wt[n : n + 256, :], 1, 1)
        cdf = 0.5 + 0.5 * lax.erf(h * (0.5**0.5))
        active.ref[:, n : n + 256] = (h * cdf).astype(BF16)
        bell = jnp.exp(h * h * -0.5) * (0.5 / np.pi) ** 0.5
        slope.ref[:, n : n + 256] = (cdf + h * bell).astype(BF16)
        if (n + 256) % 768 == 0:
            active.start(n // 768)
    slope.start()


def weight_grad(dst, left, right, step=768):
    rows = dst.ref.shape[0]
    blocks = isinstance(dst, Blocks)
    for n in range(0, rows, step):
        dst.ref[n : n + step, :] = dot(left[:, n : n + step], right[...], 0, 0).astype(BF16)
        if blocks:
            dst.start(n + step)
    if not blocks:
        dst.start()


def ffn_out_grad(sm, I, W, O, G, X):
    (ints,) = sm
    active, cot = I
    (g3,) = O
    (wide,) = X
    put(wide, slice(None), 0, cot.wait()[...].astype(F32))
    n_seq, n_col = ints[0], ints[1]

    def take(t, rows):
        at = lax.broadcasted_iota(jnp.int32, (256, 1), 0) + t
        keep = ((at % 32 < n_seq) & (at // 32 < n_col)).astype(F32)
        g3.ref[t : t + 256, :] = (rows * keep).astype(BF16)

    to_columns(wide, take)
    g3.start()
    weight_grad(G[0], active.wait(), g3.ref)


def ffn_back(sm, I, W, O, G, X):
    g3, slope, normed = I
    (grad_hidden,) = O
    wf = W[0].wait()
    gr, sl = g3.wait(), slope.wait()
    I.later()
    gh = grad_hidden.ref
    hidden = gh.shape[1]
    gv = gr[...]
    for n in range(0, hidden, 256):
        d = dot(gv, wf[n : n + 256, :], 1, 1)
        gh[:, n : n + 256] = (d * sl[:, n : n + 256].astype(F32)).astype(BF16)
    grad_hidden.start()
    weight_grad(G[0], gh, normed.wait())


def ffn_result(sm, I, W, O, G, X):
    active, after = I
    layer_out = O[0]
    (res,) = X
    width = layer_out.ref.shape[1]
    wf = W[0].wait()
    ac, ar = active.wait(), after.wait()
    I.later()
    for n in range(0, width, 256):
        put(res, slice(None), n, ar[:, n : n + 256] + dot(ac[...], wf[:, n : n + 256], 1, 0))

    def take(t, rows):
        layer_out.ref[t : t + 256, :] = rows.astype(BF16)

    to_columns(res, take)
    layer_out.start()
    stamp(O[1])


def column_back(sm, I, W, O, G, X):
    grad_hidden, after_col, g3, gb = I
    grad_after, branch, grad_mixed, sums = O
    (dn,) = X
    g2, gm = branch.ref, grad_mixed.ref
    width = g2.shape[1]
    gh = grad_hidden.wait()
    wf = W[0].wait()
    I.later()
    for n in range(0, width, 256):
        dn[:, n : n + 256] = dot(gh[...], wf[:, n : n + 256], 1, 0)
    ac, base, g = after_col.wait(), g3.wait(), gb.wait()

    def emit(t, rows):
        grad_after.ref[t : t + 256, :] = rows
        g2[t : t + 256, :] = rows.astype(BF16)

    norm_back(dn, ac, base, g, 2, 1024, emit, sums.ref)
    grad_after.start()
    sums.start()
    wo = W[1].wait()
    for n in range(0, width, 256):
        gm[:, n : n + 256] = dot(g2[...], wo[n : n + 256, :], 1, 1).astype(BF16)
    grad_mixed.start()


def column_attend_back(sm, I, W, O, G, X):
    (ints,) = sm
    packed, grad_mixed = I
    gq = O[0]
    sc, dsc = X
    pr, gm = packed.wait(), grad_mixed.wait()
    I.later()
    width = gm.shape[1]
    halves = head_masks(128)
    out = gq.ref

    def scores(b, carry):
        rows = pl.ds(pl.multiple_of(b * 128, 128), 128)
        at = pl.ds(pl.multiple_of(b * 32, 32), 32)
        for lo in range(0, width, 128):
            qs = stacked(pr[rows, lo : lo + 128] * 0.125, halves)
            k = pr[rows, width + lo : width + lo + 128]
            v = pr[rows, 2 * width + lo : 2 * width + lo + 128]
            des = stacked(gm[rows, lo : lo + 128], halves)
            sc[at, 2 * lo : 2 * lo + 256] = pick_four(dot(k, qs, 1, 1))
            dsc[at, 2 * lo : 2 * lo + 256] = pick_four(dot(v, des, 1, 1))
        return carry

    lax.fori_loop(0, 8, scores, 0)
    column_softmax(sc, ints[0])

    def pull(b, carry):
        at = pl.ds(pl.multiple_of(b * 32, 32), 32)
        p, dp = sc[at, :], dsc[at, :]
        dsc[at, :] = p * (dp - jnp.sum(p * dp, 0, keepdims=True))
        return carry

    lax.fori_loop(0, 8, pull, 0)

    def spreads(b, carry):
        rows = pl.ds(pl.multiple_of(b * 128, 128), 128)
        at = pl.ds(pl.multiple_of(b * 32, 32), 32)
        for lo in range(0, width, 128):
            qs = stacked(pr[rows, lo : lo + 128] * 0.125, halves)
            k = pr[rows, width + lo : width + lo + 128]
            des = stacked(gm[rows, lo : lo + 128], halves)
            ds = spread_four(dsc[at, 2 * lo : 2 * lo + 256])
            dq = unstack(dot(ds, k, 0, 0)) * 0.125
            out[rows, lo : lo + 128] = dq.astype(BF16)
            out[rows, width + lo : width + lo + 128] = dot(ds, qs, 1, 0).astype(BF16)
            dv = dot(spread_four(sc[at, 2 * lo : 2 * lo + 256]), des, 1, 0)
            out[rows, 2 * width + lo : 2 * width + lo + 128] = dv.astype(BF16)
        return carry

    lax.fori_loop(0, 8, spreads, 0)
    gq.start()
    stamp(O[1])


def product_grads(sm, I, W, O, G, X):
    I.later()
    for k, g in enumerate(G):
        weight_grad(g, I[2 * k].wait(), I[2 * k + 1].wait())


def row_back(sm, I, W, O, G, X):
    gq_col, after_row, grad_after, gb = I
    grad_row, branch, grad_mixed, sums = O
    dn, wide = X
    g1, gm = branch.ref, grad_mixed.ref
    width = g1.shape[1]
    wc = W[0].wait()
    gc = gq_col.wait()
    I.later()
    for n in range(0, width, 256):
        dn[:, n : n + 256] = dot(gc[...], wc[:, n : n + 256], 1, 0)
    ar, base, g = after_row.wait(), grad_after.wait(), gb.wait()

    def emit(t, rows):
        put(wide, slice(t, t + 256), 0, rows)

    norm_back(dn, ar, base, g, 1, 1024, emit, sums.ref)
    sums.start()

    def take(t, rows):
        grad_row.ref[t : t + 256, :] = rows
        g1[t : t + 256, :] = rows.astype(BF16)

    to_columns(wide, take)
    grad_row.start()
    wo = W[1].wait()
    for n in range(0, width, 256):
        gm[:, n : n + 256] = dot(g1[...], wo[n : n + 256, :], 1, 1).astype(BF16)
    grad_mixed.start()


def row_attend_back(sm, I, W, O, G, X):
    ints, flts = sm
    packed, grad_mixed, prob, logp, mixed, g1, normed, gb = I
    (gq,) = O
    (sc,) = X
    n_seq, n_col = ints[0], ints[1]
    pr, gm = packed.wait(), grad_mixed.wait()
    I.later()
    width = gm.shape[1]
    heads = width // HD
    halves = head_masks(512)
    for m in range(heads // 2):
        d, v = four(gm, m * 128), four(pr, 2 * width + m * 128)
        for e in range(2):
            h = 2 * m + e
            sc[h * 32 : (h + 1) * 32, :] = pick(dot(d * halves[e], v, 1, 1))
    p, lp = prob.wait()[...], logp.wait()[...]
    dp = sc[...]
    ent = jnp.sum(p * lp, -1, keepdims=True) * -0.25
    row = lax.broadcasted_iota(jnp.int32, ent.shape, 0) % 32
    w = jnp.where(row < n_col, penalty_weight / gb.wait()[6:7, 0:1], 0.0)
    ds = p * (dp - jnp.sum(p * dp, -1, keepdims=True) * 0.25) - w * p * (lp + ent)
    sc[...] = ds
    keep = (lax.broadcasted_iota(jnp.int32, (1024, 1), 0) // 32 < n_seq).astype(F32)
    scale = flts[0]
    out = gq.ref
    for m in range(heads // 2):
        lo = m * 128
        q, k, d = four(pr, lo), four(pr, width + lo), four(gm, lo)
        dq = dk = dv = 0.0
        for e in range(2):
            h = 2 * m + e
            pb = spread(prob.ref[h * 32 : (h + 1) * 32, :])
            sb = spread(sc[h * 32 : (h + 1) * 32, :])
            dq = dq + dot(sb, k * halves[e], 1, 0)
            dk = dk + dot(sb, q * halves[e], 0, 0)
            dv = dv + dot(pb, d * halves[e], 0, 0)
        for t in range(4):
            rows, lanes = slice(t * 256, (t + 1) * 256), slice(t * 128, (t + 1) * 128)
            out[rows, lo : lo + 128] = (
                dq[:, lanes] * (scale * keep[t * 256 : (t + 1) * 256])
            ).astype(BF16)
            out[rows, width + lo : width + lo + 128] = (dk[:, lanes] * scale).astype(BF16)
            out[rows, 2 * width + lo : 2 * width + lo + 128] = dv[:, lanes].astype(BF16)
    gq.start()
    weight_grad(G[0], mixed.wait(), g1.wait())
    weight_grad(G[1], out, normed.wait())


def input_back(sm, I, W, O, G, X):
    gq, x, grad_row, gb = I
    grad_in, sums = O
    (dn,) = X
    width = dn.shape[1]
    gr = gq.wait()
    wt = W[0].wait()
    I.later()
    for n in range(0, width, 256):
        dn[:, n : n + 256] = dot(gr[...], wt[:, n : n + 256], 1, 0)

    def emit(t, rows):
        grad_in.ref[t : t + 256, :] = rows

    norm_back(dn, x.wait(), grad_row.wait(), gb.wait(), 0, 1024, emit, sums.ref)
    grad_in.start()
    sums.start()


class Plan:
    def __init__(self, dp, fsdp, width):
        self.dp, self.fsdp, self.width = dp, fsdp, width
        self.fast = fsdp == 2 and dp == 16
        self.slots = dp * fsdp // 2
        if not self.fast:
            return
        place = [(z, x, c, y) for z in range(4) for x in range(2) for c in range(2) for y in range(2)]
        index = {p: n for n, p in enumerate(place)}

        def one(p):
            z, x, c, y = p
            return (z, 1 - x, c, y) if c == 0 else (z, x, c, 1 - y)

        def two(p):
            z, x, c, y = p
            return (z, 1 - x, c, y) if c == 1 else (z, x, c, 1 - y)

        def next_to(p):
            return (p[0] ^ 1, *p[1:])

        def across(p):
            return (p[0] ^ 2, *p[1:])

        def mate(p):
            return (p[0], p[1], 1 - p[2], p[3])

        def pairs(f):
            return [(n, index[f(p)]) for n, p in enumerate(place)]

        self.one, self.two, self.core = pairs(one), pairs(two), pairs(mate)
        self.next_to, self.across = pairs(next_to), pairs(across)
        gathered, owners = [], []
        for p in place:
            held = [p]
            for f in (across, next_to, one, two):
                held = held + [f(q) for q in held]
            gathered.append([index[q] for q in held])
            owned = [p]
            for f in (across, next_to, two, one):
                owned = owned + [f(q) for q in owned]
            owners.append([index[q] for q in owned])
        mates = [index[mate(p)] for p in place]
        self.gather_table = np.array([gathered[n] + gathered[m] for n, m in enumerate(mates)], np.int32)
        owned = np.array([owners[n] + owners[m] for n, m in enumerate(mates)], np.int32)
        self.owner_table = np.argsort(owned, 1).astype(np.int32)

    def go(self, v, perm):
        return lax.ppermute(v, AXES, perm)

    def everywhere(self, v, others, beside):
        if not self.fast:
            return lax.psum(v, AXES)
        v = after(v, *others)
        for perm in (self.core, self.one):
            v = v + lax.ppermute(v, AXES, perm)
        v = after(v, *beside.second_came)
        for perm in (self.two, self.next_to):
            v = v + lax.ppermute(v, AXES, perm)
        v = after(v, *beside.third_came)
        return v + lax.ppermute(v, AXES, self.across)


def after(v, *others):
    return lax.optimization_barrier((v, *others))[0]


class Gathering:
    def __init__(self, plan, shard):
        self.plan, self.have = plan, [shard[None]]

    def all(self, others):
        if others:
            self.have = list(lax.optimization_barrier((*self.have, *others)))[: len(self.have)]
        self.have = [jnp.concatenate(self.have, 0)] if len(self.have) > 1 else self.have
        return self.have[0]

    def step(self, perm, *others):
        self.came = self.plan.go(self.all(others), perm)
        self.have.append(self.came)
        return self.came

    def far(self, *others):
        self.mine = self.all(others)
        self.came = self.plan.go(self.mine, self.plan.two)
        return self.came

    def share(self, *others):
        mine = after(self.mine, *others) if others else self.mine
        self.mate = self.plan.go(mine, self.plan.core)
        return self.mate

    def last(self, *others):
        far = after(self.came, *others) if others else self.came
        self.end = self.plan.go(far, self.plan.core)
        return [self.mine, self.came, self.mate, self.end]


class Reduction:
    def __init__(self, plan, grads, names, shards):
        self.plan = plan
        self.names = [(n, shards[n].shape[0]) for n in names]
        if plan.fast:
            kept, self.sent = grads
            self.terms, self.size = [kept], kept.shape[0]
        else:
            self.whole = grads

    def go(self, v, perm):
        return lax.ppermute(v.astype(BF16), AXES, perm)

    def landed(self):
        return [self.came] if self.plan.fast else []

    def core(self, *others):
        if self.plan.fast:
            sent = after(self.sent, *others) if others else self.sent
            self.came = self.go(sent, self.plan.core)

    def total(self, start, stop):
        return sum(t[start:stop].astype(F32) for t in self.terms)

    def step(self, perm, *others):
        if self.plan.fast:
            came = after(self.came, *others) if others else self.came
            self.terms.append(came)
            self.size //= 2
            self.came = self.go(self.total(self.size, 2 * self.size), perm)

    def first(self, *others):
        self.step(self.plan.fast and self.plan.one, *others)

    def second(self, *others):
        self.step(self.plan.fast and self.plan.two, *others)

    def third(self, *others):
        self.second_came = self.landed()
        self.step(self.plan.fast and self.plan.next_to, *others)

    def fourth(self, *others):
        self.third_came = self.landed()
        self.step(self.plan.fast and self.plan.across, *others)

    def finish(self, *others):
        if self.plan.fast:
            self.terms.append(after(self.came, *others) if others else self.came)
            self.sum = self.total(0, 1)[0]

    def result(self):
        if self.plan.fast:
            cuts = np.cumsum([rows for _, rows in self.names])[:-1]
            return {n: v for (n, _), v in zip(self.names, jnp.split(self.sum, cuts, 0))}
        got = {}
        for (n, _), g in zip(self.names, self.whole):
            half = lax.psum_scatter(g, "dp", scatter_dimension=0, tiled=True)
            got[n] = lax.psum_scatter(half, "fsdp", scatter_dimension=1, tiled=True).astype(F32)
        return got


def local(
    plan,
    alignment_input,
    sequence_mask,
    column_length,
    output_cotangent,
    row_projection_weight,
    row_out_weight,
    column_projection_weight,
    column_out_weight,
    feedforward_in_weight,
    feedforward_out_weight,
    layer_norm_gain,
    layer_norm_bias,
):
    width = alignment_input.shape[3]
    tokens = alignment_input.shape[1] * alignment_input.shape[2]
    heads = width // HD
    hidden = feedforward_out_weight.shape[0] * plan.dp
    x = alignment_input.reshape(tokens, width)
    cot = output_cotangent.reshape(tokens, width)
    shards = dict(
        row_qkv=row_projection_weight.T,
        row_out=row_out_weight,
        col_qkv=column_projection_weight.T,
        col_out=column_out_weight,
        ffn_in=feedforward_in_weight.T,
        ffn_out=feedforward_out_weight,
    )
    whole_rows = {k: v.shape[0] * plan.dp for k, v in shards.items()}
    norms = jnp.concatenate([layer_norm_gain, layer_norm_bias], 0)
    share = norms.shape[1]
    devices = plan.dp * plan.fsdp
    me = lax.axis_index(AXES)
    n_seq = jnp.sum((sequence_mask > 0).astype(jnp.int32))
    n_col = column_length[0].astype(jnp.int32)
    ints = jnp.stack([n_seq, n_col])
    row_scale = 0.125 * lax.rsqrt(n_seq.astype(F32))

    w = {}
    if plan.fast:
        gather_row = lax.dynamic_index_in_dim(jnp.asarray(plan.gather_table), me, 0, False)
        owner_row = lax.dynamic_index_in_dim(jnp.asarray(plan.owner_table), me, 0, False)
        tables = [gather_row, owner_row]
        extra = jnp.concatenate([norms.reshape(-1), n_col.astype(BF16)[None]])
        cols = shards["row_out"].shape[1]
        extra = jnp.pad(extra[None], ((0, 15), (0, cols - extra.shape[0])))
        groups = (("row_qkv",), ("row_out", "col_qkv"), ("col_out", "ffn_in"), ("ffn_out",))
        packs = []
        for gi, names in enumerate(groups):
            parts = [shards[n] for n in names] + ([extra] if gi == 0 else [])
            packs.append(jnp.concatenate(parts, 0) if len(parts) > 1 else parts[0])
        def ready(gi, bufs):
            row0 = 0
            for n in groups[gi]:
                rows = shards[n].shape[0]
                w[n] = Weights(bufs, row0, rows, whole_rows[n], width, True)
                row0 += rows
            return bufs

        late = []
        g1, g2, g3, g4 = (Gathering(plan, p) for p in packs)
        g1.step(plan.across)
        t = [g1.step(plan.next_to)]
        t = [g1.step(plan.one), g2.step(plan.across, *t)]
        t = [g1.far(*t), g2.step(plan.next_to, *t), g3.step(plan.across, *t)]
        g1.share(*t)
        bufs = ready(0, g1.last(*t))
        t = [g2.step(plan.one, *t), g3.step(plan.next_to, *t), g1.mate, g1.end]
        early = dict(rowf=t)
        slot = [g2.far(*t), g2.share(*t), g3.step(plan.one, *t), g4.step(plan.across, *t)]
        early["colf"] = slot

        def after_rowf(token):
            ready(1, g2.last(token, *slot))
            t = [token, *slot, g2.end]
            early["cola"] = [g3.far(*t), g3.share(*t), g4.step(plan.next_to, *t)]

        def after_colf(token):
            g4.step(plan.one, token)

        def after_cola(token):
            t = [token, *early["cola"], g4.came]
            ready(2, g3.last(*t))
            t = [token, g3.end]
            early["fout"] = [g4.far(*t), g4.share(*t)]

        hooks = dict(
            rowf=lambda outs: after_rowf(outs[5]),
            colf=lambda outs: after_colf(outs[1]),
            cola=lambda outs: after_cola(outs[0][1]),
            ffnf=lambda outs: late.append(ready(3, g4.last(outs[1], *early["fout"]))[3]),
        )
        rows = shards["row_qkv"].shape[0]
        w["norms"] = Weights(bufs, rows, 16, 16 * plan.dp, width, True)
        w["norms"].raw = True
    else:
        tables = [jnp.zeros((1,), jnp.int32)] * 2
        early, hooks, late = {}, {}, []
        for n, s in shards.items():
            half = lax.all_gather(s, "fsdp", axis=1, tiled=True)
            full = lax.all_gather(half, "dp", axis=0, tiled=True)
            w[n] = Weights([full], 0, s.shape[0], whole_rows[n], width, False)
        gb = lax.all_gather(norms, "fsdp", axis=1, tiled=True)
        gb = lax.all_gather(gb, "dp", axis=1, tiled=True).astype(F32)
        count = jnp.full((1, width), lax.psum(n_col.astype(F32), AXES))
        gb = jnp.concatenate([gb, count, jnp.zeros_like(count)], 0)
    flts = row_scale[None]

    micros = dict(
        rowf=9,
        colf=8,
        cola=4,
        ffnf=12,
        fout=7,
        ffnb=12,
        colb=10,
        colt=7,
        colg=7,
        rowb=10,
        rowt=13,
        inpb=9,
        lout=9,
    )

    def arr(n, dtype, rows=tokens, vmem=True, hbm=False):
        return Out((rows, n), dtype, vmem, hbm)

    resident = {}

    def run(name, body, smem, ins, weights, outs, grads=(), scratch=(), deps=(), fetch=()):
        ins = [a.bufs[0] if isinstance(a, Weights) else a for a in ins]
        weights = [w[n] if isinstance(n, str) else n for n in weights]
        fetch = [w[a] if isinstance(a, str) else Weights.of(a) for a in fetch]
        lists = tables + list(smem), ins, weights, outs, grads
        deps = list(deps) + early.get(name, [])
        got = fused(name, body, *lists, plan, resident, micros[name], scratch, deps, fetch)
        if name in hooks:
            hooks[name](got[0])
        return got

    wide = pltpu.VMEM((tokens, width), F32)
    turn = pltpu.VMEM((width // 128, tokens, 128), F32)
    score = pltpu.VMEM((heads * 32, 128), F32)
    flat = pltpu.VMEM((tokens // 4, 2 * width), F32)
    sums = arr(width, F32, 8, False, True)
    keep = dict(vmem=False, hbm=True)
    token = arr(128, F32, 8, **keep)

    (normed_row, packed_row, mixed_row, prob, logp, ent, gb), _ = run(
        "rowf",
        row_forward,
        [ints, flts],
        [x] if plan.fast else [x, gb],
        ["row_qkv", "norms"] if plan.fast else ["row_qkv"],
        [
            arr(width, BF16, **keep),
            arr(3 * width, BF16, **keep),
            arr(width, BF16, hbm=True),
            arr(128, F32, heads * 32, **keep),
            arr(128, F32, heads * 32, **keep),
            arr(width, F32, 8, **keep),
            arr(width, F32, 8, **keep),
        ],
        (),
        [score],
    )
    (after_row, normed_col, packed_col), _ = run(
        "colf",
        column_forward,
        [],
        [x, mixed_row[0], gb],
        ["row_out", "col_qkv"],
        [arr(width, F32, hbm=True), arr(width, BF16, **keep), arr(3 * width, BF16, hbm=True)],
        (),
        [turn],
    )
    (mixed_col,), _ = run(
        "cola",
        column_attend,
        [ints],
        [packed_col[0]],
        [],
        [arr(width, BF16, hbm=True)],
        (),
        [flat],
    )
    (after_col, normed_ffn, active, slope, cot_here), _ = run(
        "ffnf",
        feed_forward,
        [],
        [after_row[0], mixed_col[0], gb],
        ["col_out", "ffn_in"],
        [
            arr(width, F32, **keep),
            arr(width, BF16, **keep),
            arr(hidden, BF16, hbm=True),
            arr(hidden, BF16),
        ],
        fetch=[cot],
    )
    (g3,), grads = run(
        "fout",
        ffn_out_grad,
        [ints],
        [active[0], cot_here],
        [],
        [arr(width, BF16)],
        [hidden],
        [turn],
    )
    r1 = Reduction(plan, grads, ["ffn_out"], shards)
    r1.core(*late)
    (grad_hidden, w_in, w_col_out, after_here), grads = run(
        "ffnb",
        ffn_back,
        [],
        [g3, slope, normed_ffn],
        ["ffn_out"],
        [arr(hidden, BF16)],
        [hidden],
        fetch=["ffn_in", "col_out", after_col],
    )
    r2 = Reduction(plan, grads, ["ffn_in"], shards)
    landed = r1.landed()
    r1.first(grads[0], *landed)
    r2.core(*landed)
    (grad_after, g2, gm_col, sums_two, packed_here, normed_here, mixed_here), _ = run(
        "colb",
        column_back,
        [],
        [grad_hidden, after_here, g3, gb],
        [w_in, w_col_out],
        [arr(width, F32, **keep), arr(width, BF16), arr(width, BF16), sums],
        (),
        [wide],
        landed,
        [packed_col[1], normed_col, mixed_col[1]],
    )
    landed = r1.landed() + r2.landed()
    r1.second(sums_two, *landed)
    r2.first(sums_two, *landed)
    (gq_col, mark, w_col_qkv, w_row_out), _ = run(
        "colt",
        column_attend_back,
        [ints],
        [packed_here, gm_col],
        [],
        [arr(3 * width, BF16), token],
        (),
        [flat, flat],
        landed,
        ["col_qkv", "row_out"],
    )
    landed = r1.landed() + r2.landed()
    r1.third(mark, *landed)
    r2.second(mark, *landed)
    (after_row_here, grad_after_here), grads = run(
        "colg",
        product_grads,
        [],
        [gq_col, normed_here, mixed_here, g2],
        [],
        [],
        [3 * width, width],
        (),
        landed,
        [after_row[1], grad_after],
    )
    r3 = Reduction(plan, grads, ["col_qkv", "col_out"], shards)
    landed = r1.landed() + r2.landed()
    r1.fourth(grads[0], *landed)
    r2.third(grads[0], *landed)
    r3.core(*landed)
    (grad_row, g1, gm_row, sums_one, packed_here, normed_here, mixed_here), _ = run(
        "rowb",
        row_back,
        [],
        [gq_col, after_row_here, grad_after_here, gb],
        [w_col_qkv, w_row_out],
        [arr(width, F32, **keep), arr(width, BF16), arr(width, BF16), sums],
        (),
        [wide, turn],
        landed,
        [packed_row, normed_row, mixed_row[1]],
    )
    landed = r1.landed() + r2.landed() + r3.landed()
    r1.finish(sums_one)
    r2.fourth(sums_one, *landed)
    r3.first(sums_one, *landed)
    (gq_row, active_here, after_here, w_out), grads = run(
        "rowt",
        row_attend_back,
        [ints, flts],
        [packed_here, gm_row, prob, logp, mixed_here, g1, normed_here, gb],
        [],
        [arr(3 * width, BF16, **keep)],
        [width, 3 * width],
        [score],
        landed,
        [active[1], after_col, "ffn_out"],
    )
    r4 = Reduction(plan, grads, ["row_out", "row_qkv"], shards)
    landed = r2.landed() + r3.landed()
    r2.finish(grads[0])
    r3.second(grads[0], *landed)
    r4.core(*landed)
    (layer_out, mark), _ = run(
        "lout",
        ffn_result,
        [],
        [active_here, after_here],
        [w_out],
        [arr(width, BF16, **keep), token],
        (),
        [turn],
        [grads[0], *landed],
    )
    landed = r3.landed() + r4.landed()
    r3.third(mark, *landed)
    r4.first(mark, *landed)
    (grad_in, sums_zero), _ = run(
        "inpb",
        input_back,
        [],
        [gq_row, x, grad_row, gb],
        ["row_qkv"],
        [arr(width, F32, **keep), sums],
        (),
        [wide],
        [mark, *landed],
    )
    landed = r3.landed() + r4.landed()
    r3.fourth(sums_zero, *landed)
    r4.second(sums_zero, *landed)
    r3.finish()
    r4.third()
    r4.fourth()
    r4.finish()
    got = {}
    for r in (r1, r2, r3, r4):
        got.update(r.result())
    sums_all = plan.everywhere(sums_zero + sums_one + sums_two + ent, landed, r4)
    owned = lax.dynamic_slice_in_dim(sums_all[:6], me * share, share, 1)
    gains, biases = owned[0::2], owned[1::2]
    shape = alignment_input.shape
    return (
        layer_out.reshape(shape),
        grad_in.reshape(shape),
        got["row_qkv"].T,
        got["row_out"],
        got["col_qkv"].T,
        got["col_out"],
        got["ffn_in"].T,
        got["ffn_out"],
        gains,
        biases[:2],
        biases[2],
        sums_all[6, 0] / gb[6, 0],
    )


def solution(mesh):
    def whole(*args):
        plan = Plan(mesh.shape["dp"], mesh.shape["fsdp"], args[0].shape[3])
        return jax.shard_map(
            lambda *blocks: local(plan, *blocks),
            mesh=mesh,
            in_specs=(
                P(AXES, None, None, None),
                P(AXES, None),
                P(AXES),
                P(AXES, None, None, None),
                P("fsdp", "dp"),
                P("dp", "fsdp"),
                P("fsdp", "dp"),
                P("dp", "fsdp"),
                P("fsdp", "dp"),
                P("dp", "fsdp"),
                P(None, AXES),
                P(None, AXES),
            ),
            out_specs=(
                P(AXES, None, None, None),
                P(AXES, None, None, None),
                P("fsdp", "dp"),
                P("dp", "fsdp"),
                P("fsdp", "dp"),
                P("dp", "fsdp"),
                P("fsdp", "dp"),
                P("dp", "fsdp"),
                P(None, AXES),
                P(None, AXES),
                P(AXES),
                P(),
            ),
            check_vma=False,
        )(*args)

    return whole
```

```python
import jax
import jax.numpy as jnp
import numpy as np
from jax import lax
from jax.experimental import pallas as pl
from jax.experimental.pallas import tpu as pltpu
from jax.sharding import PartitionSpec as P

HD = 64
AXES = ("dp", "fsdp")
norm_eps = 1e-05
penalty_weight = 1.0
masked_score = -1000000000.0
never = -1e30

F32 = jnp.float32
BF16 = jnp.bfloat16
MIB = 1 << 20
PITCH = 33


def dot(a, b, ca, cb):
    return lax.dot_general(a, b, (((ca,), (cb,)), ((), ())), preferred_element_type=F32)


class Weights:
    def __init__(self, bufs, row0, rows, whole_rows, width, blocked, table=0):
        self.raw = self.here = False
        self.dtype = BF16
        self.bufs, self.row0, self.rows, self.table = bufs, row0, rows, table
        self.whole_rows, self.width, self.blocked = whole_rows, width, blocked


    @staticmethod
    def of(a):
        w = Weights([a], 0, a.shape[0], a.shape[0], a.shape[1], False)
        w.dtype = a.dtype
        return w

    @staticmethod
    def held(a):
        w = Weights.of(a)
        w.here = True
        return w

    def copies(self, plan):
        if self.here:
            return 0
        return sum(b.shape[0] for b in self.bufs) if self.blocked else 1


class Loaded:
    def __init__(self, ref, copies):
        self.ref, self.copies = ref, copies

    def start(self, part=None):
        for c in self.copies if part is None else self.copies[part : part + 1]:
            c.start()

    def wait(self):
        for c in self.copies:
            c.wait()
        return self.ref


class Out:
    def __init__(self, shape, dtype, vmem=True, hbm=False):
        self.shape, self.dtype, self.vmem, self.hbm = shape, dtype, vmem, hbm
        self.parts = max(1, shape[1] // 768) if hbm else 0


def fused(
    name, body, smem, ins, weights, outs, grads, plan, resident, micros, scratch=(), deps=(), fetch=()
):
    arrays, index, spaces = [], {}, []

    def slot(a):
        if id(a) not in index:
            index[id(a)] = len(arrays)
            stays = id(a) in resident
            spaces.append(pltpu.VMEM if stays else pltpu.HBM)
            arrays.append(pltpu.with_memory_space_constraint(a, spaces[-1]))
        return index[id(a)]

    in_slots = [slot(a) for a in ins]
    w_slots = [[slot(b) for b in w.bufs] for w in (*weights, *fetch)]
    weights = list(weights)
    n_weights = len(weights)
    for a in deps:
        arrays.append(a)
        spaces.append(pl.ANY)
    n_smem = len(smem)
    vm, n_sem = [], 0
    for a in ins:
        if id(a) not in resident:
            vm.append(pltpu.VMEM(a.shape, a.dtype))
            n_sem += 1
    for w in (*weights, *fetch):
        n_sem += w.copies(plan)
    for w in weights:
        if w.here:
            continue
        raw = (w.whole_rows // w.rows * plan.fsdp, w.rows, w.width // plan.fsdp)
        vm.append(pltpu.VMEM(raw if w.raw else (w.whole_rows, w.width), BF16))
    out_shapes, out_spaces = [], []
    for o in outs:
        if o.vmem:
            out_shapes.append(pltpu.VMEM(o.shape, o.dtype))
            out_spaces.append(pltpu.VMEM)
        else:
            vm.append(pltpu.VMEM(o.shape, o.dtype))
        if o.hbm:
            out_shapes.append(pltpu.HBM(o.shape, o.dtype))
            out_spaces.append(pltpu.HBM)
            n_sem += o.parts
    f_at = len(out_shapes)
    for w in fetch:
        out_shapes.append(pltpu.VMEM((w.whole_rows, w.width), w.dtype))
        out_spaces.append(pltpu.VMEM)
    g_at = len(out_shapes)
    width = plan.width
    for rows in grads:
        vm.append(pltpu.VMEM((rows, width), BF16))
        n_sem += plan.dp * plan.fsdp if plan.fast else 1
    if grads and plan.fast:
        per = sum(rows // plan.dp for rows in grads)
        shape = pltpu.HBM((plan.slots, per, width // plan.fsdp), BF16)
        out_shapes += [shape, shape]
    elif grads:
        out_shapes += [pltpu.HBM((rows, width), BF16) for rows in grads]
    out_spaces += [pltpu.HBM] * (len(out_shapes) - g_at)
    n_in, n_out, n_vm = len(arrays), len(out_shapes), len(vm)
    used_vmem = sum(int(np.prod(m.shape)) * np.dtype(m.dtype).itemsize for m in (*vm, *scratch))

    def kernel(*refs):
        sm = refs[:n_smem]
        hb = refs[n_smem : n_smem + n_in]
        ob = refs[n_smem + n_in : n_smem + n_in + n_out]
        rest = refs[n_smem + n_in + n_out :]
        vrefs, extra, sems = list(rest[:n_vm]), rest[n_vm:-1], rest[-1]
        used = [0]

        def sem():
            used[0] += 1
            return sems.at[used[0] - 1]

        loads = Loads()
        for a, s in zip(ins, in_slots):
            if id(a) in resident:
                loads.append(Loaded(hb[s], []))
            else:
                ref = vrefs.pop(0)
                loads.append(Loaded(ref, [pltpu.make_async_copy(hb[s], ref, sem())]))
        wl = []
        for n, (w, slots) in enumerate(zip((*weights, *fetch), w_slots)):
            copies = []
            if w.here:
                dst = hb[slots[0]]
            elif n < n_weights:
                dst = vrefs.pop(0)
            else:
                dst = ob[f_at + n - n_weights]
            if w.here:
                pass
            elif w.blocked:
                cols = w.width // plan.fsdp
                count = 0
                for s in slots:
                    for j in range(arrays[s].shape[0]):
                        block = sm[w.table][count] if w.table is not None else count
                        count += 1
                        row = (block // plan.fsdp) * w.rows
                        col = (block % plan.fsdp) * cols
                        if w.table is not None:
                            row, col = pl.multiple_of(row, 16), pl.multiple_of(col, 128)
                        spot = dst.at[pl.ds(row, w.rows), pl.ds(col, cols)]
                        if w.raw:
                            spot = dst.at[count - 1]
                        src = hb[s].at[j, pl.ds(w.row0, w.rows), :]
                        copies.append(pltpu.make_async_copy(src, spot, sem()))
            else:
                copies.append(pltpu.make_async_copy(hb[slots[0]], dst, sem()))
            (wl if n < n_weights else loads.fetched).append(Loaded(dst, copies))
        ol = []
        at = 0
        for o in outs:
            if o.vmem:
                ref = ob[at]
                at += 1
            else:
                ref = vrefs.pop(0)
            copies = []
            if o.hbm:
                for k in range(o.parts):
                    lanes = slice(None)
                    if o.parts > 1:
                        lanes = pl.ds(k * 768, 768)
                    copies.append(
                        pltpu.make_async_copy(ref.at[:, lanes], ob[at].at[:, lanes], sem())
                    )
                at += 1
            ol.append(Loaded(ref, copies))
        gl = []
        row0 = 0
        for k, rows in enumerate(grads):
            src = vrefs.pop(0)
            if plan.fast:
                gl.append(Blocks(src, ob[g_at], ob[g_at + 1], sm[1], plan, rows, row0, sem))
                row0 += rows // plan.dp
            else:
                gl.append(Loaded(src, [pltpu.make_async_copy(src, ob[g_at + k], sem())]))
        for l in (*loads[:1], *wl[:1], *loads[1:], *wl[1:]):
            l.start()
        body(sm[:1] + sm[2:] if name == "rowf" else sm[2:], loads, wl, ol, gl, extra)
        for l in (*ol, *gl, *loads.fetched):
            l.wait()

    res = pl.pallas_call(
        kernel,
        name=name,
        out_shape=out_shapes,
        in_specs=[pl.BlockSpec(memory_space=pltpu.SMEM)] * n_smem
        + [pl.BlockSpec(memory_space=m) for m in spaces],
        out_specs=[pl.BlockSpec(memory_space=m) for m in out_spaces],
        scratch_shapes=vm + list(scratch) + [pltpu.SemaphoreType.DMA((n_sem,))],
        compiler_params=pltpu.CompilerParams(vmem_limit_bytes=used_vmem + 7 * MIB),
        cost_estimate=pl.CostEstimate(
            flops=int(micros * 1e6), bytes_accessed=int(micros * 3e3), transcendentals=0
        ),
    )(*smem, *arrays)
    got, at = [], 0
    for o in outs:
        both = res[at : at + o.vmem + o.hbm]
        at += o.vmem + o.hbm
        if o.vmem:
            resident[id(both[0])] = both[0]
        got.append(both[0] if len(both) == 1 else both)
    for a in res[f_at:g_at]:
        resident[id(a)] = a
        got.append(Weights.held(a))
    return got, res[g_at:]


class Loads(list):
    def __init__(self):
        self.fetched = []

    def later(self):
        for l in self.fetched:
            l.start()


class Blocks:
    def __init__(self, ref, kept, sent, table, plan, rows, row0, sem):
        self.ref, self.plan = ref, plan
        self.per, self.cols = rows // plan.dp, plan.width // plan.fsdp
        self.kept, self.sent, self.table, self.row0 = kept, sent, table, row0
        self.sems = [sem() for _ in range(plan.dp * plan.fsdp)]
        self.begun = 0

    def copy(self, n, out, slot):
        row, col = (n // self.plan.fsdp) * self.per, (n % self.plan.fsdp) * self.cols
        return pltpu.make_async_copy(
            self.ref.at[row : row + self.per, col : col + self.cols],
            out.at[slot, pl.ds(self.row0, self.per), :],
            self.sems[n],
        )

    def start(self, rows=None):
        rows = self.ref.shape[0] if rows is None else rows
        end = rows // self.per * self.plan.fsdp
        slots = self.plan.slots
        for n in range(self.begun, end):
            place = self.table[n]

            @pl.when(place < slots)
            def _():
                self.copy(n, self.kept, place).start()

            @pl.when(place >= slots)
            def _():
                self.copy(n, self.sent, place - slots).start()

        self.begun = end

    def wait(self):
        for n in range(self.begun):
            self.copy(n, self.kept, 0).wait()


def stamp(out):
    out.ref[...] = jnp.zeros(out.ref.shape, out.ref.dtype)
    out.start()


def normal_form(v):
    centred = v - jnp.mean(v, -1, keepdims=True)
    rstd = lax.rsqrt(jnp.mean(centred * centred, -1, keepdims=True) + norm_eps)
    return centred * rstd, rstd


def norm_rows(src, dst, gb, k, total):
    for t in range(0, total, 256):
        xhat, _ = normal_form(src[t : t + 256, :].astype(F32))
        dst[t : t + 256, :] = (xhat * gb[k : k + 1, :] + gb[k + 3 : k + 4, :]).astype(BF16)


def norm_back(dn_ref, src, base, gb, k, total, emit, sums):
    gain = gb[k : k + 1, :]
    gain_sum = jnp.zeros_like(gain)
    bias_sum = jnp.zeros_like(gain)
    for t in range(0, total, 256):
        xhat, rstd = normal_form(src[t : t + 256, :].astype(F32))
        dn = dn_ref[t : t + 256, :]
        gain_sum = gain_sum + jnp.sum(dn * xhat, 0, keepdims=True)
        bias_sum = bias_sum + jnp.sum(dn, 0, keepdims=True)
        dx = dn * gain
        low = jnp.mean(dx, -1, keepdims=True)
        mix = jnp.mean(dx * xhat, -1, keepdims=True)
        emit(t, base[t : t + 256, :].astype(F32) + rstd * (dx - low - xhat * mix))
    none = jnp.zeros((1, gain.shape[1]), F32)
    rows = [none] * (2 * k) + [gain_sum, bias_sum] + [none] * (6 - 2 * k)
    sums[...] = jnp.concatenate(rows, 0)


def head_masks(lanes):
    lane = lax.broadcasted_iota(jnp.int32, (1, lanes), 1)
    low = ((lane // HD) % 2 == 0).astype(F32)
    return low.astype(BF16), (1.0 - low).astype(BF16)


def four(ref, col):
    return jnp.concatenate([ref[g * 256 : (g + 1) * 256, col : col + 128] for g in range(4)], 1)


def pick(big):
    seg = lax.broadcasted_iota(jnp.int32, (32, 256), 1) // 32
    out = big[:32, :]
    for k in range(1, 8):
        out = jnp.where(seg == k, big[k * 32 : (k + 1) * 32, :], out)
    out = out[:, :128] + out[:, 128:]
    out = out + pltpu.roll(out, 64, 1)
    return out + pltpu.roll(out, 32, 1)


def spread(small):
    seg = lax.broadcasted_iota(jnp.int32, (32, 256), 1) // 32
    wide = jnp.concatenate([small, small], 1)
    return jnp.concatenate([jnp.where(seg == k, wide, 0.0).astype(BF16) for k in range(8)], 0)


def gathered_norms(blocks, table):
    slots = blocks.shape[0]
    values = jnp.sum(blocks[...].astype(F32), 1).astype(BF16)
    place = lax.broadcasted_iota(jnp.int32, (slots, 1), 0)
    owner = jnp.zeros((slots, 1), jnp.int32)
    for j in range(slots):
        owner = jnp.where(place == j, table[j], owner)
    share = 768 // slots
    lane = lax.broadcasted_iota(jnp.int32, (1, 768), 1)
    row = lax.broadcasted_iota(jnp.int32, (values.shape[1], 1), 0)
    mine = lane // share == owner
    rows = []
    for k in range(6):
        spot = (row == k * share + lane % share).astype(F32).astype(BF16)
        rows.append(jnp.sum(jnp.where(mine, dot(values, spot, 1, 0), 0.0), 0, keepdims=True))
    count = jnp.where(lax.broadcasted_iota(jnp.int32, (1, values.shape[1]), 1) == 6 * share, 1.0, 0.0)
    total = jnp.sum(values.astype(F32) * count)
    rows.append(jnp.full((1, 768), total, F32))
    rows.append(jnp.zeros((1, 768), F32))
    return jnp.concatenate(rows, 0)


def row_forward(sm, I, W, O, G, X):
    ints, flts = sm[-2:]
    x = I[0]
    normed, packed, mixed, prob, logp, ent, norms = O
    sc = X[0]
    if len(W) > 1:
        norms.ref[...] = gathered_norms(W[0].wait(), sm[0])
    else:
        norms.ref[...] = I[1].wait()[...]
    norms.start()
    xr, g = x.wait(), norms.ref
    norm_rows(xr, normed.ref, g, 0, 1024)
    normed.start()
    wt = W[-1].wait()
    nr = normed.ref[...]
    n_seq, n_col = ints[0], ints[1]
    keep = (lax.broadcasted_iota(jnp.int32, (1024, 1), 0) // 32 < n_seq).astype(F32)
    width = nr.shape[1]
    heads = width // HD
    pr = packed.ref
    for n in range(0, 3 * width, 256):
        out = dot(nr, wt[n : n + 256, :], 1, 1)
        if n < width:
            out = out * keep
        pr[:, n : n + 256] = out.astype(BF16)
        if (n + 256) % 768 == 0:
            packed.start(n // 768)
    halves = head_masks(512)
    for m in range(heads // 2):
        q, k = four(pr, m * 128), four(pr, width + m * 128)
        for e in range(2):
            h = 2 * m + e
            sc[h * 32 : (h + 1) * 32, :] = pick(dot(q * halves[e], k, 1, 1))
    lane = lax.broadcasted_iota(jnp.int32, (1, 128), 1) % 32
    s = jnp.where(lane < n_col, sc[...] * flts[0], masked_score)
    top = jnp.max(s, -1, keepdims=True)
    total = jnp.sum(jnp.exp(s - top), -1, keepdims=True) * 0.25
    lp = s - (top + jnp.log(total))
    p = jnp.exp(lp)
    prob.ref[...] = p
    logp.ref[...] = lp
    prob.start()
    logp.start()
    entropy = jnp.sum(p * lp, -1, keepdims=True) * -0.25
    row = lax.broadcasted_iota(jnp.int32, entropy.shape, 0) % 32
    total = jnp.sum(jnp.where(row < n_col, entropy, 0.0))
    share = total / norms.ref[6:7, :]
    ent.ref[...] = jnp.where(lax.broadcasted_iota(jnp.int32, ent.ref.shape, 0) == 6, share, 0.0)
    ent.start()
    second = (lax.broadcasted_iota(jnp.int32, (1, 512), 1) // HD) % 2 == 1
    for m in range(heads // 2):
        v = four(pr, 2 * width + m * 128)
        both = [
            dot(spread(prob.ref[h * 32 : (h + 1) * 32, :]), v, 1, 0) for h in (2 * m, 2 * m + 1)
        ]
        out = jnp.where(second, both[1], both[0]).astype(BF16)
        for t in range(4):
            mixed.ref[t * 256 : (t + 1) * 256, m * 128 : (m + 1) * 128] = out[
                :, t * 128 : (t + 1) * 128
            ]
    mixed.start()


def stacked(x, halves):
    return jnp.concatenate([x * halves[0], x * halves[1]], 0)


def segment(rows):
    return (lax.broadcasted_iota(jnp.int32, (rows, 256), 1) // 32) % 4


def pick_four(big):
    seg = segment(32)
    out = big[:32, :]
    for k in range(1, 4):
        out = jnp.where(seg == k, big[k * 32 : (k + 1) * 32, :], out)
    return out


def spread_four(small):
    seg = segment(32)
    return jnp.concatenate([jnp.where(seg == k, small, 0.0).astype(BF16) for k in range(4)], 0)


def unstack(both):
    lane = lax.broadcasted_iota(jnp.int32, (128, 128), 1)
    return jnp.where(lane < HD, both[:128], both[128:])


def to_columns(src, take):
    for t in range(0, 1024, 256):
        lanes = [
            jnp.concatenate([src[j, pl.ds(t // 32 + k, 32, stride=PITCH), :] for k in range(8)], 0)
            for j in range(src.shape[0])
        ]
        take(t, jnp.concatenate(lanes, 1))


def put(dst, start, n, value):
    for r in range(value.shape[0] // 32):
        at = (start // 32 + r) * PITCH
        for j in range(value.shape[1] // 128):
            piece = value[r * 32 : (r + 1) * 32, j * 128 : (j + 1) * 128]
            dst[n // 128 + j, at : at + 32, :] = piece


def column_forward(sm, I, W, O, G, X):
    x, mixed_row, gb = I
    after, normed, packed = O
    (ar,) = X
    width = normed.ref.shape[1]
    mr, xr = mixed_row.wait(), x.wait()
    wo = W[0].wait()
    for n in range(0, width, 256):
        out = xr[:, n : n + 256].astype(F32) + dot(mr[...], wo[:, n : n + 256], 1, 0)
        put(ar, 0, n, out)
    g = gb.wait()

    def take(t, rows):
        after.ref[t : t + 256, :] = rows

    to_columns(ar, take)
    after.start()
    norm_rows(after.ref, normed.ref, g, 1, 1024)
    normed.start()
    wt = W[1].wait()
    nr = normed.ref[...]
    pr = packed.ref
    for n in range(0, 3 * width, 256):
        pr[:, n : n + 256] = dot(nr, wt[n : n + 256, :], 1, 1).astype(BF16)
        if (n + 256) % 768 == 0:
            packed.start(n // 768)


def column_softmax(sc, n_seq):
    def block(b, carry):
        at = pl.ds(pl.multiple_of(b * 32, 32), 32)
        s = sc[at, :]
        s = jnp.where(lax.broadcasted_iota(jnp.int32, s.shape, 0) < n_seq, s, never)
        p = jnp.exp(s - jnp.max(s, 0, keepdims=True))
        sc[at, :] = p * (1.0 / jnp.sum(p, 0, keepdims=True))
        return carry

    lax.fori_loop(0, sc.shape[0] // 32, block, 0)


def column_attend(sm, I, W, O, G, X):
    (ints,) = sm
    (mixed,) = O
    (sc,) = X
    width = mixed.ref.shape[1]
    pr = I[0].wait()
    halves = head_masks(128)

    def scores(b, carry):
        rows = pl.ds(pl.multiple_of(b * 128, 128), 128)
        at = pl.ds(pl.multiple_of(b * 32, 32), 32)
        for lo in range(0, width, 128):
            qs = stacked(pr[rows, lo : lo + 128] * 0.125, halves)
            k = pr[rows, width + lo : width + lo + 128]
            sc[at, 2 * lo : 2 * lo + 256] = pick_four(dot(k, qs, 1, 1))
        return carry

    lax.fori_loop(0, 8, scores, 0)
    column_softmax(sc, ints[0])

    def mix(b, carry):
        rows = pl.ds(pl.multiple_of(b * 128, 128), 128)
        at = pl.ds(pl.multiple_of(b * 32, 32), 32)
        for lo in range(0, width, 128):
            v = pr[rows, 2 * width + lo : 2 * width + lo + 128]
            p = spread_four(sc[at, 2 * lo : 2 * lo + 256])
            mixed.ref[rows, lo : lo + 128] = unstack(dot(p, v, 0, 0)).astype(BF16)
        return carry

    lax.fori_loop(0, 8, mix, 0)
    mixed.start()


def feed_forward(sm, I, W, O, G, X):
    after_row, mixed, gb = I
    after, normed, active, slope = O
    width = normed.ref.shape[1]
    hidden = active.ref.shape[1]
    ar, mr = after_row.wait(), mixed.wait()
    wo = W[0].wait()
    for n in range(0, width, 256):
        after.ref[:, n : n + 256] = ar[:, n : n + 256] + dot(mr[...], wo[:, n : n + 256], 1, 0)
    after.start()
    norm_rows(after.ref, normed.ref, gb.wait(), 2, 1024)
    normed.start()
    wt = W[1].wait()
    I.later()
    nr = normed.ref[...]
    for n in range(0, hidden, 256):
        h = dot(nr, wt[n : n + 256, :], 1, 1)
        cdf = 0.5 + 0.5 * lax.erf(h * (0.5**0.5))
        active.ref[:, n : n + 256] = (h * cdf).astype(BF16)
        bell = jnp.exp(h * h * -0.5) * (0.5 / np.pi) ** 0.5
        slope.ref[:, n : n + 256] = (cdf + h * bell).astype(BF16)
        if (n + 256) % 768 == 0:
            active.start(n // 768)
    slope.start()


def weight_grad(dst, left, right, step=768):
    rows = dst.ref.shape[0]
    blocks = isinstance(dst, Blocks)
    for n in range(0, rows, step):
        dst.ref[n : n + step, :] = dot(left[:, n : n + step], right[...], 0, 0).astype(BF16)
        if blocks:
            dst.start(n + step)
    if not blocks:
        dst.start()


def ffn_out_grad(sm, I, W, O, G, X):
    (ints,) = sm
    active, cot = I
    (g3,) = O
    (wide,) = X
    put(wide, 0, 0, cot.wait()[...].astype(F32))
    n_seq, n_col = ints[0], ints[1]

    def take(t, rows):
        at = lax.broadcasted_iota(jnp.int32, (256, 1), 0) + t
        keep = ((at % 32 < n_seq) & (at // 32 < n_col)).astype(F32)
        g3.ref[t : t + 256, :] = (rows * keep).astype(BF16)

    to_columns(wide, take)
    g3.start()
    weight_grad(G[0], active.wait(), g3.ref)


def ffn_back(sm, I, W, O, G, X):
    g3, slope, normed = I
    (grad_hidden,) = O
    wf = W[0].wait()
    gr, sl = g3.wait(), slope.wait()
    I.later()
    gh = grad_hidden.ref
    hidden = gh.shape[1]
    gv = gr[...]
    for n in range(0, hidden, 256):
        d = dot(gv, wf[n : n + 256, :], 1, 1)
        gh[:, n : n + 256] = (d * sl[:, n : n + 256].astype(F32)).astype(BF16)
    grad_hidden.start()
    weight_grad(G[0], gh, normed.wait())


def ffn_result(sm, I, W, O, G, X):
    active, after = I
    layer_out = O[0]
    (res,) = X
    width = layer_out.ref.shape[1]
    wf = W[0].wait()
    ac, ar = active.wait(), after.wait()
    I.later()
    for n in range(0, width, 256):
        put(res, 0, n, ar[:, n : n + 256] + dot(ac[...], wf[:, n : n + 256], 1, 0))

    def take(t, rows):
        layer_out.ref[t : t + 256, :] = rows.astype(BF16)

    to_columns(res, take)
    layer_out.start()
    stamp(O[1])


def column_back(sm, I, W, O, G, X):
    grad_hidden, after_col, g3, gb = I
    grad_after, branch, grad_mixed, sums = O
    (dn,) = X
    g2, gm = branch.ref, grad_mixed.ref
    width = g2.shape[1]
    gh = grad_hidden.wait()
    wf = W[0].wait()
    I.later()
    for n in range(0, width, 256):
        dn[:, n : n + 256] = dot(gh[...], wf[:, n : n + 256], 1, 0)
    ac, base, g = after_col.wait(), g3.wait(), gb.wait()

    def emit(t, rows):
        grad_after.ref[t : t + 256, :] = rows
        g2[t : t + 256, :] = rows.astype(BF16)

    norm_back(dn, ac, base, g, 2, 1024, emit, sums.ref)
    grad_after.start()
    sums.start()
    wo = W[1].wait()
    for n in range(0, width, 256):
        gm[:, n : n + 256] = dot(g2[...], wo[n : n + 256, :], 1, 1).astype(BF16)
    grad_mixed.start()


def column_attend_back(sm, I, W, O, G, X):
    (ints,) = sm
    packed, grad_mixed = I
    gq = O[0]
    sc, dsc = X
    pr, gm = packed.wait(), grad_mixed.wait()
    I.later()
    width = gm.shape[1]
    halves = head_masks(128)
    out = gq.ref

    def scores(b, carry):
        rows = pl.ds(pl.multiple_of(b * 128, 128), 128)
        at = pl.ds(pl.multiple_of(b * 32, 32), 32)
        for lo in range(0, width, 128):
            qs = stacked(pr[rows, lo : lo + 128] * 0.125, halves)
            k = pr[rows, width + lo : width + lo + 128]
            v = pr[rows, 2 * width + lo : 2 * width + lo + 128]
            des = stacked(gm[rows, lo : lo + 128], halves)
            sc[at, 2 * lo : 2 * lo + 256] = pick_four(dot(k, qs, 1, 1))
            dsc[at, 2 * lo : 2 * lo + 256] = pick_four(dot(v, des, 1, 1))
        return carry

    lax.fori_loop(0, 8, scores, 0)
    column_softmax(sc, ints[0])

    def pull(b, carry):
        at = pl.ds(pl.multiple_of(b * 32, 32), 32)
        p, dp = sc[at, :], dsc[at, :]
        dsc[at, :] = p * (dp - jnp.sum(p * dp, 0, keepdims=True))
        return carry

    lax.fori_loop(0, 8, pull, 0)

    def spreads(b, carry):
        rows = pl.ds(pl.multiple_of(b * 128, 128), 128)
        at = pl.ds(pl.multiple_of(b * 32, 32), 32)
        for lo in range(0, width, 128):
            qs = stacked(pr[rows, lo : lo + 128] * 0.125, halves)
            k = pr[rows, width + lo : width + lo + 128]
            des = stacked(gm[rows, lo : lo + 128], halves)
            ds = spread_four(dsc[at, 2 * lo : 2 * lo + 256])
            dq = unstack(dot(ds, k, 0, 0)) * 0.125
            out[rows, lo : lo + 128] = dq.astype(BF16)
            out[rows, width + lo : width + lo + 128] = dot(ds, qs, 1, 0).astype(BF16)
            dv = dot(spread_four(sc[at, 2 * lo : 2 * lo + 256]), des, 1, 0)
            out[rows, 2 * width + lo : 2 * width + lo + 128] = dv.astype(BF16)
        return carry

    lax.fori_loop(0, 8, spreads, 0)
    gq.start()
    stamp(O[1])


def product_grads(sm, I, W, O, G, X):
    I.later()
    for k, g in enumerate(G):
        weight_grad(g, I[2 * k].wait(), I[2 * k + 1].wait())


def row_back(sm, I, W, O, G, X):
    gq_col, after_row, grad_after, gb = I
    grad_row, branch, grad_mixed, sums = O
    dn, wide = X
    g1, gm = branch.ref, grad_mixed.ref
    width = g1.shape[1]
    wc = W[0].wait()
    gc = gq_col.wait()
    I.later()
    for n in range(0, width, 256):
        dn[:, n : n + 256] = dot(gc[...], wc[:, n : n + 256], 1, 0)
    ar, base, g = after_row.wait(), grad_after.wait(), gb.wait()

    def emit(t, rows):
        put(wide, t, 0, rows)

    norm_back(dn, ar, base, g, 1, 1024, emit, sums.ref)
    sums.start()

    def take(t, rows):
        grad_row.ref[t : t + 256, :] = rows
        g1[t : t + 256, :] = rows.astype(BF16)

    to_columns(wide, take)
    grad_row.start()
    wo = W[1].wait()
    for n in range(0, width, 256):
        gm[:, n : n + 256] = dot(g1[...], wo[n : n + 256, :], 1, 1).astype(BF16)
    grad_mixed.start()


def row_attend_back(sm, I, W, O, G, X):
    ints, flts = sm
    packed, grad_mixed, prob, logp, mixed, g1, normed, gb = I
    (gq,) = O
    (sc,) = X
    n_seq, n_col = ints[0], ints[1]
    pr, gm = packed.wait(), grad_mixed.wait()
    I.later()
    width = gm.shape[1]
    heads = width // HD
    halves = head_masks(512)
    for m in range(heads // 2):
        d, v = four(gm, m * 128), four(pr, 2 * width + m * 128)
        for e in range(2):
            h = 2 * m + e
            sc[h * 32 : (h + 1) * 32, :] = pick(dot(d * halves[e], v, 1, 1))
    p, lp = prob.wait()[...], logp.wait()[...]
    dp = sc[...]
    ent = jnp.sum(p * lp, -1, keepdims=True) * -0.25
    row = lax.broadcasted_iota(jnp.int32, ent.shape, 0) % 32
    w = jnp.where(row < n_col, penalty_weight / gb.wait()[6:7, 0:1], 0.0)
    ds = p * (dp - jnp.sum(p * dp, -1, keepdims=True) * 0.25) - w * p * (lp + ent)
    sc[...] = ds
    keep = (lax.broadcasted_iota(jnp.int32, (1024, 1), 0) // 32 < n_seq).astype(F32)
    scale = flts[0]
    out = gq.ref
    for m in range(heads // 2):
        lo = m * 128
        q, k, d = four(pr, lo), four(pr, width + lo), four(gm, lo)
        dq = dk = dv = 0.0
        for e in range(2):
            h = 2 * m + e
            pb = spread(prob.ref[h * 32 : (h + 1) * 32, :])
            sb = spread(sc[h * 32 : (h + 1) * 32, :])
            dq = dq + dot(sb, k * halves[e], 1, 0)
            dk = dk + dot(sb, q * halves[e], 0, 0)
            dv = dv + dot(pb, d * halves[e], 0, 0)
        for t in range(4):
            rows, lanes = slice(t * 256, (t + 1) * 256), slice(t * 128, (t + 1) * 128)
            out[rows, lo : lo + 128] = (
                dq[:, lanes] * (scale * keep[t * 256 : (t + 1) * 256])
            ).astype(BF16)
            out[rows, width + lo : width + lo + 128] = (dk[:, lanes] * scale).astype(BF16)
            out[rows, 2 * width + lo : 2 * width + lo + 128] = dv[:, lanes].astype(BF16)
    gq.start()
    weight_grad(G[0], mixed.wait(), g1.wait())
    weight_grad(G[1], out, normed.wait())


def input_back(sm, I, W, O, G, X):
    gq, x, grad_row, gb = I
    grad_in, sums = O
    (dn,) = X
    width = dn.shape[1]
    gr = gq.wait()
    wt = W[0].wait()
    I.later()
    for n in range(0, width, 256):
        dn[:, n : n + 256] = dot(gr[...], wt[:, n : n + 256], 1, 0)

    def emit(t, rows):
        grad_in.ref[t : t + 256, :] = rows

    norm_back(dn, x.wait(), grad_row.wait(), gb.wait(), 0, 1024, emit, sums.ref)
    grad_in.start()
    sums.start()


class Plan:
    def __init__(self, dp, fsdp, width):
        self.dp, self.fsdp, self.width = dp, fsdp, width
        self.fast = fsdp == 2 and dp == 16
        self.slots = dp * fsdp // 2
        if not self.fast:
            return
        place = [(z, x, c, y) for z in range(4) for x in range(2) for c in range(2) for y in range(2)]
        index = {p: n for n, p in enumerate(place)}

        def one(p):
            z, x, c, y = p
            return (z, 1 - x, c, y) if c == 0 else (z, x, c, 1 - y)

        def two(p):
            z, x, c, y = p
            return (z, 1 - x, c, y) if c == 1 else (z, x, c, 1 - y)

        def next_to(p):
            return (p[0] ^ 1, *p[1:])

        def across(p):
            return (p[0] ^ 2, *p[1:])

        def mate(p):
            return (p[0], p[1], 1 - p[2], p[3])

        def pairs(f):
            return [(n, index[f(p)]) for n, p in enumerate(place)]

        self.one, self.two, self.core = pairs(one), pairs(two), pairs(mate)
        self.next_to, self.across = pairs(next_to), pairs(across)
        gathered, owners = [], []
        for p in place:
            held = [p]
            for f in (across, next_to, one, two):
                held = held + [f(q) for q in held]
            gathered.append([index[q] for q in held])
            owners.append([])
            for order in ((across, next_to, two, one), (two, across, next_to, one)):
                owned = [p]
                for f in order:
                    owned = owned + [f(q) for q in owned]
                owners[-1].append([index[q] for q in owned])
        mates = [index[mate(p)] for p in place]
        self.gather_table = np.array([gathered[n] + gathered[m] for n, m in enumerate(mates)], np.int32)
        self.owner_tables = []
        for k in range(2):
            owned = np.array([owners[n][k] + owners[m][k] for n, m in enumerate(mates)], np.int32)
            self.owner_tables.append(np.argsort(owned, 1).astype(np.int32))

    def go(self, v, perm):
        return lax.ppermute(v, AXES, perm)

    def everywhere(self, v, beside):
        if not self.fast:
            return lax.psum(v, AXES)
        for perm in (self.core, self.one):
            v = v + lax.ppermute(v, AXES, perm)
        v = after(v, *beside.second_came)
        for perm in (self.two, self.next_to):
            v = v + lax.ppermute(v, AXES, perm)
        v = after(v, *beside.third_came)
        return v + lax.ppermute(v, AXES, self.across)


def after(v, *others):
    return lax.optimization_barrier((v, *others))[0]


class Gathering:
    def __init__(self, plan, shard):
        self.plan, self.have = plan, [shard[None]]

    def all(self, others):
        if others:
            self.have = list(lax.optimization_barrier((*self.have, *others)))[: len(self.have)]
        self.have = [jnp.concatenate(self.have, 0)] if len(self.have) > 1 else self.have
        return self.have[0]

    def step(self, perm, *others):
        self.came = self.plan.go(self.all(others), perm)
        self.have.append(self.came)
        return self.came

    def far(self, *others):
        self.mine = self.all(others)
        self.came = self.plan.go(self.mine, self.plan.two)
        return self.came

    def share(self, *others):
        mine = after(self.mine, *others) if others else self.mine
        self.mate = self.plan.go(mine, self.plan.core)
        return self.mate

    def last(self, *others):
        far = after(self.came, *others) if others else self.came
        self.end = self.plan.go(far, self.plan.core)
        return [self.mine, self.came, self.mate, self.end]


class Reduction:
    def __init__(self, plan, grads, names, shards):
        self.plan = plan
        self.names = [(n, shards[n].shape[0]) for n in names]
        if plan.fast:
            kept, self.sent = grads
            self.terms, self.size = [kept], kept.shape[0]
        else:
            self.whole = grads

    def go(self, v, perm):
        return lax.ppermute(v.astype(BF16), AXES, perm)

    def landed(self):
        return [self.came] if self.plan.fast else []

    def core(self, *others):
        if self.plan.fast:
            sent = after(self.sent, *others) if others else self.sent
            self.came = self.go(sent, self.plan.core)

    def total(self, start, stop):
        return sum(t[start:stop].astype(F32) for t in self.terms)

    def step(self, perm, *others):
        if self.plan.fast:
            came = after(self.came, *others) if others else self.came
            self.terms.append(came)
            self.size //= 2
            self.came = self.go(self.total(self.size, 2 * self.size), perm)

    def first(self, *others):
        self.step(self.plan.fast and self.plan.one, *others)

    def second(self, *others):
        self.step(self.plan.fast and self.plan.two, *others)

    def third(self, *others):
        self.second_came = self.landed()
        self.step(self.plan.fast and self.plan.next_to, *others)

    def fourth(self, *others):
        self.third_came = self.landed()
        self.step(self.plan.fast and self.plan.across, *others)

    def finish(self, *others):
        if self.plan.fast:
            self.terms.append(after(self.came, *others) if others else self.came)
            self.sum = self.total(0, 1)[0]

    def result(self):
        if self.plan.fast:
            cuts = np.cumsum([rows for _, rows in self.names])[:-1]
            return {n: v for (n, _), v in zip(self.names, jnp.split(self.sum, cuts, 0))}
        got = {}
        for (n, _), g in zip(self.names, self.whole):
            half = lax.psum_scatter(g, "dp", scatter_dimension=0, tiled=True)
            got[n] = lax.psum_scatter(half, "fsdp", scatter_dimension=1, tiled=True).astype(F32)
        return got


def local(
    plan,
    alignment_input,
    sequence_mask,
    column_length,
    output_cotangent,
    row_projection_weight,
    row_out_weight,
    column_projection_weight,
    column_out_weight,
    feedforward_in_weight,
    feedforward_out_weight,
    layer_norm_gain,
    layer_norm_bias,
):
    width = alignment_input.shape[3]
    tokens = alignment_input.shape[1] * alignment_input.shape[2]
    heads = width // HD
    hidden = feedforward_out_weight.shape[0] * plan.dp
    x = alignment_input.reshape(tokens, width)
    cot = output_cotangent.reshape(tokens, width)
    shards = dict(
        row_qkv=row_projection_weight.T,
        row_out=row_out_weight,
        col_qkv=column_projection_weight.T,
        col_out=column_out_weight,
        ffn_in=feedforward_in_weight.T,
        ffn_out=feedforward_out_weight,
    )
    whole_rows = {k: v.shape[0] * plan.dp for k, v in shards.items()}
    norms = jnp.concatenate([layer_norm_gain, layer_norm_bias], 0)
    share = norms.shape[1]
    devices = plan.dp * plan.fsdp
    me = lax.axis_index(AXES)
    n_seq = jnp.sum((sequence_mask > 0).astype(jnp.int32))
    n_col = column_length[0].astype(jnp.int32)
    ints = jnp.stack([n_seq, n_col])
    row_scale = 0.125 * lax.rsqrt(n_seq.astype(F32))

    w = {}
    if plan.fast:
        gather_row = lax.dynamic_index_in_dim(jnp.asarray(plan.gather_table), me, 0, False)
        owner_row, first_row = (
            lax.dynamic_index_in_dim(jnp.asarray(t), me, 0, False) for t in plan.owner_tables
        )
        tables = [gather_row, owner_row]
        own_tables = {n: [gather_row, first_row] for n in ("colg",)}
        extra = jnp.concatenate([norms.reshape(-1), n_col.astype(BF16)[None]])
        cols = shards["row_out"].shape[1]
        extra = jnp.pad(extra[None], ((0, 15), (0, cols - extra.shape[0])))
        groups = (("row_qkv",), ("row_out", "col_qkv"), ("col_out", "ffn_in"), ("ffn_out",))
        packs = []
        for gi, names in enumerate(groups):
            parts = [shards[n] for n in names] + ([extra] if gi == 0 else [])
            packs.append(jnp.concatenate(parts, 0) if len(parts) > 1 else parts[0])
        def ready(gi, bufs):
            row0 = 0
            for n in groups[gi]:
                rows = shards[n].shape[0]
                w[n] = Weights(bufs, row0, rows, whole_rows[n], width, True)
                row0 += rows
            return bufs

        late = []
        g1, g2, g3, g4 = (Gathering(plan, p) for p in packs)
        g1.step(plan.across)
        t = [g1.step(plan.next_to)]
        t = [g1.step(plan.one), g2.step(plan.across, *t)]
        t = [g1.far(*t), g2.step(plan.next_to, *t), g3.step(plan.across, *t)]
        g1.share(*t)
        bufs = ready(0, g1.last(*t))
        t = [g2.step(plan.one, *t), g3.step(plan.next_to, *t), g1.mate, g1.end]
        early = dict(rowf=t)
        slot = [g2.far(*t), g2.share(*t), g3.step(plan.one, *t), g4.step(plan.across, *t)]
        early["colf"] = slot

        def after_rowf(token):
            ready(1, g2.last(token, *slot))
            t = [token, *slot, g2.end]
            early["cola"] = [g3.far(*t), g3.share(*t), g4.step(plan.next_to, *t)]

        def after_colf(token):
            g4.step(plan.one, token)

        def after_cola(token):
            t = [token, *early["cola"], g4.came]
            ready(2, g3.last(*t))
            t = [token, g3.end]
            early["fout"] = [g4.far(*t), g4.share(*t)]

        hooks = dict(
            rowf=lambda outs: after_rowf(outs[5]),
            colf=lambda outs: after_colf(outs[1]),
            cola=lambda outs: after_cola(outs[0][1]),
            ffnf=lambda outs: late.append(ready(3, g4.last(outs[1], *early["fout"]))[3]),
        )
        rows = shards["row_qkv"].shape[0]
        w["norms"] = Weights(bufs, rows, 16, 16 * plan.dp, width, True)
        w["norms"].raw = True
    else:
        tables, own_tables = [jnp.zeros((1,), jnp.int32)] * 2, {}
        early, hooks, late = {}, {}, []
        for n, s in shards.items():
            half = lax.all_gather(s, "fsdp", axis=1, tiled=True)
            full = lax.all_gather(half, "dp", axis=0, tiled=True)
            w[n] = Weights([full], 0, s.shape[0], whole_rows[n], width, False)
        gb = lax.all_gather(norms, "fsdp", axis=1, tiled=True)
        gb = lax.all_gather(gb, "dp", axis=1, tiled=True).astype(F32)
        count = jnp.full((1, width), lax.psum(n_col.astype(F32), AXES))
        gb = jnp.concatenate([gb, count, jnp.zeros_like(count)], 0)
    flts = row_scale[None]

    micros = dict(
        rowf=9,
        colf=8,
        cola=4,
        ffnf=12,
        fout=7,
        ffnb=12,
        colb=10,
        colt=7,
        colg=7,
        rowb=10,
        rowt=13,
        inpb=9,
        lout=9,
    )

    def arr(n, dtype, rows=tokens, vmem=True, hbm=False):
        return Out((rows, n), dtype, vmem, hbm)

    resident = {}

    def run(name, body, smem, ins, weights, outs, grads=(), scratch=(), deps=(), fetch=()):
        ins = [a.bufs[0] if isinstance(a, Weights) else a for a in ins]
        weights = [w[n] if isinstance(n, str) else n for n in weights]
        fetch = [w[a] if isinstance(a, str) else Weights.of(a) for a in fetch]
        lists = own_tables.get(name, tables) + list(smem), ins, weights, outs, grads
        deps = list(deps) + early.get(name, [])
        got = fused(name, body, *lists, plan, resident, micros[name], scratch, deps, fetch)
        if name in hooks:
            hooks[name](got[0])
        return got

    wide = pltpu.VMEM((tokens, width), F32)
    turn = pltpu.VMEM((width // 128, 32 * PITCH + 8, 128), F32)
    score = pltpu.VMEM((heads * 32, 128), F32)
    flat = pltpu.VMEM((tokens // 4, 2 * width), F32)
    moment = arr(width, F32, 8, False, True)
    keep = dict(vmem=False, hbm=True)
    token = arr(128, F32, 8, **keep)

    (normed_row, packed_row, mixed_row, prob, logp, ent, gb), _ = run(
        "rowf",
        row_forward,
        [ints, flts],
        [x] if plan.fast else [x, gb],
        ["norms", "row_qkv"] if plan.fast else ["row_qkv"],
        [
            arr(width, BF16, **keep),
            arr(3 * width, BF16, **keep),
            arr(width, BF16, hbm=True),
            arr(128, F32, heads * 32, **keep),
            arr(128, F32, heads * 32, **keep),
            arr(width, F32, 8, **keep),
            arr(width, F32, 8, **keep),
        ],
        (),
        [score],
    )
    (after_row, normed_col, packed_col), _ = run(
        "colf",
        column_forward,
        [],
        [x, mixed_row[0], gb],
        ["row_out", "col_qkv"],
        [arr(width, F32, hbm=True), arr(width, BF16, **keep), arr(3 * width, BF16, hbm=True)],
        (),
        [turn],
    )
    (mixed_col,), _ = run(
        "cola",
        column_attend,
        [ints],
        [packed_col[0]],
        [],
        [arr(width, BF16, hbm=True)],
        (),
        [flat],
    )
    (after_col, normed_ffn, active, slope, cot_here), _ = run(
        "ffnf",
        feed_forward,
        [],
        [after_row[0], mixed_col[0], gb],
        ["col_out", "ffn_in"],
        [
            arr(width, F32, **keep),
            arr(width, BF16, **keep),
            arr(hidden, BF16, hbm=True),
            arr(hidden, BF16),
        ],
        fetch=[cot],
    )
    (g3,), grads = run(
        "fout",
        ffn_out_grad,
        [ints],
        [active[0], cot_here],
        [],
        [arr(width, BF16)],
        [hidden],
        [turn],
    )
    r1 = Reduction(plan, grads, ["ffn_out"], shards)
    r1.core(*late)
    (grad_hidden, w_in, w_col_out, after_here), grads = run(
        "ffnb",
        ffn_back,
        [],
        [g3, slope, normed_ffn],
        ["ffn_out"],
        [arr(hidden, BF16)],
        [hidden],
        fetch=["ffn_in", "col_out", after_col],
    )
    r2 = Reduction(plan, grads, ["ffn_in"], shards)
    landed = r1.landed()
    r1.first(grads[0], *landed)
    r2.core(*landed)
    (grad_after, g2, gm_col, sums_two, packed_here, normed_here, mixed_here), _ = run(
        "colb",
        column_back,
        [],
        [grad_hidden, after_here, g3, gb],
        [w_in, w_col_out],
        [arr(width, F32, **keep), arr(width, BF16), arr(width, BF16), moment],
        (),
        [wide],
        landed,
        [packed_col[1], normed_col, mixed_col[1]],
    )
    landed = r1.landed() + r2.landed()
    r1.second(sums_two, *landed)
    r2.first(sums_two, *landed)
    (gq_col, mark, active_here, after_here, w_out), _ = run(
        "colt",
        column_attend_back,
        [ints],
        [packed_here, gm_col],
        [],
        [arr(3 * width, BF16), token],
        (),
        [flat, flat],
        landed,
        [active[1], after_col, "ffn_out"],
    )
    (layer_out, mark), _ = run(
        "lout",
        ffn_result,
        [],
        [active_here, after_here],
        [w_out],
        [arr(width, BF16, **keep), token],
        (),
        [turn],
        [mark],
    )
    landed = r1.landed() + r2.landed()
    r1.third(mark, *landed)
    r2.second(mark, *landed)
    (w_col_qkv, w_row_out, after_row_here, grad_after_here), grads = run(
        "colg",
        product_grads,
        [],
        [gq_col, normed_here, mixed_here, g2],
        [],
        [],
        [3 * width, width],
        (),
        landed,
        ["col_qkv", "row_out", after_row[1], grad_after],
    )
    r3 = Reduction(plan, grads, ["col_qkv", "col_out"], shards)
    landed = r1.landed() + r2.landed()
    r1.fourth(grads[0], *landed)
    r2.third(grads[0], *landed)
    r3.core(*landed)
    (grad_row, g1, gm_row, sums_one, packed_here, normed_here, mixed_here), _ = run(
        "rowb",
        row_back,
        [],
        [gq_col, after_row_here, grad_after_here, gb],
        [w_col_qkv, w_row_out],
        [arr(width, F32, **keep), arr(width, BF16), arr(width, BF16), moment],
        (),
        [wide, turn],
        landed,
        [packed_row, normed_row, mixed_row[1]],
    )
    landed = r1.landed() + r2.landed() + r3.landed()
    r2.fourth(sums_one, *landed)
    r3.first(sums_one, *landed)
    (gq_row,), grads = run(
        "rowt",
        row_attend_back,
        [ints, flts],
        [packed_here, gm_row, prob, logp, mixed_here, g1, normed_here, gb],
        [],
        [arr(3 * width, BF16, **keep)],
        [width, 3 * width],
        [score],
        landed,
    )
    r4 = Reduction(plan, grads, ["row_out", "row_qkv"], shards)
    landed = r1.landed() + r2.landed() + r3.landed()
    r4.core(*landed)
    landed = landed + r4.landed()
    r1.finish()
    r2.finish()
    sums = [r.sum for r in (r1, r2)] if plan.fast else []
    r3.third(grads[0], *landed)
    r4.first(*landed, *sums)
    (grad_in, sums_zero), _ = run(
        "inpb",
        input_back,
        [],
        [gq_row, x, grad_row, gb],
        ["row_qkv"],
        [arr(width, F32, **keep), moment],
        (),
        [wide],
        [grads[0], *landed],
    )
    landed = r3.landed() + r4.landed()
    r4.second(sums_zero, *landed)
    r3.fourth(sums_zero, *landed)
    r4.third()
    landed = r4.landed()
    r3.second(*landed)
    r4.fourth()
    r3.finish()
    r4.finish(*([r3.sum] if plan.fast else []))
    got = {}
    for r in (r1, r2, r3, r4):
        got.update(r.result())
    sums_all = plan.everywhere(sums_zero + sums_one + sums_two + ent, r4)
    owned = lax.dynamic_slice_in_dim(sums_all[:6], me * share, share, 1)
    gains, biases = owned[0::2], owned[1::2]
    shape = alignment_input.shape
    return (
        layer_out.reshape(shape),
        grad_in.reshape(shape),
        got["row_qkv"].T,
        got["row_out"],
        got["col_qkv"].T,
        got["col_out"],
        got["ffn_in"].T,
        got["ffn_out"],
        gains,
        biases[:2],
        biases[2],
        sums_all[6, 0],
    )


def solution(mesh):
    def whole(*args):
        plan = Plan(mesh.shape["dp"], mesh.shape["fsdp"], args[0].shape[3])
        return jax.shard_map(
            lambda *blocks: local(plan, *blocks),
            mesh=mesh,
            in_specs=(
                P(AXES, None, None, None),
                P(AXES, None),
                P(AXES),
                P(AXES, None, None, None),
                P("fsdp", "dp"),
                P("dp", "fsdp"),
                P("fsdp", "dp"),
                P("dp", "fsdp"),
                P("fsdp", "dp"),
                P("dp", "fsdp"),
                P(None, AXES),
                P(None, AXES),
            ),
            out_specs=(
                P(AXES, None, None, None),
                P(AXES, None, None, None),
                P("fsdp", "dp"),
                P("dp", "fsdp"),
                P("fsdp", "dp"),
                P("dp", "fsdp"),
                P("fsdp", "dp"),
                P("dp", "fsdp"),
                P(None, AXES),
                P(None, AXES),
                P(AXES),
                P(),
            ),
            check_vma=False,
        )(*args)

    return whole
```

```python
import jax
import jax.numpy as jnp
import numpy as np
from jax import lax
from jax.experimental import pallas as pl
from jax.experimental.pallas import tpu as pltpu
from jax.sharding import PartitionSpec as P

HD = 64
AXES = ("dp", "fsdp")
norm_eps = 1e-05
penalty_weight = 1.0
masked_score = -1000000000.0
never = -1e30

F32 = jnp.float32
BF16 = jnp.bfloat16
MIB = 1 << 20
PITCH = 33


def dot(a, b, ca, cb):
    return lax.dot_general(a, b, (((ca,), (cb,)), ((), ())), preferred_element_type=F32)


class Weights:
    def __init__(self, bufs, row0, rows, whole_rows, width, blocked, table=0):
        self.raw = self.here = False
        self.dtype = BF16
        self.bufs, self.row0, self.rows, self.table = bufs, row0, rows, table
        self.whole_rows, self.width, self.blocked = whole_rows, width, blocked


    @staticmethod
    def of(a):
        w = Weights([a], 0, a.shape[0], a.shape[0], a.shape[1], False)
        w.dtype = a.dtype
        return w

    @staticmethod
    def held(a):
        w = Weights.of(a)
        w.here = True
        return w

    def copies(self, plan):
        if self.here:
            return 0
        return sum(b.shape[0] for b in self.bufs) if self.blocked else 1


class Loaded:
    def __init__(self, ref, copies):
        self.ref, self.copies = ref, copies

    def start(self, part=None):
        for c in self.copies if part is None else self.copies[part : part + 1]:
            c.start()

    def wait(self):
        for c in self.copies:
            c.wait()
        return self.ref


class Out:
    def __init__(self, shape, dtype, vmem=True, hbm=False):
        self.shape, self.dtype, self.vmem, self.hbm = shape, dtype, vmem, hbm
        self.parts = max(1, shape[1] // 768) if hbm else 0


def fused(
    name, body, smem, ins, weights, outs, grads, plan, resident, micros, scratch=(), deps=(), fetch=()
):
    arrays, index, spaces = [], {}, []

    def slot(a):
        if id(a) not in index:
            index[id(a)] = len(arrays)
            stays = id(a) in resident
            spaces.append(pltpu.VMEM if stays else pltpu.HBM)
            arrays.append(pltpu.with_memory_space_constraint(a, spaces[-1]))
        return index[id(a)]

    in_slots = [slot(a) for a in ins]
    w_slots = [[slot(b) for b in w.bufs] for w in (*weights, *fetch)]
    weights = list(weights)
    n_weights = len(weights)
    for a in deps:
        arrays.append(a)
        spaces.append(pl.ANY)
    n_smem = len(smem)
    vm, n_sem = [], 0
    for a in ins:
        if id(a) not in resident:
            vm.append(pltpu.VMEM(a.shape, a.dtype))
            n_sem += 1
    for w in (*weights, *fetch):
        n_sem += w.copies(plan)
    for w in weights:
        if w.here:
            continue
        raw = (w.whole_rows // w.rows * plan.fsdp, w.rows, w.width // plan.fsdp)
        vm.append(pltpu.VMEM(raw if w.raw else (w.whole_rows, w.width), BF16))
    out_shapes, out_spaces = [], []
    for o in outs:
        if o.vmem:
            out_shapes.append(pltpu.VMEM(o.shape, o.dtype))
            out_spaces.append(pltpu.VMEM)
        else:
            vm.append(pltpu.VMEM(o.shape, o.dtype))
        if o.hbm:
            out_shapes.append(pltpu.HBM(o.shape, o.dtype))
            out_spaces.append(pltpu.HBM)
            n_sem += o.parts
    f_at = len(out_shapes)
    for w in fetch:
        out_shapes.append(pltpu.VMEM((w.whole_rows, w.width), w.dtype))
        out_spaces.append(pltpu.VMEM)
    g_at = len(out_shapes)
    width = plan.width
    for rows in grads:
        vm.append(pltpu.VMEM((rows, width), BF16))
        n_sem += plan.dp * plan.fsdp if plan.fast else 1
    if grads and plan.fast:
        per = sum(rows // plan.dp for rows in grads)
        shape = pltpu.HBM((plan.slots, per, width // plan.fsdp), BF16)
        out_shapes += [shape, shape]
    elif grads:
        out_shapes += [pltpu.HBM((rows, width), BF16) for rows in grads]
    out_spaces += [pltpu.HBM] * (len(out_shapes) - g_at)
    n_in, n_out, n_vm = len(arrays), len(out_shapes), len(vm)
    used_vmem = sum(int(np.prod(m.shape)) * np.dtype(m.dtype).itemsize for m in (*vm, *scratch))

    def kernel(*refs):
        sm = refs[:n_smem]
        hb = refs[n_smem : n_smem + n_in]
        ob = refs[n_smem + n_in : n_smem + n_in + n_out]
        rest = refs[n_smem + n_in + n_out :]
        vrefs, extra, sems = list(rest[:n_vm]), rest[n_vm:-1], rest[-1]
        used = [0]

        def sem():
            used[0] += 1
            return sems.at[used[0] - 1]

        loads = Loads()
        for a, s in zip(ins, in_slots):
            if id(a) in resident:
                loads.append(Loaded(hb[s], []))
            else:
                ref = vrefs.pop(0)
                loads.append(Loaded(ref, [pltpu.make_async_copy(hb[s], ref, sem())]))
        wl = []
        for n, (w, slots) in enumerate(zip((*weights, *fetch), w_slots)):
            copies = []
            if w.here:
                dst = hb[slots[0]]
            elif n < n_weights:
                dst = vrefs.pop(0)
            else:
                dst = ob[f_at + n - n_weights]
            if w.here:
                pass
            elif w.blocked:
                cols = w.width // plan.fsdp
                count = 0
                for s in slots:
                    for j in range(arrays[s].shape[0]):
                        block = sm[w.table][count] if w.table is not None else count
                        count += 1
                        row = (block // plan.fsdp) * w.rows
                        col = (block % plan.fsdp) * cols
                        if w.table is not None:
                            row, col = pl.multiple_of(row, 16), pl.multiple_of(col, 128)
                        spot = dst.at[pl.ds(row, w.rows), pl.ds(col, cols)]
                        if w.raw:
                            spot = dst.at[count - 1]
                        src = hb[s].at[j, pl.ds(w.row0, w.rows), :]
                        copies.append(pltpu.make_async_copy(src, spot, sem()))
            else:
                copies.append(pltpu.make_async_copy(hb[slots[0]], dst, sem()))
            (wl if n < n_weights else loads.fetched).append(Loaded(dst, copies))
        ol = []
        at = 0
        for o in outs:
            if o.vmem:
                ref = ob[at]
                at += 1
            else:
                ref = vrefs.pop(0)
            copies = []
            if o.hbm:
                for k in range(o.parts):
                    lanes = slice(None)
                    if o.parts > 1:
                        lanes = pl.ds(k * 768, 768)
                    copies.append(
                        pltpu.make_async_copy(ref.at[:, lanes], ob[at].at[:, lanes], sem())
                    )
                at += 1
            ol.append(Loaded(ref, copies))
        gl = []
        row0 = 0
        for k, rows in enumerate(grads):
            src = vrefs.pop(0)
            if plan.fast:
                gl.append(Blocks(src, ob[g_at], ob[g_at + 1], sm[1], plan, rows, row0, sem))
                row0 += rows // plan.dp
            else:
                gl.append(Loaded(src, [pltpu.make_async_copy(src, ob[g_at + k], sem())]))
        for l in (*loads[:1], *wl[:1], *loads[1:], *wl[1:]):
            l.start()
        body(sm[:1] + sm[3:] if name == "rowf" else sm[3:], loads, wl, ol, gl, extra)
        for l in (*ol, *gl, *loads.fetched):
            l.wait()

    res = pl.pallas_call(
        kernel,
        name=name,
        out_shape=out_shapes,
        in_specs=[pl.BlockSpec(memory_space=pltpu.SMEM)] * n_smem
        + [pl.BlockSpec(memory_space=m) for m in spaces],
        out_specs=[pl.BlockSpec(memory_space=m) for m in out_spaces],
        scratch_shapes=vm + list(scratch) + [pltpu.SemaphoreType.DMA((n_sem,))],
        compiler_params=pltpu.CompilerParams(vmem_limit_bytes=used_vmem + 7 * MIB),
        cost_estimate=pl.CostEstimate(
            flops=int(micros * 1e6), bytes_accessed=int(micros * 3e3), transcendentals=0
        ),
    )(*smem, *arrays)
    got, at = [], 0
    for o in outs:
        both = res[at : at + o.vmem + o.hbm]
        at += o.vmem + o.hbm
        if o.vmem:
            resident[id(both[0])] = both[0]
        got.append(both[0] if len(both) == 1 else both)
    for a in res[f_at:g_at]:
        resident[id(a)] = a
        got.append(Weights.held(a))
    return got, res[g_at:]


class Loads(list):
    def __init__(self):
        self.fetched = []

    def later(self):
        for l in self.fetched:
            l.start()


class Blocks:
    def __init__(self, ref, kept, sent, table, plan, rows, row0, sem):
        self.ref, self.plan = ref, plan
        self.per, self.cols = rows // plan.dp, plan.width // plan.fsdp
        self.kept, self.sent, self.table, self.row0 = kept, sent, table, row0
        self.sems = [sem() for _ in range(plan.dp * plan.fsdp)]
        self.begun = 0

    def copy(self, n, out, slot):
        row, col = (n // self.plan.fsdp) * self.per, (n % self.plan.fsdp) * self.cols
        return pltpu.make_async_copy(
            self.ref.at[row : row + self.per, col : col + self.cols],
            out.at[slot, pl.ds(self.row0, self.per), :],
            self.sems[n],
        )

    def start(self, rows=None):
        rows = self.ref.shape[0] if rows is None else rows
        end = rows // self.per * self.plan.fsdp
        slots = self.plan.slots
        for n in range(self.begun, end):
            place = self.table[n]

            @pl.when(place < slots)
            def _():
                self.copy(n, self.kept, place).start()

            @pl.when(place >= slots)
            def _():
                self.copy(n, self.sent, place - slots).start()

        self.begun = end

    def wait(self):
        for n in range(self.begun):
            self.copy(n, self.kept, 0).wait()


def stamp(out):
    out.ref[...] = jnp.zeros(out.ref.shape, out.ref.dtype)
    out.start()


def normal_form(v):
    centred = v - jnp.mean(v, -1, keepdims=True)
    rstd = lax.rsqrt(jnp.mean(centred * centred, -1, keepdims=True) + norm_eps)
    return centred * rstd, rstd


def norm_rows(src, dst, gb, k, total):
    for t in range(0, total, 256):
        xhat, _ = normal_form(src[t : t + 256, :].astype(F32))
        dst[t : t + 256, :] = (xhat * gb[k : k + 1, :] + gb[k + 3 : k + 4, :]).astype(BF16)


def norm_back(dn_ref, src, base, gb, k, total, emit, sums):
    gain = gb[k : k + 1, :]
    gain_sum = jnp.zeros_like(gain)
    bias_sum = jnp.zeros_like(gain)
    for t in range(0, total, 256):
        xhat, rstd = normal_form(src[t : t + 256, :].astype(F32))
        dn = dn_ref[t : t + 256, :]
        gain_sum = gain_sum + jnp.sum(dn * xhat, 0, keepdims=True)
        bias_sum = bias_sum + jnp.sum(dn, 0, keepdims=True)
        dx = dn * gain
        low = jnp.mean(dx, -1, keepdims=True)
        mix = jnp.mean(dx * xhat, -1, keepdims=True)
        emit(t, base[t : t + 256, :].astype(F32) + rstd * (dx - low - xhat * mix))
    none = jnp.zeros((1, gain.shape[1]), F32)
    rows = [none] * (2 * k) + [gain_sum, bias_sum] + [none] * (6 - 2 * k)
    sums[...] = jnp.concatenate(rows, 0)


def head_masks(lanes):
    lane = lax.broadcasted_iota(jnp.int32, (1, lanes), 1)
    low = ((lane // HD) % 2 == 0).astype(F32)
    return low.astype(BF16), (1.0 - low).astype(BF16)


def four(ref, col):
    return jnp.concatenate([ref[g * 256 : (g + 1) * 256, col : col + 128] for g in range(4)], 1)


def pick(big):
    seg = lax.broadcasted_iota(jnp.int32, (32, 256), 1) // 32
    out = big[:32, :]
    for k in range(1, 8):
        out = jnp.where(seg == k, big[k * 32 : (k + 1) * 32, :], out)
    out = out[:, :128] + out[:, 128:]
    out = out + pltpu.roll(out, 64, 1)
    return out + pltpu.roll(out, 32, 1)


def spread(small):
    seg = lax.broadcasted_iota(jnp.int32, (32, 256), 1) // 32
    wide = jnp.concatenate([small, small], 1)
    return jnp.concatenate([jnp.where(seg == k, wide, 0.0).astype(BF16) for k in range(8)], 0)


def gathered_norms(blocks, table):
    slots = blocks.shape[0]
    values = jnp.sum(blocks[...].astype(F32), 1).astype(BF16)
    place = lax.broadcasted_iota(jnp.int32, (slots, 1), 0)
    owner = jnp.zeros((slots, 1), jnp.int32)
    for j in range(slots):
        owner = jnp.where(place == j, table[j], owner)
    share = 768 // slots
    lane = lax.broadcasted_iota(jnp.int32, (1, 768), 1)
    row = lax.broadcasted_iota(jnp.int32, (values.shape[1], 1), 0)
    mine = lane // share == owner
    rows = []
    for k in range(6):
        spot = (row == k * share + lane % share).astype(F32).astype(BF16)
        rows.append(jnp.sum(jnp.where(mine, dot(values, spot, 1, 0), 0.0), 0, keepdims=True))
    count = jnp.where(lax.broadcasted_iota(jnp.int32, (1, values.shape[1]), 1) == 6 * share, 1.0, 0.0)
    total = jnp.sum(values.astype(F32) * count)
    rows.append(jnp.full((1, 768), total, F32))
    rows.append(jnp.zeros((1, 768), F32))
    return jnp.concatenate(rows, 0)


def row_forward(sm, I, W, O, G, X):
    ints, flts = sm[-2:]
    x = I[0]
    normed, packed, mixed, prob, logp, ent, norms = O
    sc = X[0]
    if len(W) > 1:
        norms.ref[...] = gathered_norms(W[0].wait(), sm[0])
    else:
        norms.ref[...] = I[1].wait()[...]
    norms.start()
    xr, g = x.wait(), norms.ref
    norm_rows(xr, normed.ref, g, 0, 1024)
    normed.start()
    wt = W[-1].wait()
    nr = normed.ref[...]
    n_seq, n_col = ints[0], ints[1]
    keep = (lax.broadcasted_iota(jnp.int32, (1024, 1), 0) // 32 < n_seq).astype(F32)
    width = nr.shape[1]
    heads = width // HD
    pr = packed.ref
    for n in range(0, 3 * width, 256):
        out = dot(nr, wt[n : n + 256, :], 1, 1)
        if n < width:
            out = out * keep
        pr[:, n : n + 256] = out.astype(BF16)
        if (n + 256) % 768 == 0:
            packed.start(n // 768)
    halves = head_masks(512)
    for m in range(heads // 2):
        q, k = four(pr, m * 128), four(pr, width + m * 128)
        for e in range(2):
            h = 2 * m + e
            sc[h * 32 : (h + 1) * 32, :] = pick(dot(q * halves[e], k, 1, 1))
    lane = lax.broadcasted_iota(jnp.int32, (1, 128), 1) % 32
    s = jnp.where(lane < n_col, sc[...] * flts[0], masked_score)
    top = jnp.max(s, -1, keepdims=True)
    total = jnp.sum(jnp.exp(s - top), -1, keepdims=True) * 0.25
    lp = s - (top + jnp.log(total))
    p = jnp.exp(lp)
    prob.ref[...] = p
    logp.ref[...] = lp
    prob.start()
    logp.start()
    entropy = jnp.sum(p * lp, -1, keepdims=True) * -0.25
    row = lax.broadcasted_iota(jnp.int32, entropy.shape, 0) % 32
    total = jnp.sum(jnp.where(row < n_col, entropy, 0.0))
    share = total / norms.ref[6:7, :]
    ent.ref[...] = jnp.where(lax.broadcasted_iota(jnp.int32, ent.ref.shape, 0) == 6, share, 0.0)
    ent.start()
    second = (lax.broadcasted_iota(jnp.int32, (1, 512), 1) // HD) % 2 == 1
    for m in range(heads // 2):
        v = four(pr, 2 * width + m * 128)
        both = [
            dot(spread(prob.ref[h * 32 : (h + 1) * 32, :]), v, 1, 0) for h in (2 * m, 2 * m + 1)
        ]
        out = jnp.where(second, both[1], both[0]).astype(BF16)
        for t in range(4):
            mixed.ref[t * 256 : (t + 1) * 256, m * 128 : (m + 1) * 128] = out[
                :, t * 128 : (t + 1) * 128
            ]
    mixed.start()


def stacked(x, halves):
    return jnp.concatenate([x * halves[0], x * halves[1]], 0)


def segment(rows):
    return (lax.broadcasted_iota(jnp.int32, (rows, 256), 1) // 32) % 4


def pick_four(big):
    seg = segment(32)
    out = big[:32, :]
    for k in range(1, 4):
        out = jnp.where(seg == k, big[k * 32 : (k + 1) * 32, :], out)
    return out


def spread_four(small):
    seg = segment(32)
    return jnp.concatenate([jnp.where(seg == k, small, 0.0).astype(BF16) for k in range(4)], 0)


def unstack(both):
    lane = lax.broadcasted_iota(jnp.int32, (128, 128), 1)
    return jnp.where(lane < HD, both[:128], both[128:])


def to_columns(src, take):
    for t in range(0, 1024, 256):
        lanes = [
            jnp.concatenate([src[j, pl.ds(t // 32 + k, 32, stride=PITCH), :] for k in range(8)], 0)
            for j in range(src.shape[0])
        ]
        take(t, jnp.concatenate(lanes, 1))


def put(dst, start, n, value):
    for r in range(value.shape[0] // 32):
        at = (start // 32 + r) * PITCH
        for j in range(value.shape[1] // 128):
            piece = value[r * 32 : (r + 1) * 32, j * 128 : (j + 1) * 128]
            dst[n // 128 + j, at : at + 32, :] = piece


def column_forward(sm, I, W, O, G, X):
    x, mixed_row, gb = I
    after, normed, packed = O
    (ar,) = X
    width = normed.ref.shape[1]
    mr, xr = mixed_row.wait(), x.wait()
    wo = W[0].wait()
    for n in range(0, width, 256):
        out = xr[:, n : n + 256].astype(F32) + dot(mr[...], wo[:, n : n + 256], 1, 0)
        put(ar, 0, n, out)
    g = gb.wait()

    def take(t, rows):
        after.ref[t : t + 256, :] = rows

    to_columns(ar, take)
    after.start()
    norm_rows(after.ref, normed.ref, g, 1, 1024)
    normed.start()
    wt = W[1].wait()
    nr = normed.ref[...]
    pr = packed.ref
    for n in range(0, 3 * width, 256):
        pr[:, n : n + 256] = dot(nr, wt[n : n + 256, :], 1, 1).astype(BF16)
        if (n + 256) % 768 == 0:
            packed.start(n // 768)


def column_softmax(sc, n_seq):
    def block(b, carry):
        at = pl.ds(pl.multiple_of(b * 32, 32), 32)
        s = sc[at, :]
        s = jnp.where(lax.broadcasted_iota(jnp.int32, s.shape, 0) < n_seq, s, never)
        p = jnp.exp(s - jnp.max(s, 0, keepdims=True))
        sc[at, :] = p * (1.0 / jnp.sum(p, 0, keepdims=True))
        return carry

    lax.fori_loop(0, sc.shape[0] // 32, block, 0)


def column_attend(sm, I, W, O, G, X):
    (ints,) = sm
    (mixed,) = O
    (sc,) = X
    width = mixed.ref.shape[1]
    pr = I[0].wait()
    halves = head_masks(128)

    def scores(b, carry):
        rows = pl.ds(pl.multiple_of(b * 128, 128), 128)
        at = pl.ds(pl.multiple_of(b * 32, 32), 32)
        for lo in range(0, width, 128):
            qs = stacked(pr[rows, lo : lo + 128] * 0.125, halves)
            k = pr[rows, width + lo : width + lo + 128]
            sc[at, 2 * lo : 2 * lo + 256] = pick_four(dot(k, qs, 1, 1))
        return carry

    lax.fori_loop(0, 8, scores, 0)
    column_softmax(sc, ints[0])

    def mix(b, carry):
        rows = pl.ds(pl.multiple_of(b * 128, 128), 128)
        at = pl.ds(pl.multiple_of(b * 32, 32), 32)
        for lo in range(0, width, 128):
            v = pr[rows, 2 * width + lo : 2 * width + lo + 128]
            p = spread_four(sc[at, 2 * lo : 2 * lo + 256])
            mixed.ref[rows, lo : lo + 128] = unstack(dot(p, v, 0, 0)).astype(BF16)
        return carry

    lax.fori_loop(0, 8, mix, 0)
    mixed.start()


def column_all(sm, I, W, O, G, X):
    column_forward((), I, W, O[:3], G, X[:1])
    column_attend(sm, [Loaded(O[2].ref, [])], W, O[3:], G, X[1:])


def feed_forward(sm, I, W, O, G, X):
    after_row, mixed, gb = I
    after, normed, active, slope = O
    width = normed.ref.shape[1]
    hidden = active.ref.shape[1]
    ar, mr = after_row.wait(), mixed.wait()
    wo = W[0].wait()
    for n in range(0, width, 256):
        after.ref[:, n : n + 256] = ar[:, n : n + 256] + dot(mr[...], wo[:, n : n + 256], 1, 0)
    after.start()
    norm_rows(after.ref, normed.ref, gb.wait(), 2, 1024)
    normed.start()
    wt = W[1].wait()
    I.later()
    nr = normed.ref[...]
    for n in range(0, hidden, 256):
        h = dot(nr, wt[n : n + 256, :], 1, 1)
        cdf = 0.5 + 0.5 * lax.erf(h * (0.5**0.5))
        active.ref[:, n : n + 256] = (h * cdf).astype(BF16)
        bell = jnp.exp(h * h * -0.5) * (0.5 / np.pi) ** 0.5
        slope.ref[:, n : n + 256] = (cdf + h * bell).astype(BF16)
        if (n + 256) % 768 == 0:
            active.start(n // 768)
    slope.start()


def weight_grad(dst, left, right, step=768):
    rows = dst.ref.shape[0]
    blocks = isinstance(dst, Blocks)
    for n in range(0, rows, step):
        dst.ref[n : n + step, :] = dot(left[:, n : n + step], right[...], 0, 0).astype(BF16)
        if blocks:
            dst.start(n + step)
    if not blocks:
        dst.start()


def ffn_out_grad(sm, I, W, O, G, X):
    (ints,) = sm
    active, cot = I
    (g3,) = O
    (wide,) = X
    put(wide, 0, 0, cot.wait()[...].astype(F32))
    n_seq, n_col = ints[0], ints[1]

    def take(t, rows):
        at = lax.broadcasted_iota(jnp.int32, (256, 1), 0) + t
        keep = ((at % 32 < n_seq) & (at // 32 < n_col)).astype(F32)
        g3.ref[t : t + 256, :] = (rows * keep).astype(BF16)

    to_columns(wide, take)
    g3.start()
    weight_grad(G[0], active.wait(), g3.ref)


def ffn_back(sm, I, W, O, G, X):
    g3, slope, normed = I
    (grad_hidden,) = O
    wf = W[0].wait()
    gr, sl = g3.wait(), slope.wait()
    I.later()
    gh = grad_hidden.ref
    hidden = gh.shape[1]
    gv = gr[...]
    for n in range(0, hidden, 256):
        d = dot(gv, wf[n : n + 256, :], 1, 1)
        gh[:, n : n + 256] = (d * sl[:, n : n + 256].astype(F32)).astype(BF16)
    grad_hidden.start()
    weight_grad(G[0], gh, normed.wait())


def ffn_result(sm, I, W, O, G, X):
    active, after = I
    layer_out = O[0]
    (res,) = X
    width = layer_out.ref.shape[1]
    wf = W[0].wait()
    ac, ar = active.wait(), after.wait()
    I.later()
    for n in range(0, width, 256):
        put(res, 0, n, ar[:, n : n + 256] + dot(ac[...], wf[:, n : n + 256], 1, 0))

    def take(t, rows):
        layer_out.ref[t : t + 256, :] = rows.astype(BF16)

    to_columns(res, take)
    layer_out.start()
    stamp(O[1])


def column_back(sm, I, W, O, G, X):
    grad_hidden, after_col, g3, gb = I
    grad_after, branch, grad_mixed, sums = O
    (dn,) = X
    g2, gm = branch.ref, grad_mixed.ref
    width = g2.shape[1]
    gh = grad_hidden.wait()
    wf = W[0].wait()
    I.later()
    for n in range(0, width, 256):
        dn[:, n : n + 256] = dot(gh[...], wf[:, n : n + 256], 1, 0)
    ac, base, g = after_col.wait(), g3.wait(), gb.wait()

    def emit(t, rows):
        grad_after.ref[t : t + 256, :] = rows
        g2[t : t + 256, :] = rows.astype(BF16)

    norm_back(dn, ac, base, g, 2, 1024, emit, sums.ref)
    grad_after.start()
    sums.start()
    wo = W[1].wait()
    for n in range(0, width, 256):
        gm[:, n : n + 256] = dot(g2[...], wo[n : n + 256, :], 1, 1).astype(BF16)
    grad_mixed.start()


def column_attend_back(sm, I, W, O, G, X):
    (ints,) = sm
    packed, grad_mixed = I
    gq = O[0]
    sc, dsc = X
    pr, gm = packed.wait(), grad_mixed.wait()
    I.later()
    width = gm.shape[1]
    halves = head_masks(128)
    out = gq.ref

    def scores(b, carry):
        rows = pl.ds(pl.multiple_of(b * 128, 128), 128)
        at = pl.ds(pl.multiple_of(b * 32, 32), 32)
        for lo in range(0, width, 128):
            qs = stacked(pr[rows, lo : lo + 128] * 0.125, halves)
            k = pr[rows, width + lo : width + lo + 128]
            v = pr[rows, 2 * width + lo : 2 * width + lo + 128]
            des = stacked(gm[rows, lo : lo + 128], halves)
            sc[at, 2 * lo : 2 * lo + 256] = pick_four(dot(k, qs, 1, 1))
            dsc[at, 2 * lo : 2 * lo + 256] = pick_four(dot(v, des, 1, 1))
        return carry

    lax.fori_loop(0, 8, scores, 0)
    column_softmax(sc, ints[0])

    def pull(b, carry):
        at = pl.ds(pl.multiple_of(b * 32, 32), 32)
        p, dp = sc[at, :], dsc[at, :]
        dsc[at, :] = p * (dp - jnp.sum(p * dp, 0, keepdims=True))
        return carry

    lax.fori_loop(0, 8, pull, 0)

    def spreads(b, carry):
        rows = pl.ds(pl.multiple_of(b * 128, 128), 128)
        at = pl.ds(pl.multiple_of(b * 32, 32), 32)
        for lo in range(0, width, 128):
            qs = stacked(pr[rows, lo : lo + 128] * 0.125, halves)
            k = pr[rows, width + lo : width + lo + 128]
            des = stacked(gm[rows, lo : lo + 128], halves)
            ds = spread_four(dsc[at, 2 * lo : 2 * lo + 256])
            dq = unstack(dot(ds, k, 0, 0)) * 0.125
            out[rows, lo : lo + 128] = dq.astype(BF16)
            out[rows, width + lo : width + lo + 128] = dot(ds, qs, 1, 0).astype(BF16)
            dv = dot(spread_four(sc[at, 2 * lo : 2 * lo + 256]), des, 1, 0)
            out[rows, 2 * width + lo : 2 * width + lo + 128] = dv.astype(BF16)
        return carry

    lax.fori_loop(0, 8, spreads, 0)
    gq.start()


def column_back_and_result(sm, I, W, O, G, X):
    attend, rest = Loads(), Loads()
    attend.extend(I[:2])
    rest.extend(I[2:])
    column_attend_back(sm, attend, W, O[:1], G, X[:2])
    ffn_result((), rest, W, O[1:], G, X[2:])


def product_grads(sm, I, W, O, G, X):
    I.later()
    for k, g in enumerate(G):
        weight_grad(g, I[2 * k].wait(), I[2 * k + 1].wait())


def row_back(sm, I, W, O, G, X):
    gq_col, after_row, grad_after, gb = I
    grad_row, branch, grad_mixed, sums = O
    dn, wide = X
    g1, gm = branch.ref, grad_mixed.ref
    width = g1.shape[1]
    wc = W[0].wait()
    gc = gq_col.wait()
    I.later()
    for n in range(0, width, 256):
        dn[:, n : n + 256] = dot(gc[...], wc[:, n : n + 256], 1, 0)
    ar, base, g = after_row.wait(), grad_after.wait(), gb.wait()

    def emit(t, rows):
        put(wide, t, 0, rows)

    norm_back(dn, ar, base, g, 1, 1024, emit, sums.ref)
    sums.start()

    def take(t, rows):
        grad_row.ref[t : t + 256, :] = rows
        g1[t : t + 256, :] = rows.astype(BF16)

    to_columns(wide, take)
    grad_row.start()
    wo = W[1].wait()
    for n in range(0, width, 256):
        gm[:, n : n + 256] = dot(g1[...], wo[n : n + 256, :], 1, 1).astype(BF16)
    grad_mixed.start()


def row_attend_back(sm, I, W, O, G, X):
    ints, flts = sm
    packed, grad_mixed, prob, logp, mixed, g1, normed, gb = I
    (gq,) = O
    (sc,) = X
    n_seq, n_col = ints[0], ints[1]
    pr, gm = packed.wait(), grad_mixed.wait()
    I.later()
    width = gm.shape[1]
    heads = width // HD
    halves = head_masks(512)
    for m in range(heads // 2):
        d, v = four(gm, m * 128), four(pr, 2 * width + m * 128)
        for e in range(2):
            h = 2 * m + e
            sc[h * 32 : (h + 1) * 32, :] = pick(dot(d * halves[e], v, 1, 1))
    p, lp = prob.wait()[...], logp.wait()[...]
    dp = sc[...]
    ent = jnp.sum(p * lp, -1, keepdims=True) * -0.25
    row = lax.broadcasted_iota(jnp.int32, ent.shape, 0) % 32
    w = jnp.where(row < n_col, penalty_weight / gb.wait()[6:7, 0:1], 0.0)
    ds = p * (dp - jnp.sum(p * dp, -1, keepdims=True) * 0.25) - w * p * (lp + ent)
    sc[...] = ds
    keep = (lax.broadcasted_iota(jnp.int32, (1024, 1), 0) // 32 < n_seq).astype(F32)
    scale = flts[0]
    out = gq.ref
    for m in range(heads // 2):
        lo = m * 128
        q, k, d = four(pr, lo), four(pr, width + lo), four(gm, lo)
        dq = dk = dv = 0.0
        for e in range(2):
            h = 2 * m + e
            pb = spread(prob.ref[h * 32 : (h + 1) * 32, :])
            sb = spread(sc[h * 32 : (h + 1) * 32, :])
            dq = dq + dot(sb, k * halves[e], 1, 0)
            dk = dk + dot(sb, q * halves[e], 0, 0)
            dv = dv + dot(pb, d * halves[e], 0, 0)
        for t in range(4):
            rows, lanes = slice(t * 256, (t + 1) * 256), slice(t * 128, (t + 1) * 128)
            out[rows, lo : lo + 128] = (
                dq[:, lanes] * (scale * keep[t * 256 : (t + 1) * 256])
            ).astype(BF16)
            out[rows, width + lo : width + lo + 128] = (dk[:, lanes] * scale).astype(BF16)
            out[rows, 2 * width + lo : 2 * width + lo + 128] = dv[:, lanes].astype(BF16)
    gq.start()
    weight_grad(G[0], mixed.wait(), g1.wait())
    weight_grad(G[1], out, normed.wait())


def input_back(sm, I, W, O, G, X):
    gq, x, grad_row, gb = I
    grad_in, sums = O
    (dn,) = X
    width = dn.shape[1]
    gr = gq.wait()
    wt = W[0].wait()
    I.later()
    for n in range(0, width, 256):
        dn[:, n : n + 256] = dot(gr[...], wt[:, n : n + 256], 1, 0)

    def emit(t, rows):
        grad_in.ref[t : t + 256, :] = rows

    norm_back(dn, x.wait(), grad_row.wait(), gb.wait(), 0, 1024, emit, sums.ref)
    grad_in.start()
    sums.start()


class Plan:
    def __init__(self, dp, fsdp, width):
        self.dp, self.fsdp, self.width = dp, fsdp, width
        self.fast = fsdp == 2 and dp == 16
        self.slots = dp * fsdp // 2
        if not self.fast:
            return
        place = [(z, x, c, y) for z in range(4) for x in range(2) for c in range(2) for y in range(2)]
        index = {p: n for n, p in enumerate(place)}

        def one(p):
            z, x, c, y = p
            return (z, 1 - x, c, y) if c == 0 else (z, x, c, 1 - y)

        def two(p):
            z, x, c, y = p
            return (z, 1 - x, c, y) if c == 1 else (z, x, c, 1 - y)

        def next_to(p):
            return (p[0] ^ 1, *p[1:])

        def across(p):
            return (p[0] ^ 2, *p[1:])

        def mate(p):
            return (p[0], p[1], 1 - p[2], p[3])

        def pairs(f):
            return [(n, index[f(p)]) for n, p in enumerate(place)]

        self.one, self.two, self.core = pairs(one), pairs(two), pairs(mate)
        self.next_to, self.across = pairs(next_to), pairs(across)
        gathered, owners = [], []
        for p in place:
            gathered.append([])
            for order in ((across, next_to, one, two), (one, across, next_to, two)):
                held = [p]
                for f in order:
                    held = held + [f(q) for q in held]
                gathered[-1].append([index[q] for q in held])
            owners.append([])
            for order in ((across, next_to, two, one), (two, across, next_to, one)):
                owned = [p]
                for f in order:
                    owned = owned + [f(q) for q in owned]
                owners[-1].append([index[q] for q in owned])
        mates = [index[mate(p)] for p in place]
        self.gather_tables = [
            np.array([gathered[n][k] + gathered[m][k] for n, m in enumerate(mates)], np.int32)
            for k in range(2)
        ]
        self.owner_tables = []
        for k in range(2):
            owned = np.array([owners[n][k] + owners[m][k] for n, m in enumerate(mates)], np.int32)
            self.owner_tables.append(np.argsort(owned, 1).astype(np.int32))

    def go(self, v, perm):
        return lax.ppermute(v, AXES, perm)

    def everywhere(self, v, beside):
        if not self.fast:
            return lax.psum(v, AXES)
        for perm in (self.core, self.one):
            v = v + lax.ppermute(v, AXES, perm)
        v = after(v, *beside.second_came)
        for perm in (self.two, self.next_to):
            v = v + lax.ppermute(v, AXES, perm)
        v = after(v, *beside.third_came)
        return v + lax.ppermute(v, AXES, self.across)


def after(v, *others):
    return lax.optimization_barrier((v, *others))[0]


class Gathering:
    def __init__(self, plan, shard):
        self.plan, self.have = plan, [shard[None]]

    def all(self, others):
        if others:
            self.have = list(lax.optimization_barrier((*self.have, *others)))[: len(self.have)]
        self.have = [jnp.concatenate(self.have, 0)] if len(self.have) > 1 else self.have
        return self.have[0]

    def step(self, perm, *others):
        self.came = self.plan.go(self.all(others), perm)
        self.have.append(self.came)
        return self.came

    def far(self, *others):
        self.mine = self.all(others)
        self.came = self.plan.go(self.mine, self.plan.two)
        return self.came

    def share(self, *others):
        mine = after(self.mine, *others) if others else self.mine
        self.mate = self.plan.go(mine, self.plan.core)
        return self.mate

    def last(self, *others):
        far = after(self.came, *others) if others else self.came
        self.end = self.plan.go(far, self.plan.core)
        return [self.mine, self.came, self.mate, self.end]


class Reduction:
    def __init__(self, plan, grads, names, shards):
        self.plan = plan
        self.names = [(n, shards[n].shape[0]) for n in names]
        if plan.fast:
            kept, self.sent = grads
            self.terms, self.size = [kept], kept.shape[0]
        else:
            self.whole = grads

    def go(self, v, perm):
        return lax.ppermute(v.astype(BF16), AXES, perm)

    def landed(self):
        return [self.came] if self.plan.fast else []

    def core(self, *others):
        if self.plan.fast:
            sent = after(self.sent, *others) if others else self.sent
            self.came = self.go(sent, self.plan.core)

    def total(self, start, stop):
        return sum(t[start:stop].astype(F32) for t in self.terms)

    def step(self, perm, *others):
        if self.plan.fast:
            came = after(self.came, *others) if others else self.came
            self.terms.append(came)
            self.size //= 2
            self.came = self.go(self.total(self.size, 2 * self.size), perm)

    def first(self, *others):
        self.step(self.plan.fast and self.plan.one, *others)

    def second(self, *others):
        self.step(self.plan.fast and self.plan.two, *others)

    def third(self, *others):
        self.second_came = self.landed()
        self.step(self.plan.fast and self.plan.next_to, *others)

    def fourth(self, *others):
        self.third_came = self.landed()
        self.step(self.plan.fast and self.plan.across, *others)

    def finish(self, *others):
        if self.plan.fast:
            self.terms.append(after(self.came, *others) if others else self.came)
            self.sum = self.total(0, 1)[0]

    def result(self):
        if self.plan.fast:
            cuts = np.cumsum([rows for _, rows in self.names])[:-1]
            return {n: v for (n, _), v in zip(self.names, jnp.split(self.sum, cuts, 0))}
        got = {}
        for (n, _), g in zip(self.names, self.whole):
            half = lax.psum_scatter(g, "dp", scatter_dimension=0, tiled=True)
            got[n] = lax.psum_scatter(half, "fsdp", scatter_dimension=1, tiled=True).astype(F32)
        return got


def local(
    plan,
    alignment_input,
    sequence_mask,
    column_length,
    output_cotangent,
    row_projection_weight,
    row_out_weight,
    column_projection_weight,
    column_out_weight,
    feedforward_in_weight,
    feedforward_out_weight,
    layer_norm_gain,
    layer_norm_bias,
):
    width = alignment_input.shape[3]
    tokens = alignment_input.shape[1] * alignment_input.shape[2]
    heads = width // HD
    hidden = feedforward_out_weight.shape[0] * plan.dp
    x = alignment_input.reshape(tokens, width)
    cot = output_cotangent.reshape(tokens, width)
    shards = dict(
        row_qkv=row_projection_weight.T,
        row_out=row_out_weight,
        col_qkv=column_projection_weight.T,
        col_out=column_out_weight,
        ffn_in=feedforward_in_weight.T,
        ffn_out=feedforward_out_weight,
    )
    whole_rows = {k: v.shape[0] * plan.dp for k, v in shards.items()}
    norms = jnp.concatenate([layer_norm_gain, layer_norm_bias], 0)
    share = norms.shape[1]
    devices = plan.dp * plan.fsdp
    me = lax.axis_index(AXES)
    n_seq = jnp.sum((sequence_mask > 0).astype(jnp.int32))
    n_col = column_length[0].astype(jnp.int32)
    ints = jnp.stack([n_seq, n_col])
    row_scale = 0.125 * lax.rsqrt(n_seq.astype(F32))

    w = {}
    if plan.fast:
        gather_row, early_row = (
            lax.dynamic_index_in_dim(jnp.asarray(t), me, 0, False) for t in plan.gather_tables
        )
        owner_row, first_row = (
            lax.dynamic_index_in_dim(jnp.asarray(t), me, 0, False) for t in plan.owner_tables
        )
        tables = [gather_row, owner_row, early_row]
        own_tables = dict(colg=[gather_row, first_row, early_row])
        extra = jnp.concatenate([norms.reshape(-1), n_col.astype(BF16)[None]])
        cols = shards["row_out"].shape[1]
        extra = jnp.pad(extra[None], ((0, 15), (0, cols - extra.shape[0])))
        groups = (("row_qkv",), ("row_out", "col_qkv"), ("col_out", "ffn_in"), ("ffn_out",))
        packs = []
        for gi, names in enumerate(groups):
            parts = [shards[n] for n in names] + ([extra] if gi == 0 else [])
            packs.append(jnp.concatenate(parts, 0) if len(parts) > 1 else parts[0])
        def ready(gi, bufs):
            row0 = 0
            for n in groups[gi]:
                rows = shards[n].shape[0]
                w[n] = Weights(bufs, row0, rows, whole_rows[n], width, True, 2 if gi == 3 else 0)
                row0 += rows
            return bufs

        late = []
        g1, g2, g3, g4 = (Gathering(plan, p) for p in packs)
        g1.step(plan.across)
        g4.step(plan.one)
        t = [g1.step(plan.next_to, g4.came, ints, *tables, first_row)]
        t = [g1.step(plan.one), g2.step(plan.across, *t)]
        t = [g1.far(*t), g2.step(plan.next_to, *t), g3.step(plan.across, *t)]
        g1.share(*t)
        bufs = ready(0, g1.last(*t))
        t = [g2.step(plan.one, *t), g3.step(plan.next_to, *t), g1.mate, g1.end]
        early = dict(rowf=t)
        slot = [g2.far(*t), g2.share(*t), g3.step(plan.one, *t), g4.step(plan.across, *t)]
        early["colf"] = slot

        def after_rowf(token):
            ready(1, g2.last(token, *slot))
            t = [token, *slot, g2.end]
            early["ffnf"] = [g3.far(*t), g3.share(*t), g4.step(plan.next_to, *t)]

        def after_colf(token):
            t = [token, *early["ffnf"]]
            ready(2, g3.last(*t))
            t = [token, g3.end]
            early["fout"] = [g4.far(*t), g4.share(*t)]

        hooks = dict(
            rowf=lambda outs: after_rowf(outs[5]),
            colf=lambda outs: after_colf(outs[1]),
            ffnf=lambda outs: late.append(ready(3, g4.last(outs[1], *early["fout"]))[3]),
        )
        rows = shards["row_qkv"].shape[0]
        w["norms"] = Weights(bufs, rows, 16, 16 * plan.dp, width, True)
        w["norms"].raw = True
    else:
        tables, own_tables = [jnp.zeros((1,), jnp.int32)] * 3, {}
        early, hooks, late = {}, {}, []
        for n, s in shards.items():
            half = lax.all_gather(s, "fsdp", axis=1, tiled=True)
            full = lax.all_gather(half, "dp", axis=0, tiled=True)
            w[n] = Weights([full], 0, s.shape[0], whole_rows[n], width, False)
        gb = lax.all_gather(norms, "fsdp", axis=1, tiled=True)
        gb = lax.all_gather(gb, "dp", axis=1, tiled=True).astype(F32)
        count = jnp.full((1, width), lax.psum(n_col.astype(F32), AXES))
        gb = jnp.concatenate([gb, count, jnp.zeros_like(count)], 0)
    flts = row_scale[None]

    micros = dict(
        rowf=9,
        colf=8,
        cola=4,
        ffnf=12,
        fout=7,
        ffnb=12,
        colb=10,
        colt=7,
        colg=7,
        rowb=10,
        rowt=13,
        inpb=9,
        lout=9,
    )

    def arr(n, dtype, rows=tokens, vmem=True, hbm=False):
        return Out((rows, n), dtype, vmem, hbm)

    resident = {}

    def run(name, body, smem, ins, weights, outs, grads=(), scratch=(), deps=(), fetch=()):
        ins = [a.bufs[0] if isinstance(a, Weights) else a for a in ins]
        weights = [w[n] if isinstance(n, str) else n for n in weights]
        fetch = [w[a] if isinstance(a, str) else Weights.of(a) for a in fetch]
        lists = own_tables.get(name, tables) + list(smem), ins, weights, outs, grads
        deps = list(deps) + early.get(name, [])
        got = fused(name, body, *lists, plan, resident, micros[name], scratch, deps, fetch)
        if name in hooks:
            hooks[name](got[0])
        return got

    wide = pltpu.VMEM((tokens, width), F32)
    turn = pltpu.VMEM((width // 128, 32 * PITCH + 8, 128), F32)
    score = pltpu.VMEM((heads * 32, 128), F32)
    flat = pltpu.VMEM((tokens // 4, 2 * width), F32)
    moment = arr(width, F32, 8, False, True)
    keep = dict(vmem=False, hbm=True)
    token = arr(128, F32, 8, **keep)

    (normed_row, packed_row, mixed_row, prob, logp, ent, gb), _ = run(
        "rowf",
        row_forward,
        [ints, flts],
        [x] if plan.fast else [x, gb],
        ["norms", "row_qkv"] if plan.fast else ["row_qkv"],
        [
            arr(width, BF16, **keep),
            arr(3 * width, BF16, **keep),
            arr(width, BF16, hbm=True),
            arr(128, F32, heads * 32, **keep),
            arr(128, F32, heads * 32, **keep),
            arr(width, F32, 8, **keep),
            arr(width, F32, 8, **keep),
        ],
        (),
        [score],
    )
    (after_row, normed_col, packed_col, mixed_col), _ = run(
        "colf",
        column_all,
        [ints],
        [x, mixed_row[0], gb],
        ["row_out", "col_qkv"],
        [
            arr(width, F32, hbm=True),
            arr(width, BF16, **keep),
            arr(3 * width, BF16, **keep),
            arr(width, BF16, hbm=True),
        ],
        (),
        [turn, flat],
    )
    (after_col, normed_ffn, active, slope, cot_here), _ = run(
        "ffnf",
        feed_forward,
        [],
        [after_row[0], mixed_col[0], gb],
        ["col_out", "ffn_in"],
        [
            arr(width, F32, **keep),
            arr(width, BF16, **keep),
            arr(hidden, BF16, hbm=True),
            arr(hidden, BF16),
        ],
        fetch=[cot],
    )
    (g3,), grads = run(
        "fout",
        ffn_out_grad,
        [ints],
        [active[0], cot_here],
        [],
        [arr(width, BF16)],
        [hidden],
        [turn],
    )
    r1 = Reduction(plan, grads, ["ffn_out"], shards)
    r1.core(*late)
    (grad_hidden, w_in, w_col_out, after_here), grads = run(
        "ffnb",
        ffn_back,
        [],
        [g3, slope, normed_ffn],
        ["ffn_out"],
        [arr(hidden, BF16)],
        [hidden],
        fetch=["ffn_in", "col_out", after_col],
    )
    r2 = Reduction(plan, grads, ["ffn_in"], shards)
    landed = r1.landed()
    r1.first(grads[0], *landed)
    r2.core(*landed)
    (grad_after, g2, gm_col, sums_two, packed_here, normed_here, mixed_here), _ = run(
        "colb",
        column_back,
        [],
        [grad_hidden, after_here, g3, gb],
        [w_in, w_col_out],
        [arr(width, F32, **keep), arr(width, BF16), arr(width, BF16), moment],
        (),
        [wide],
        landed,
        [packed_col, normed_col, mixed_col[1]],
    )
    landed = r1.landed() + r2.landed()
    r1.second(sums_two, *landed)
    r2.first(sums_two, *landed)
    (gq_col, layer_out, mark), _ = run(
        "colt",
        column_back_and_result,
        [ints],
        [packed_here, gm_col, active[1], after_col],
        ["ffn_out"],
        [arr(3 * width, BF16), arr(width, BF16, **keep), token],
        (),
        [flat, flat, turn],
        landed,
    )
    landed = r1.landed() + r2.landed()
    r1.third(mark, *landed)
    r2.second(mark, *landed)
    (w_col_qkv, w_row_out, after_row_here, grad_after_here), grads = run(
        "colg",
        product_grads,
        [],
        [gq_col, normed_here, mixed_here, g2],
        [],
        [],
        [3 * width, width],
        (),
        landed,
        ["col_qkv", "row_out", after_row[1], grad_after],
    )
    r3 = Reduction(plan, grads, ["col_qkv", "col_out"], shards)
    landed = r1.landed() + r2.landed()
    r1.fourth(grads[0], *landed)
    r2.third(grads[0], *landed)
    r3.core(*landed)
    (grad_row, g1, gm_row, sums_one, packed_here, normed_here, mixed_here), _ = run(
        "rowb",
        row_back,
        [],
        [gq_col, after_row_here, grad_after_here, gb],
        [w_col_qkv, w_row_out],
        [arr(width, F32, **keep), arr(width, BF16), arr(width, BF16), moment],
        (),
        [wide, turn],
        landed,
        [packed_row, normed_row, mixed_row[1]],
    )
    landed = r1.landed() + r2.landed() + r3.landed()
    r2.fourth(sums_one, *landed)
    r3.first(sums_one, *landed)
    (gq_row,), grads = run(
        "rowt",
        row_attend_back,
        [ints, flts],
        [packed_here, gm_row, prob, logp, mixed_here, g1, normed_here, gb],
        [],
        [arr(3 * width, BF16, **keep)],
        [width, 3 * width],
        [score],
        landed,
    )
    r4 = Reduction(plan, grads, ["row_out", "row_qkv"], shards)
    landed = r1.landed() + r2.landed() + r3.landed()
    r4.core(*landed)
    landed = landed + r4.landed()
    r1.finish()
    r2.finish()
    sums = [r.sum for r in (r1, r2)] if plan.fast else []
    r3.third(grads[0], *landed)
    r4.first(*landed, *sums)
    (grad_in, sums_zero), _ = run(
        "inpb",
        input_back,
        [],
        [gq_row, x, grad_row, gb],
        ["row_qkv"],
        [arr(width, F32, **keep), moment],
        (),
        [wide],
        [grads[0], *landed],
    )
    landed = r3.landed() + r4.landed()
    r4.second(sums_zero, *landed)
    r3.fourth(sums_zero, *landed)
    r4.third()
    landed = r4.landed()
    r3.second(*landed)
    r4.fourth()
    r3.finish()
    r4.finish(*([r3.sum] if plan.fast else []))
    got = {}
    for r in (r1, r2, r3, r4):
        got.update(r.result())
    sums_all = plan.everywhere(sums_zero + sums_one + sums_two + ent, r4)
    owned = lax.dynamic_slice_in_dim(sums_all[:6], me * share, share, 1)
    gains, biases = owned[0::2], owned[1::2]
    shape = alignment_input.shape
    return (
        layer_out.reshape(shape),
        grad_in.reshape(shape),
        got["row_qkv"].T,
        got["row_out"],
        got["col_qkv"].T,
        got["col_out"],
        got["ffn_in"].T,
        got["ffn_out"],
        gains,
        biases[:2],
        biases[2],
        sums_all[6, 0],
    )


def solution(mesh):
    def whole(*args):
        plan = Plan(mesh.shape["dp"], mesh.shape["fsdp"], args[0].shape[3])
        return jax.shard_map(
            lambda *blocks: local(plan, *blocks),
            mesh=mesh,
            in_specs=(
                P(AXES, None, None, None),
                P(AXES, None),
                P(AXES),
                P(AXES, None, None, None),
                P("fsdp", "dp"),
                P("dp", "fsdp"),
                P("fsdp", "dp"),
                P("dp", "fsdp"),
                P("fsdp", "dp"),
                P("dp", "fsdp"),
                P(None, AXES),
                P(None, AXES),
            ),
            out_specs=(
                P(AXES, None, None, None),
                P(AXES, None, None, None),
                P("fsdp", "dp"),
                P("dp", "fsdp"),
                P("fsdp", "dp"),
                P("dp", "fsdp"),
                P("fsdp", "dp"),
                P("dp", "fsdp"),
                P(None, AXES),
                P(None, AXES),
                P(AXES),
                P(),
            ),
            check_vma=False,
        )(*args)

    return whole
```

```python
import jax
import jax.numpy as jnp
import numpy as np
from jax import lax
from jax.experimental import pallas as pl
from jax.experimental.pallas import tpu as pltpu
from jax.sharding import PartitionSpec as P

HD = 64
AXES = ("dp", "fsdp")
norm_eps = 1e-05
penalty_weight = 1.0
masked_score = -1000000000.0
never = -1e30

F32 = jnp.float32
BF16 = jnp.bfloat16
MIB = 1 << 20
PITCH = 33


def dot(a, b, ca, cb):
    return lax.dot_general(a, b, (((ca,), (cb,)), ((), ())), preferred_element_type=F32)


class Weights:
    def __init__(self, bufs, row0, rows, whole_rows, width, blocked, table=0):
        self.raw = self.here = False
        self.dtype = BF16
        self.bufs, self.row0, self.rows, self.table = bufs, row0, rows, table
        self.whole_rows, self.width, self.blocked = whole_rows, width, blocked


    @staticmethod
    def of(a):
        w = Weights([a], 0, a.shape[0], a.shape[0], a.shape[1], False)
        w.dtype = a.dtype
        return w

    @staticmethod
    def held(a):
        w = Weights.of(a)
        w.here = True
        return w

    def copies(self, plan):
        if self.here:
            return 0
        return sum(b.shape[0] for b in self.bufs) if self.blocked else 1


class Loaded:
    def __init__(self, ref, copies):
        self.ref, self.copies = ref, copies

    def start(self, part=None):
        for c in self.copies if part is None else self.copies[part : part + 1]:
            c.start()

    def wait(self):
        for c in self.copies:
            c.wait()
        return self.ref


class Out:
    def __init__(self, shape, dtype, vmem=True, hbm=False):
        self.shape, self.dtype, self.vmem, self.hbm = shape, dtype, vmem, hbm
        self.parts = max(1, shape[1] // 768) if hbm else 0


def fused(
    name, body, smem, ins, weights, outs, grads, plan, resident, micros, scratch=(), deps=(), fetch=()
):
    arrays, index, spaces = [], {}, []

    def slot(a):
        if id(a) not in index:
            index[id(a)] = len(arrays)
            stays = id(a) in resident
            spaces.append(pltpu.VMEM if stays else pltpu.HBM)
            arrays.append(pltpu.with_memory_space_constraint(a, spaces[-1]))
        return index[id(a)]

    in_slots = [slot(a) for a in ins]
    w_slots = [[slot(b) for b in w.bufs] for w in (*weights, *fetch)]
    weights = list(weights)
    n_weights = len(weights)
    for a in deps:
        arrays.append(a)
        spaces.append(pl.ANY)
    n_smem = len(smem)
    vm, n_sem = [], 0
    for a in ins:
        if id(a) not in resident:
            vm.append(pltpu.VMEM(a.shape, a.dtype))
            n_sem += 1
    for w in (*weights, *fetch):
        n_sem += w.copies(plan)
    for w in weights:
        if w.here:
            continue
        raw = (w.whole_rows // w.rows * plan.fsdp, w.rows, w.width // plan.fsdp)
        vm.append(pltpu.VMEM(raw if w.raw else (w.whole_rows, w.width), BF16))
    out_shapes, out_spaces = [], []
    for o in outs:
        if o.vmem:
            out_shapes.append(pltpu.VMEM(o.shape, o.dtype))
            out_spaces.append(pltpu.VMEM)
        else:
            vm.append(pltpu.VMEM(o.shape, o.dtype))
        if o.hbm:
            out_shapes.append(pltpu.HBM(o.shape, o.dtype))
            out_spaces.append(pltpu.HBM)
            n_sem += o.parts
    f_at = len(out_shapes)
    for w in fetch:
        out_shapes.append(pltpu.VMEM((w.whole_rows, w.width), w.dtype))
        out_spaces.append(pltpu.VMEM)
    g_at = len(out_shapes)
    width = plan.width
    for rows in grads:
        vm.append(pltpu.VMEM((rows, width), BF16))
        n_sem += plan.dp * plan.fsdp if plan.fast else 1
    if grads and plan.fast:
        per = sum(rows // plan.dp for rows in grads)
        shape = pltpu.HBM((plan.slots, per, width // plan.fsdp), BF16)
        out_shapes += [shape, shape]
    elif grads:
        out_shapes += [pltpu.HBM((rows, width), BF16) for rows in grads]
    out_spaces += [pltpu.HBM] * (len(out_shapes) - g_at)
    n_in, n_out, n_vm = len(arrays), len(out_shapes), len(vm)
    used_vmem = sum(int(np.prod(m.shape)) * np.dtype(m.dtype).itemsize for m in (*vm, *scratch))

    def kernel(*refs):
        sm = refs[:n_smem]
        hb = refs[n_smem : n_smem + n_in]
        ob = refs[n_smem + n_in : n_smem + n_in + n_out]
        rest = refs[n_smem + n_in + n_out :]
        vrefs, extra, sems = list(rest[:n_vm]), rest[n_vm:-1], rest[-1]
        used = [0]

        def sem():
            used[0] += 1
            return sems.at[used[0] - 1]

        loads = Loads()
        for a, s in zip(ins, in_slots):
            if id(a) in resident:
                loads.append(Loaded(hb[s], []))
            else:
                ref = vrefs.pop(0)
                loads.append(Loaded(ref, [pltpu.make_async_copy(hb[s], ref, sem())]))
        wl = []
        for n, (w, slots) in enumerate(zip((*weights, *fetch), w_slots)):
            copies = []
            if w.here:
                dst = hb[slots[0]]
            elif n < n_weights:
                dst = vrefs.pop(0)
            else:
                dst = ob[f_at + n - n_weights]
            if w.here:
                pass
            elif w.blocked:
                cols = w.width // plan.fsdp
                count = 0
                for s in slots:
                    for j in range(arrays[s].shape[0]):
                        block = sm[w.table][count] if w.table is not None else count
                        count += 1
                        row = (block // plan.fsdp) * w.rows
                        col = (block % plan.fsdp) * cols
                        if w.table is not None:
                            row, col = pl.multiple_of(row, 16), pl.multiple_of(col, 128)
                        spot = dst.at[pl.ds(row, w.rows), pl.ds(col, cols)]
                        if w.raw:
                            spot = dst.at[count - 1]
                        src = hb[s].at[j, pl.ds(w.row0, w.rows), :]
                        copies.append(pltpu.make_async_copy(src, spot, sem()))
            else:
                copies.append(pltpu.make_async_copy(hb[slots[0]], dst, sem()))
            (wl if n < n_weights else loads.fetched).append(Loaded(dst, copies))
        ol = []
        at = 0
        for o in outs:
            if o.vmem:
                ref = ob[at]
                at += 1
            else:
                ref = vrefs.pop(0)
            copies = []
            if o.hbm:
                for k in range(o.parts):
                    lanes = slice(None)
                    if o.parts > 1:
                        lanes = pl.ds(k * 768, 768)
                    copies.append(
                        pltpu.make_async_copy(ref.at[:, lanes], ob[at].at[:, lanes], sem())
                    )
                at += 1
            ol.append(Loaded(ref, copies))
        gl = []
        row0 = 0
        for k, rows in enumerate(grads):
            src = vrefs.pop(0)
            if plan.fast:
                gl.append(Blocks(src, ob[g_at], ob[g_at + 1], sm[1], plan, rows, row0, sem))
                row0 += rows // plan.dp
            else:
                gl.append(Loaded(src, [pltpu.make_async_copy(src, ob[g_at + k], sem())]))
        for l in (*loads[:1], *wl[:1], *loads[1:], *wl[1:]):
            l.start()
        body(sm[:1] + sm[3:] if name == "rowf" else sm[3:], loads, wl, ol, gl, extra)
        for l in (*ol, *gl, *loads.fetched):
            l.wait()

    res = pl.pallas_call(
        kernel,
        name=name,
        out_shape=out_shapes,
        in_specs=[pl.BlockSpec(memory_space=pltpu.SMEM)] * n_smem
        + [pl.BlockSpec(memory_space=m) for m in spaces],
        out_specs=[pl.BlockSpec(memory_space=m) for m in out_spaces],
        scratch_shapes=vm + list(scratch) + [pltpu.SemaphoreType.DMA((n_sem,))],
        compiler_params=pltpu.CompilerParams(vmem_limit_bytes=used_vmem + 7 * MIB),
        cost_estimate=pl.CostEstimate(
            flops=int(micros * 1e6), bytes_accessed=int(micros * 3e3), transcendentals=0
        ),
    )(*smem, *arrays)
    got, at = [], 0
    for o in outs:
        both = res[at : at + o.vmem + o.hbm]
        at += o.vmem + o.hbm
        if o.vmem:
            resident[id(both[0])] = both[0]
        got.append(both[0] if len(both) == 1 else both)
    for a in res[f_at:g_at]:
        resident[id(a)] = a
        got.append(Weights.held(a))
    return got, res[g_at:]


class Loads(list):
    def __init__(self):
        self.fetched = []

    def later(self):
        for l in self.fetched:
            l.start()


class Blocks:
    def __init__(self, ref, kept, sent, table, plan, rows, row0, sem):
        self.ref, self.plan = ref, plan
        self.per, self.cols = rows // plan.dp, plan.width // plan.fsdp
        self.kept, self.sent, self.table, self.row0 = kept, sent, table, row0
        self.sems = [sem() for _ in range(plan.dp * plan.fsdp)]
        self.begun = 0

    def copy(self, n, out, slot):
        row, col = (n // self.plan.fsdp) * self.per, (n % self.plan.fsdp) * self.cols
        return pltpu.make_async_copy(
            self.ref.at[row : row + self.per, col : col + self.cols],
            out.at[slot, pl.ds(self.row0, self.per), :],
            self.sems[n],
        )

    def start(self, rows=None):
        rows = self.ref.shape[0] if rows is None else rows
        end = rows // self.per * self.plan.fsdp
        slots = self.plan.slots
        for n in range(self.begun, end):
            place = self.table[n]

            @pl.when(place < slots)
            def _():
                self.copy(n, self.kept, place).start()

            @pl.when(place >= slots)
            def _():
                self.copy(n, self.sent, place - slots).start()

        self.begun = end

    def wait(self):
        for n in range(self.begun):
            self.copy(n, self.kept, 0).wait()


def stamp(out):
    out.ref[...] = jnp.zeros(out.ref.shape, out.ref.dtype)
    out.start()


def normal_form(v):
    centred = v - jnp.mean(v, -1, keepdims=True)
    rstd = lax.rsqrt(jnp.mean(centred * centred, -1, keepdims=True) + norm_eps)
    return centred * rstd, rstd


def norm_rows(src, dst, gb, k, total):
    for t in range(0, total, 256):
        xhat, _ = normal_form(src[t : t + 256, :].astype(F32))
        dst[t : t + 256, :] = (xhat * gb[k : k + 1, :] + gb[k + 3 : k + 4, :]).astype(BF16)


def norm_back(dn_ref, src, base, gb, k, total, emit, sums):
    gain = gb[k : k + 1, :]
    gain_sum = jnp.zeros_like(gain)
    bias_sum = jnp.zeros_like(gain)
    for t in range(0, total, 256):
        xhat, rstd = normal_form(src[t : t + 256, :].astype(F32))
        dn = dn_ref[t : t + 256, :]
        gain_sum = gain_sum + jnp.sum(dn * xhat, 0, keepdims=True)
        bias_sum = bias_sum + jnp.sum(dn, 0, keepdims=True)
        dx = dn * gain
        low = jnp.mean(dx, -1, keepdims=True)
        mix = jnp.mean(dx * xhat, -1, keepdims=True)
        emit(t, base[t : t + 256, :].astype(F32) + rstd * (dx - low - xhat * mix))
    none = jnp.zeros((1, gain.shape[1]), F32)
    rows = [none] * (2 * k) + [gain_sum, bias_sum] + [none] * (6 - 2 * k)
    sums[...] = jnp.concatenate(rows, 0)


def head_masks(lanes):
    lane = lax.broadcasted_iota(jnp.int32, (1, lanes), 1)
    low = ((lane // HD) % 2 == 0).astype(F32)
    return low.astype(BF16), (1.0 - low).astype(BF16)


def four(ref, col):
    return jnp.concatenate([ref[g * 256 : (g + 1) * 256, col : col + 128] for g in range(4)], 1)


def pick(big):
    seg = lax.broadcasted_iota(jnp.int32, (32, 256), 1) // 32
    out = big[:32, :]
    for k in range(1, 8):
        out = jnp.where(seg == k, big[k * 32 : (k + 1) * 32, :], out)
    out = out[:, :128] + out[:, 128:]
    out = out + pltpu.roll(out, 64, 1)
    return out + pltpu.roll(out, 32, 1)


def spread(small):
    seg = lax.broadcasted_iota(jnp.int32, (32, 256), 1) // 32
    wide = jnp.concatenate([small, small], 1)
    return jnp.concatenate([jnp.where(seg == k, wide, 0.0).astype(BF16) for k in range(8)], 0)


def gathered_norms(blocks, table):
    slots = blocks.shape[0]
    values = jnp.sum(blocks[...].astype(F32), 1).astype(BF16)
    place = lax.broadcasted_iota(jnp.int32, (slots, 1), 0)
    owner = jnp.zeros((slots, 1), jnp.int32)
    for j in range(slots):
        owner = jnp.where(place == j, table[j], owner)
    share = 768 // slots
    lane = lax.broadcasted_iota(jnp.int32, (1, 768), 1)
    row = lax.broadcasted_iota(jnp.int32, (values.shape[1], 1), 0)
    mine = lane // share == owner
    rows = []
    for k in range(6):
        spot = (row == k * share + lane % share).astype(F32).astype(BF16)
        rows.append(jnp.sum(jnp.where(mine, dot(values, spot, 1, 0), 0.0), 0, keepdims=True))
    count = jnp.where(lax.broadcasted_iota(jnp.int32, (1, values.shape[1]), 1) == 6 * share, 1.0, 0.0)
    total = jnp.sum(values.astype(F32) * count)
    rows.append(jnp.full((1, 768), total, F32))
    rows.append(jnp.zeros((1, 768), F32))
    return jnp.concatenate(rows, 0)


def row_forward(sm, I, W, O, G, X):
    ints, flts = sm[-2:]
    x = I[0]
    normed, packed, mixed, prob, logp, ent, norms = O
    sc = X[0]
    if len(W) > 1:
        norms.ref[...] = gathered_norms(W[0].wait(), sm[0])
    else:
        norms.ref[...] = I[1].wait()[...]
    norms.start()
    xr, g = x.wait(), norms.ref
    norm_rows(xr, normed.ref, g, 0, 1024)
    normed.start()
    wt = W[-1].wait()
    nr = normed.ref[...]
    n_seq, n_col = ints[0], ints[1]
    keep = (lax.broadcasted_iota(jnp.int32, (1024, 1), 0) // 32 < n_seq).astype(F32)
    width = nr.shape[1]
    heads = width // HD
    pr = packed.ref
    for n in range(0, 3 * width, 256):
        out = dot(nr, wt[n : n + 256, :], 1, 1)
        if n < width:
            out = out * keep
        pr[:, n : n + 256] = out.astype(BF16)
        if (n + 256) % 768 == 0:
            packed.start(n // 768)
    halves = head_masks(512)
    for m in range(heads // 2):
        q, k = four(pr, m * 128), four(pr, width + m * 128)
        for e in range(2):
            h = 2 * m + e
            sc[h * 32 : (h + 1) * 32, :] = pick(dot(q * halves[e], k, 1, 1))
    lane = lax.broadcasted_iota(jnp.int32, (1, 128), 1) % 32
    s = jnp.where(lane < n_col, sc[...] * flts[0], masked_score)
    top = jnp.max(s, -1, keepdims=True)
    total = jnp.sum(jnp.exp(s - top), -1, keepdims=True) * 0.25
    lp = s - (top + jnp.log(total))
    p = jnp.exp(lp)
    prob.ref[...] = p
    logp.ref[...] = lp
    prob.start()
    logp.start()
    entropy = jnp.sum(p * lp, -1, keepdims=True) * -0.25
    row = lax.broadcasted_iota(jnp.int32, entropy.shape, 0) % 32
    total = jnp.sum(jnp.where(row < n_col, entropy, 0.0))
    share = total / norms.ref[6:7, :]
    ent.ref[...] = jnp.where(lax.broadcasted_iota(jnp.int32, ent.ref.shape, 0) == 6, share, 0.0)
    ent.start()
    second = (lax.broadcasted_iota(jnp.int32, (1, 512), 1) // HD) % 2 == 1
    for m in range(heads // 2):
        v = four(pr, 2 * width + m * 128)
        both = [
            dot(spread(prob.ref[h * 32 : (h + 1) * 32, :]), v, 1, 0) for h in (2 * m, 2 * m + 1)
        ]
        out = jnp.where(second, both[1], both[0]).astype(BF16)
        for t in range(4):
            mixed.ref[t * 256 : (t + 1) * 256, m * 128 : (m + 1) * 128] = out[
                :, t * 128 : (t + 1) * 128
            ]
    mixed.start()


def stacked(x, halves):
    return jnp.concatenate([x * halves[0], x * halves[1]], 0)


def segment(rows):
    return (lax.broadcasted_iota(jnp.int32, (rows, 256), 1) // 32) % 4


def pick_four(big):
    seg = segment(32)
    out = big[:32, :]
    for k in range(1, 4):
        out = jnp.where(seg == k, big[k * 32 : (k + 1) * 32, :], out)
    return out


def spread_four(small):
    seg = segment(32)
    return jnp.concatenate([jnp.where(seg == k, small, 0.0).astype(BF16) for k in range(4)], 0)


def unstack(both):
    lane = lax.broadcasted_iota(jnp.int32, (128, 128), 1)
    return jnp.where(lane < HD, both[:128], both[128:])


def to_columns(src, take):
    for t in range(0, 1024, 256):
        lanes = [
            jnp.concatenate([src[j, pl.ds(t // 32 + k, 32, stride=PITCH), :] for k in range(8)], 0)
            for j in range(src.shape[0])
        ]
        take(t, jnp.concatenate(lanes, 1))


def put(dst, start, n, value):
    for r in range(value.shape[0] // 32):
        at = (start // 32 + r) * PITCH
        for j in range(value.shape[1] // 128):
            piece = value[r * 32 : (r + 1) * 32, j * 128 : (j + 1) * 128]
            dst[n // 128 + j, at : at + 32, :] = piece


def column_forward(sm, I, W, O, G, X):
    x, mixed_row, gb = I
    after, normed, packed = O
    (ar,) = X
    width = normed.ref.shape[1]
    mr, xr = mixed_row.wait(), x.wait()
    wo = W[0].wait()
    for n in range(0, width, 256):
        out = xr[:, n : n + 256].astype(F32) + dot(mr[...], wo[:, n : n + 256], 1, 0)
        put(ar, 0, n, out)
    g = gb.wait()

    def take(t, rows):
        after.ref[t : t + 256, :] = rows

    to_columns(ar, take)
    after.start()
    norm_rows(after.ref, normed.ref, g, 1, 1024)
    normed.start()
    wt = W[1].wait()
    nr = normed.ref[...]
    pr = packed.ref
    for n in range(0, 3 * width, 256):
        pr[:, n : n + 256] = dot(nr, wt[n : n + 256, :], 1, 1).astype(BF16)
        if (n + 256) % 768 == 0:
            packed.start(n // 768)


def column_softmax(sc, n_seq):
    def block(b, carry):
        at = pl.ds(pl.multiple_of(b * 32, 32), 32)
        s = sc[at, :]
        s = jnp.where(lax.broadcasted_iota(jnp.int32, s.shape, 0) < n_seq, s, never)
        p = jnp.exp(s - jnp.max(s, 0, keepdims=True))
        sc[at, :] = p * (1.0 / jnp.sum(p, 0, keepdims=True))
        return carry

    lax.fori_loop(0, sc.shape[0] // 32, block, 0)


def column_attend(sm, I, W, O, G, X):
    (ints,) = sm
    (mixed,) = O
    (sc,) = X
    width = mixed.ref.shape[1]
    pr = I[0].wait()
    halves = head_masks(128)

    def scores(b, carry):
        rows = pl.ds(pl.multiple_of(b * 128, 128), 128)
        at = pl.ds(pl.multiple_of(b * 32, 32), 32)
        for lo in range(0, width, 128):
            qs = stacked(pr[rows, lo : lo + 128] * 0.125, halves)
            k = pr[rows, width + lo : width + lo + 128]
            sc[at, 2 * lo : 2 * lo + 256] = pick_four(dot(k, qs, 1, 1))
        return carry

    lax.fori_loop(0, 8, scores, 0)
    column_softmax(sc, ints[0])

    def mix(b, carry):
        rows = pl.ds(pl.multiple_of(b * 128, 128), 128)
        at = pl.ds(pl.multiple_of(b * 32, 32), 32)
        for lo in range(0, width, 128):
            v = pr[rows, 2 * width + lo : 2 * width + lo + 128]
            p = spread_four(sc[at, 2 * lo : 2 * lo + 256])
            mixed.ref[rows, lo : lo + 128] = unstack(dot(p, v, 0, 0)).astype(BF16)
        return carry

    lax.fori_loop(0, 8, mix, 0)
    mixed.start()


def column_all(sm, I, W, O, G, X):
    column_forward((), I, W, O[:3], G, X[:1])
    column_attend(sm, [Loaded(O[2].ref, [])], W, O[3:], G, X[1:])


def feed_forward(sm, I, W, O, G, X):
    after_row, mixed, gb = I
    after, normed, active, slope = O
    width = normed.ref.shape[1]
    hidden = active.ref.shape[1]
    ar, mr = after_row.wait(), mixed.wait()
    wo = W[0].wait()
    for n in range(0, width, 256):
        after.ref[:, n : n + 256] = ar[:, n : n + 256] + dot(mr[...], wo[:, n : n + 256], 1, 0)
    after.start()
    norm_rows(after.ref, normed.ref, gb.wait(), 2, 1024)
    normed.start()
    wt = W[1].wait()
    I.later()
    nr = normed.ref[...]
    for n in range(0, hidden, 256):
        h = dot(nr, wt[n : n + 256, :], 1, 1)
        cdf = 0.5 + 0.5 * lax.erf(h * (0.5**0.5))
        active.ref[:, n : n + 256] = (h * cdf).astype(BF16)
        bell = jnp.exp(h * h * -0.5) * (0.5 / np.pi) ** 0.5
        slope.ref[:, n : n + 256] = (cdf + h * bell).astype(BF16)
        if (n + 256) % 768 == 0:
            active.start(n // 768)
    slope.start()


def weight_grad(dst, left, right, step=768):
    rows = dst.ref.shape[0]
    blocks = isinstance(dst, Blocks)
    for n in range(0, rows, step):
        dst.ref[n : n + step, :] = dot(left[:, n : n + step], right[...], 0, 0).astype(BF16)
        if blocks:
            dst.start(n + step)
    if not blocks:
        dst.start()


def ffn_out_grad(sm, I, W, O, G, X):
    (ints,) = sm
    active, cot = I
    (g3,) = O
    (wide,) = X
    put(wide, 0, 0, cot.wait()[...].astype(F32))
    n_seq, n_col = ints[0], ints[1]

    def take(t, rows):
        at = lax.broadcasted_iota(jnp.int32, (256, 1), 0) + t
        keep = ((at % 32 < n_seq) & (at // 32 < n_col)).astype(F32)
        g3.ref[t : t + 256, :] = (rows * keep).astype(BF16)

    to_columns(wide, take)
    g3.start()
    weight_grad(G[0], active.wait(), g3.ref)


def ffn_back(sm, I, W, O, G, X):
    g3, slope, normed = I
    (grad_hidden,) = O
    wf = W[0].wait()
    gr, sl = g3.wait(), slope.wait()
    I.later()
    gh = grad_hidden.ref
    hidden = gh.shape[1]
    gv = gr[...]
    for n in range(0, hidden, 256):
        d = dot(gv, wf[n : n + 256, :], 1, 1)
        gh[:, n : n + 256] = (d * sl[:, n : n + 256].astype(F32)).astype(BF16)
    grad_hidden.start()
    weight_grad(G[0], gh, normed.wait())


def ffn_result(sm, I, W, O, G, X):
    active, after = I
    layer_out = O[0]
    (res,) = X
    width = layer_out.ref.shape[1]
    wf = W[0].wait()
    ac, ar = active.wait(), after.wait()
    I.later()
    for n in range(0, width, 256):
        put(res, 0, n, ar[:, n : n + 256] + dot(ac[...], wf[:, n : n + 256], 1, 0))

    def take(t, rows):
        layer_out.ref[t : t + 256, :] = rows.astype(BF16)

    to_columns(res, take)
    layer_out.start()
    stamp(O[1])


def column_back(sm, I, W, O, G, X):
    grad_hidden, after_col, g3, gb = I
    grad_after, branch, grad_mixed, sums = O
    (dn,) = X
    g2, gm = branch.ref, grad_mixed.ref
    width = g2.shape[1]
    gh = grad_hidden.wait()
    wf = W[0].wait()
    I.later()
    for n in range(0, width, 256):
        dn[:, n : n + 256] = dot(gh[...], wf[:, n : n + 256], 1, 0)
    ac, base, g = after_col.wait(), g3.wait(), gb.wait()

    def emit(t, rows):
        grad_after.ref[t : t + 256, :] = rows
        g2[t : t + 256, :] = rows.astype(BF16)

    norm_back(dn, ac, base, g, 2, 1024, emit, sums.ref)
    grad_after.start()
    sums.start()
    wo = W[1].wait()
    for n in range(0, width, 256):
        gm[:, n : n + 256] = dot(g2[...], wo[n : n + 256, :], 1, 1).astype(BF16)
    grad_mixed.start()


def column_attend_back(sm, I, W, O, G, X):
    (ints,) = sm
    packed, grad_mixed = I
    gq = O[0]
    sc, dsc = X
    pr, gm = packed.wait(), grad_mixed.wait()
    I.later()
    width = gm.shape[1]
    halves = head_masks(128)
    out = gq.ref

    def scores(b, carry):
        rows = pl.ds(pl.multiple_of(b * 128, 128), 128)
        at = pl.ds(pl.multiple_of(b * 32, 32), 32)
        for lo in range(0, width, 128):
            qs = stacked(pr[rows, lo : lo + 128] * 0.125, halves)
            k = pr[rows, width + lo : width + lo + 128]
            v = pr[rows, 2 * width + lo : 2 * width + lo + 128]
            des = stacked(gm[rows, lo : lo + 128], halves)
            sc[at, 2 * lo : 2 * lo + 256] = pick_four(dot(k, qs, 1, 1))
            dsc[at, 2 * lo : 2 * lo + 256] = pick_four(dot(v, des, 1, 1))
        return carry

    lax.fori_loop(0, 8, scores, 0)
    column_softmax(sc, ints[0])

    def pull(b, carry):
        at = pl.ds(pl.multiple_of(b * 32, 32), 32)
        p, dp = sc[at, :], dsc[at, :]
        dsc[at, :] = p * (dp - jnp.sum(p * dp, 0, keepdims=True))
        return carry

    lax.fori_loop(0, 8, pull, 0)

    def spreads(b, carry):
        rows = pl.ds(pl.multiple_of(b * 128, 128), 128)
        at = pl.ds(pl.multiple_of(b * 32, 32), 32)
        for lo in range(0, width, 128):
            qs = stacked(pr[rows, lo : lo + 128] * 0.125, halves)
            k = pr[rows, width + lo : width + lo + 128]
            des = stacked(gm[rows, lo : lo + 128], halves)
            ds = spread_four(dsc[at, 2 * lo : 2 * lo + 256])
            dq = unstack(dot(ds, k, 0, 0)) * 0.125
            out[rows, lo : lo + 128] = dq.astype(BF16)
            out[rows, width + lo : width + lo + 128] = dot(ds, qs, 1, 0).astype(BF16)
            dv = dot(spread_four(sc[at, 2 * lo : 2 * lo + 256]), des, 1, 0)
            out[rows, 2 * width + lo : 2 * width + lo + 128] = dv.astype(BF16)
        return carry

    lax.fori_loop(0, 8, spreads, 0)
    gq.start()


def column_back_and_result(sm, I, W, O, G, X):
    attend, rest = Loads(), Loads()
    attend.extend(I[:2])
    rest.extend(I[2:])
    I.later()
    column_attend_back(sm, attend, W, O[:1], G, X[:2])
    ffn_result((), rest, W, O[1:], G, X[2:])


def product_grads(sm, I, W, O, G, X):
    I.later()
    for k, g in enumerate(G):
        weight_grad(g, I[2 * k].wait(), I[2 * k + 1].wait())


def row_back(sm, I, W, O, G, X):
    gq_col, after_row, grad_after, gb = I
    grad_row, branch, grad_mixed, sums = O
    dn, wide = X
    g1, gm = branch.ref, grad_mixed.ref
    width = g1.shape[1]
    wc = W[0].wait()
    gc = gq_col.wait()
    I.later()
    for n in range(0, width, 256):
        dn[:, n : n + 256] = dot(gc[...], wc[:, n : n + 256], 1, 0)
    ar, base, g = after_row.wait(), grad_after.wait(), gb.wait()

    def emit(t, rows):
        put(wide, t, 0, rows)

    norm_back(dn, ar, base, g, 1, 1024, emit, sums.ref)
    sums.start()

    def take(t, rows):
        grad_row.ref[t : t + 256, :] = rows
        g1[t : t + 256, :] = rows.astype(BF16)

    to_columns(wide, take)
    grad_row.start()
    wo = W[1].wait()
    for n in range(0, width, 256):
        gm[:, n : n + 256] = dot(g1[...], wo[n : n + 256, :], 1, 1).astype(BF16)
    grad_mixed.start()


def row_attend_back(sm, I, W, O, G, X):
    ints, flts = sm
    packed, grad_mixed, prob, logp, mixed, g1, normed, gb = I
    (gq,) = O
    (sc,) = X
    n_seq, n_col = ints[0], ints[1]
    pr, gm = packed.wait(), grad_mixed.wait()
    I.later()
    width = gm.shape[1]
    heads = width // HD
    halves = head_masks(512)
    for m in range(heads // 2):
        d, v = four(gm, m * 128), four(pr, 2 * width + m * 128)
        for e in range(2):
            h = 2 * m + e
            sc[h * 32 : (h + 1) * 32, :] = pick(dot(d * halves[e], v, 1, 1))
    p, lp = prob.wait()[...], logp.wait()[...]
    dp = sc[...]
    ent = jnp.sum(p * lp, -1, keepdims=True) * -0.25
    row = lax.broadcasted_iota(jnp.int32, ent.shape, 0) % 32
    w = jnp.where(row < n_col, penalty_weight / gb.wait()[6:7, 0:1], 0.0)
    ds = p * (dp - jnp.sum(p * dp, -1, keepdims=True) * 0.25) - w * p * (lp + ent)
    sc[...] = ds
    keep = (lax.broadcasted_iota(jnp.int32, (1024, 1), 0) // 32 < n_seq).astype(F32)
    scale = flts[0]
    out = gq.ref
    for m in range(heads // 2):
        lo = m * 128
        q, k, d = four(pr, lo), four(pr, width + lo), four(gm, lo)
        dq = dk = dv = 0.0
        for e in range(2):
            h = 2 * m + e
            pb = spread(prob.ref[h * 32 : (h + 1) * 32, :])
            sb = spread(sc[h * 32 : (h + 1) * 32, :])
            dq = dq + dot(sb, k * halves[e], 1, 0)
            dk = dk + dot(sb, q * halves[e], 0, 0)
            dv = dv + dot(pb, d * halves[e], 0, 0)
        for t in range(4):
            rows, lanes = slice(t * 256, (t + 1) * 256), slice(t * 128, (t + 1) * 128)
            out[rows, lo : lo + 128] = (
                dq[:, lanes] * (scale * keep[t * 256 : (t + 1) * 256])
            ).astype(BF16)
            out[rows, width + lo : width + lo + 128] = (dk[:, lanes] * scale).astype(BF16)
            out[rows, 2 * width + lo : 2 * width + lo + 128] = dv[:, lanes].astype(BF16)
    gq.start()
    weight_grad(G[0], mixed.wait(), g1.wait())
    weight_grad(G[1], out, normed.wait())


def input_back(sm, I, W, O, G, X):
    gq, x, grad_row, gb = I
    grad_in, sums = O
    (dn,) = X
    width = dn.shape[1]
    gr = gq.wait()
    wt = W[0].wait()
    I.later()
    for n in range(0, width, 256):
        dn[:, n : n + 256] = dot(gr[...], wt[:, n : n + 256], 1, 0)

    def emit(t, rows):
        grad_in.ref[t : t + 256, :] = rows

    norm_back(dn, x.wait(), grad_row.wait(), gb.wait(), 0, 1024, emit, sums.ref)
    grad_in.start()
    sums.start()


class Plan:
    def __init__(self, dp, fsdp, width):
        self.dp, self.fsdp, self.width = dp, fsdp, width
        self.fast = fsdp == 2 and dp == 16
        self.slots = dp * fsdp // 2
        if not self.fast:
            return
        place = [(z, x, c, y) for z in range(4) for x in range(2) for c in range(2) for y in range(2)]
        index = {p: n for n, p in enumerate(place)}

        def one(p):
            z, x, c, y = p
            return (z, 1 - x, c, y) if c == 0 else (z, x, c, 1 - y)

        def two(p):
            z, x, c, y = p
            return (z, 1 - x, c, y) if c == 1 else (z, x, c, 1 - y)

        def next_to(p):
            return (p[0] ^ 1, *p[1:])

        def across(p):
            return (p[0] ^ 2, *p[1:])

        def mate(p):
            return (p[0], p[1], 1 - p[2], p[3])

        def pairs(f):
            return [(n, index[f(p)]) for n, p in enumerate(place)]

        self.one, self.two, self.core = pairs(one), pairs(two), pairs(mate)
        self.next_to, self.across = pairs(next_to), pairs(across)
        gathered, owners = [], []
        for p in place:
            gathered.append([])
            for order in ((across, next_to, one, two), (one, across, next_to, two)):
                held = [p]
                for f in order:
                    held = held + [f(q) for q in held]
                gathered[-1].append([index[q] for q in held])
            owners.append([])
            for order in ((across, next_to, two, one), (two, across, next_to, one)):
                owned = [p]
                for f in order:
                    owned = owned + [f(q) for q in owned]
                owners[-1].append([index[q] for q in owned])
        mates = [index[mate(p)] for p in place]
        self.gather_tables = [
            np.array([gathered[n][k] + gathered[m][k] for n, m in enumerate(mates)], np.int32)
            for k in range(2)
        ]
        self.owner_tables = []
        for k in range(2):
            owned = np.array([owners[n][k] + owners[m][k] for n, m in enumerate(mates)], np.int32)
            self.owner_tables.append(np.argsort(owned, 1).astype(np.int32))

    def go(self, v, perm):
        return lax.ppermute(v, AXES, perm)

    def everywhere(self, v, beside):
        if not self.fast:
            return lax.psum(v, AXES)
        for perm in (self.core, self.one):
            v = v + lax.ppermute(v, AXES, perm)
        v = after(v, *beside.second_came)
        for perm in (self.two, self.next_to):
            v = v + lax.ppermute(v, AXES, perm)
        v = after(v, *beside.third_came)
        return v + lax.ppermute(v, AXES, self.across)


def after(v, *others):
    return lax.optimization_barrier((v, *others))[0]


class Gathering:
    def __init__(self, plan, shard):
        self.plan, self.have = plan, [shard[None]]

    def all(self, others):
        if others:
            self.have = list(lax.optimization_barrier((*self.have, *others)))[: len(self.have)]
        self.have = [jnp.concatenate(self.have, 0)] if len(self.have) > 1 else self.have
        return self.have[0]

    def step(self, perm, *others):
        self.came = self.plan.go(self.all(others), perm)
        self.have.append(self.came)
        return self.came

    def far(self, *others):
        self.mine = self.all(others)
        self.came = self.plan.go(self.mine, self.plan.two)
        return self.came

    def share(self, *others):
        mine = after(self.mine, *others) if others else self.mine
        self.mate = self.plan.go(mine, self.plan.core)
        return self.mate

    def last(self, *others):
        far = after(self.came, *others) if others else self.came
        self.end = self.plan.go(far, self.plan.core)
        return [self.mine, self.came, self.mate, self.end]


class Reduction:
    def __init__(self, plan, grads, names, shards):
        self.plan = plan
        self.names = [(n, shards[n].shape[0]) for n in names]
        if plan.fast:
            kept, self.sent = grads
            self.terms, self.size = [kept], kept.shape[0]
        else:
            self.whole = grads

    def go(self, v, perm):
        return lax.ppermute(v.astype(BF16), AXES, perm)

    def landed(self):
        return [self.came] if self.plan.fast else []

    def core(self, *others):
        if self.plan.fast:
            sent = after(self.sent, *others) if others else self.sent
            self.came = self.go(sent, self.plan.core)

    def total(self, start, stop):
        return sum(t[start:stop].astype(F32) for t in self.terms)

    def step(self, perm, *others):
        if self.plan.fast:
            came = after(self.came, *others) if others else self.came
            self.terms.append(came)
            self.size //= 2
            self.came = self.go(self.total(self.size, 2 * self.size), perm)

    def first(self, *others):
        self.step(self.plan.fast and self.plan.one, *others)

    def second(self, *others):
        self.step(self.plan.fast and self.plan.two, *others)

    def third(self, *others):
        self.second_came = self.landed()
        self.step(self.plan.fast and self.plan.next_to, *others)

    def fourth(self, *others):
        self.third_came = self.landed()
        self.step(self.plan.fast and self.plan.across, *others)

    def finish(self, *others):
        if self.plan.fast:
            self.terms.append(after(self.came, *others) if others else self.came)
            self.sum = self.total(0, 1)[0]

    def result(self):
        if self.plan.fast:
            cuts = np.cumsum([rows for _, rows in self.names])[:-1]
            return {n: v for (n, _), v in zip(self.names, jnp.split(self.sum, cuts, 0))}
        got = {}
        for (n, _), g in zip(self.names, self.whole):
            half = lax.psum_scatter(g, "dp", scatter_dimension=0, tiled=True)
            got[n] = lax.psum_scatter(half, "fsdp", scatter_dimension=1, tiled=True).astype(F32)
        return got


def local(
    plan,
    alignment_input,
    sequence_mask,
    column_length,
    output_cotangent,
    row_projection_weight,
    row_out_weight,
    column_projection_weight,
    column_out_weight,
    feedforward_in_weight,
    feedforward_out_weight,
    layer_norm_gain,
    layer_norm_bias,
):
    width = alignment_input.shape[3]
    tokens = alignment_input.shape[1] * alignment_input.shape[2]
    heads = width // HD
    hidden = feedforward_out_weight.shape[0] * plan.dp
    x = alignment_input.reshape(tokens, width)
    cot = output_cotangent.reshape(tokens, width)
    shards = dict(
        row_qkv=row_projection_weight.T,
        row_out=row_out_weight,
        col_qkv=column_projection_weight.T,
        col_out=column_out_weight,
        ffn_in=feedforward_in_weight.T,
        ffn_out=feedforward_out_weight,
    )
    whole_rows = {k: v.shape[0] * plan.dp for k, v in shards.items()}
    norms = jnp.concatenate([layer_norm_gain, layer_norm_bias], 0)
    share = norms.shape[1]
    devices = plan.dp * plan.fsdp
    me = lax.axis_index(AXES)
    n_seq = jnp.sum((sequence_mask > 0).astype(jnp.int32))
    n_col = column_length[0].astype(jnp.int32)
    ints = jnp.stack([n_seq, n_col])
    row_scale = 0.125 * lax.rsqrt(n_seq.astype(F32))

    w = {}
    if plan.fast:
        gather_row, early_row = (
            lax.dynamic_index_in_dim(jnp.asarray(t), me, 0, False) for t in plan.gather_tables
        )
        owner_row, first_row = (
            lax.dynamic_index_in_dim(jnp.asarray(t), me, 0, False) for t in plan.owner_tables
        )
        tables = [gather_row, owner_row, early_row]
        own_tables = dict(colg=[gather_row, first_row, early_row])
        extra = jnp.concatenate([norms.reshape(-1), n_col.astype(BF16)[None]])
        cols = shards["row_out"].shape[1]
        extra = jnp.pad(extra[None], ((0, 15), (0, cols - extra.shape[0])))
        groups = (("row_qkv",), ("row_out", "col_qkv"), ("col_out", "ffn_in"), ("ffn_out",))
        packs = []
        for gi, names in enumerate(groups):
            parts = [shards[n] for n in names] + ([extra] if gi == 0 else [])
            packs.append(jnp.concatenate(parts, 0) if len(parts) > 1 else parts[0])
        def ready(gi, bufs):
            row0 = 0
            for n in groups[gi]:
                rows = shards[n].shape[0]
                w[n] = Weights(bufs, row0, rows, whole_rows[n], width, True, 2 if gi == 3 else 0)
                row0 += rows
            return bufs

        late = []
        g1, g2, g3, g4 = (Gathering(plan, p) for p in packs)
        g1.step(plan.across)
        g4.step(plan.one)
        t = [g1.step(plan.next_to, g4.came, ints, *tables, first_row)]
        t = [g1.step(plan.one), g2.step(plan.across, *t)]
        t = [g1.far(*t), g2.step(plan.next_to, *t), g3.step(plan.across, *t)]
        g1.share(*t)
        bufs = ready(0, g1.last(*t))
        t = [g2.step(plan.one, *t), g3.step(plan.next_to, *t), g1.mate, g1.end]
        early = dict(rowf=t)
        slot = [g2.far(*t), g2.share(*t), g3.step(plan.one, *t), g4.step(plan.across, *t)]
        early["colf"] = slot

        def after_rowf(token):
            ready(1, g2.last(token, *slot))
            t = [token, *slot, g2.end]
            early["ffnf"] = [g3.far(*t), g3.share(*t), g4.step(plan.next_to, *t)]

        def after_colf(token):
            t = [token, *early["ffnf"]]
            ready(2, g3.last(*t))
            t = [token, g3.end]
            early["fout"] = [g4.far(*t), g4.share(*t)]

        hooks = dict(
            rowf=lambda outs: after_rowf(outs[5]),
            colf=lambda outs: after_colf(outs[1]),
            ffnf=lambda outs: late.append(ready(3, g4.last(outs[1], *early["fout"]))[3]),
        )
        rows = shards["row_qkv"].shape[0]
        w["norms"] = Weights(bufs, rows, 16, 16 * plan.dp, width, True)
        w["norms"].raw = True
    else:
        tables, own_tables = [jnp.zeros((1,), jnp.int32)] * 3, {}
        early, hooks, late = {}, {}, []
        for n, s in shards.items():
            half = lax.all_gather(s, "fsdp", axis=1, tiled=True)
            full = lax.all_gather(half, "dp", axis=0, tiled=True)
            w[n] = Weights([full], 0, s.shape[0], whole_rows[n], width, False)
        gb = lax.all_gather(norms, "fsdp", axis=1, tiled=True)
        gb = lax.all_gather(gb, "dp", axis=1, tiled=True).astype(F32)
        count = jnp.full((1, width), lax.psum(n_col.astype(F32), AXES))
        gb = jnp.concatenate([gb, count, jnp.zeros_like(count)], 0)
    flts = row_scale[None]

    micros = dict(
        rowf=9,
        colf=8,
        cola=4,
        ffnf=12,
        fout=7,
        ffnb=12,
        colb=10,
        colt=7,
        colg=7,
        rowb=10,
        rowt=13,
        inpb=9,
        lout=9,
    )

    def arr(n, dtype, rows=tokens, vmem=True, hbm=False):
        return Out((rows, n), dtype, vmem, hbm)

    resident = {}

    def run(name, body, smem, ins, weights, outs, grads=(), scratch=(), deps=(), fetch=()):
        ins = [a.bufs[0] if isinstance(a, Weights) else a for a in ins]
        weights = [w[n] if isinstance(n, str) else n for n in weights]
        fetch = [w[a] if isinstance(a, str) else Weights.of(a) for a in fetch]
        lists = own_tables.get(name, tables) + list(smem), ins, weights, outs, grads
        deps = list(deps) + early.get(name, [])
        got = fused(name, body, *lists, plan, resident, micros[name], scratch, deps, fetch)
        if name in hooks:
            hooks[name](got[0])
        return got

    wide = pltpu.VMEM((tokens, width), F32)
    turn = pltpu.VMEM((width // 128, 32 * PITCH + 8, 128), F32)
    score = pltpu.VMEM((heads * 32, 128), F32)
    flat = pltpu.VMEM((tokens // 4, 2 * width), F32)
    moment = arr(width, F32, 8, False, True)
    keep = dict(vmem=False, hbm=True)
    token = arr(128, F32, 8, **keep)

    (normed_row, packed_row, mixed_row, prob, logp, ent, gb), _ = run(
        "rowf",
        row_forward,
        [ints, flts],
        [x] if plan.fast else [x, gb],
        ["norms", "row_qkv"] if plan.fast else ["row_qkv"],
        [
            arr(width, BF16, **keep),
            arr(3 * width, BF16, **keep),
            arr(width, BF16, hbm=True),
            arr(128, F32, heads * 32, **keep),
            arr(128, F32, heads * 32, **keep),
            arr(width, F32, 8, **keep),
            arr(width, F32, 8, **keep),
        ],
        (),
        [score],
    )
    (after_row, normed_col, packed_col, mixed_col), _ = run(
        "colf",
        column_all,
        [ints],
        [x, mixed_row[0], gb],
        ["row_out", "col_qkv"],
        [
            arr(width, F32, hbm=True),
            arr(width, BF16, **keep),
            arr(3 * width, BF16, **keep),
            arr(width, BF16, hbm=True),
        ],
        (),
        [turn, flat],
    )
    (after_col, normed_ffn, active, slope, cot_here), _ = run(
        "ffnf",
        feed_forward,
        [],
        [after_row[0], mixed_col[0], gb],
        ["col_out", "ffn_in"],
        [
            arr(width, F32, **keep),
            arr(width, BF16, **keep),
            arr(hidden, BF16, hbm=True),
            arr(hidden, BF16),
        ],
        fetch=[cot],
    )
    (g3,), grads = run(
        "fout",
        ffn_out_grad,
        [ints],
        [active[0], cot_here],
        [],
        [arr(width, BF16)],
        [hidden],
        [turn],
    )
    r1 = Reduction(plan, grads, ["ffn_out"], shards)
    r1.core(*late)
    (grad_hidden, w_in, w_col_out, after_here), grads = run(
        "ffnb",
        ffn_back,
        [],
        [g3, slope, normed_ffn],
        ["ffn_out"],
        [arr(hidden, BF16)],
        [hidden],
        fetch=["ffn_in", "col_out", after_col],
    )
    r2 = Reduction(plan, grads, ["ffn_in"], shards)
    landed = r1.landed()
    r1.first(grads[0], *landed)
    r2.core(*landed)
    (grad_after, g2, gm_col, sums_two, packed_here, normed_here, mixed_here), _ = run(
        "colb",
        column_back,
        [],
        [grad_hidden, after_here, g3, gb],
        [w_in, w_col_out],
        [arr(width, F32, **keep), arr(width, BF16), arr(width, BF16), moment],
        (),
        [wide],
        landed,
        [packed_col, normed_col, mixed_col[1]],
    )
    landed = r1.landed() + r2.landed()
    r1.second(sums_two, *landed)
    r2.first(sums_two, *landed)
    (gq_col, layer_out, mark, w_col_qkv, w_row_out), _ = run(
        "colt",
        column_back_and_result,
        [ints],
        [packed_here, gm_col, active[1], after_col],
        ["ffn_out"],
        [arr(3 * width, BF16), arr(width, BF16, **keep), token],
        (),
        [flat, flat, turn],
        landed,
        ["col_qkv", "row_out"],
    )
    landed = r1.landed() + r2.landed()
    r1.third(mark, *landed)
    r2.second(mark, *landed)
    (after_row_here, grad_after_here), grads = run(
        "colg",
        product_grads,
        [],
        [gq_col, normed_here, mixed_here, g2],
        [],
        [],
        [3 * width, width],
        (),
        landed,
        [after_row[1], grad_after],
    )
    r3 = Reduction(plan, grads, ["col_qkv", "col_out"], shards)
    landed = r1.landed() + r2.landed()
    r1.fourth(grads[0], *landed)
    r2.third(grads[0], *landed)
    r3.core(*landed)
    (grad_row, g1, gm_row, sums_one, packed_here, normed_here, mixed_here), _ = run(
        "rowb",
        row_back,
        [],
        [gq_col, after_row_here, grad_after_here, gb],
        [w_col_qkv, w_row_out],
        [arr(width, F32, **keep), arr(width, BF16), arr(width, BF16), moment],
        (),
        [wide, turn],
        landed,
        [packed_row, normed_row, mixed_row[1]],
    )
    landed = r1.landed() + r2.landed() + r3.landed()
    r2.fourth(sums_one, *landed)
    r3.first(sums_one, *landed)
    (gq_row,), grads = run(
        "rowt",
        row_attend_back,
        [ints, flts],
        [packed_here, gm_row, prob, logp, mixed_here, g1, normed_here, gb],
        [],
        [arr(3 * width, BF16, **keep)],
        [width, 3 * width],
        [score],
        landed,
    )
    r4 = Reduction(plan, grads, ["row_out", "row_qkv"], shards)
    landed = r1.landed() + r2.landed() + r3.landed()
    r4.core(*landed)
    landed = landed + r4.landed()
    r1.finish()
    r2.finish()
    sums = [r.sum for r in (r1, r2)] if plan.fast else []
    r3.third(grads[0], *landed)
    r4.first(*landed, *sums)
    (grad_in, sums_zero), _ = run(
        "inpb",
        input_back,
        [],
        [gq_row, x, grad_row, gb],
        ["row_qkv"],
        [arr(width, F32, **keep), moment],
        (),
        [wide],
        [grads[0], *landed],
    )
    landed = r3.landed() + r4.landed()
    r4.second(sums_zero, *landed)
    r3.fourth(sums_zero, *landed)
    r4.third()
    landed = r4.landed()
    r3.second(*landed)
    r4.fourth()
    r3.finish()
    r4.finish(*([r3.sum] if plan.fast else []))
    got = {}
    for r in (r1, r2, r3, r4):
        got.update(r.result())
    sums_all = plan.everywhere(sums_zero + sums_one + sums_two + ent, r4)
    owned = lax.dynamic_slice_in_dim(sums_all[:6], me * share, share, 1)
    gains, biases = owned[0::2], owned[1::2]
    shape = alignment_input.shape
    return (
        layer_out.reshape(shape),
        grad_in.reshape(shape),
        got["row_qkv"].T,
        got["row_out"],
        got["col_qkv"].T,
        got["col_out"],
        got["ffn_in"].T,
        got["ffn_out"],
        gains,
        biases[:2],
        biases[2],
        sums_all[6, 0],
    )


def solution(mesh):
    def whole(*args):
        plan = Plan(mesh.shape["dp"], mesh.shape["fsdp"], args[0].shape[3])
        return jax.shard_map(
            lambda *blocks: local(plan, *blocks),
            mesh=mesh,
            in_specs=(
                P(AXES, None, None, None),
                P(AXES, None),
                P(AXES),
                P(AXES, None, None, None),
                P("fsdp", "dp"),
                P("dp", "fsdp"),
                P("fsdp", "dp"),
                P("dp", "fsdp"),
                P("fsdp", "dp"),
                P("dp", "fsdp"),
                P(None, AXES),
                P(None, AXES),
            ),
            out_specs=(
                P(AXES, None, None, None),
                P(AXES, None, None, None),
                P("fsdp", "dp"),
                P("dp", "fsdp"),
                P("fsdp", "dp"),
                P("dp", "fsdp"),
                P("fsdp", "dp"),
                P("dp", "fsdp"),
                P(None, AXES),
                P(None, AXES),
                P(AXES),
                P(),
            ),
            check_vma=False,
        )(*args)

    return whole
```
